256 devices in a mesh: orb: 64 (over x, z, core), box: 4 (over y).
Axes of the slice: x: 4, y: 4, z: 8, core: 2. Of those that a mesh axis runs over, the one named last changes fastest.
Arguments:
- psi: float32 [512, 64, 4096], P('orb', 'box'), may hold values from -6 to 6
- potential: float32 [64, 4096], P('box'), may hold values from -3 to 3
- orbital_slot: int32 [256], replicated, may hold values from 0 to 511, as said below
Outputs:
- residual: float32 [256, 64, 4096], P('orb', 'box')
- direction: float32 [256, 64, 4096], P('orb', 'box')
- multipliers: float32 [256, 256], replicated
The draws below stay inside these ranges and needn't reach their ends.
Inputs may be any that keep to these rules, and one draw needn't show every extreme that they name: The values are distinct slots: orbital j sits in slot orbital_slot[j]. The 8 slots of one index of orb hold up to 8 orbitals, and in every draw all slots of one index are filled.
All inputs are finite; a program needn't handle non-finite values.
Results may differ from the reference program's by a relative error of at most 0.0002.
Values sent between devices are 32-bit elements; how exact they have to be, the bound alone decides.
A program may use at most 64 MiB of HBM per device.

```python
import math
import jax
import jax.numpy as jnp
import numpy as np
from jax import lax

G = 64
MTAPS = 16
KREACH = 14
SWEEPS = 4
SLOTS = 8
ORBS = 256
SLOTS_ALL = 512


def draw_orbital_slot(key, part):
    base_key = jax.random.fold_in(key, 7)
    key_full, key_order, key_other = jax.random.split(base_key, 3)
    owners = SLOTS_ALL // SLOTS
    full_owner = jax.random.randint(key_full, (), 0, owners, dtype=jnp.int32)
    orbital_order = jax.random.permutation(key_order, ORBS)
    other_slots = jax.random.permutation(key_other, SLOTS_ALL - SLOTS)[:ORBS - SLOTS].astype(jnp.int32)
    other_slots = other_slots + SLOTS * (other_slots >= full_owner * SLOTS).astype(jnp.int32)
    placed = jnp.concatenate([full_owner * SLOTS + jnp.arange(SLOTS, dtype=jnp.int32), other_slots])
    return jnp.zeros((ORBS,), jnp.int32).at[orbital_order].set(placed)


def shard_levels(rng, shape, shards, smallest, high):
    def one(dim, blocks):
        heights = jax.random.uniform(jax.random.fold_in(jax.random.fold_in(rng, 6), dim), (blocks,), jnp.float32, smallest / len(shards), high / len(shards))
        return jnp.repeat(jnp.exp(heights), shape[dim] // blocks).reshape((-1,) + (1,) * (len(shape) - dim - 1))

    loudness = one(*shards[0])
    for cut in shards[1:]:
        loudness = loudness * one(*cut)
    return loudness


def bell_draw(rng, shape, scale, most, shards=(), kind=jnp.bfloat16):
    factor_of = shard_levels(rng, shape, shards, -0.22, 0.18) if shards else 1.0
    entries = jax.random.normal(rng, shape, jnp.float32) * scale * factor_of
    return jnp.minimum(jnp.maximum(entries, -most), most).astype(kind)


def setup_inputs(seed: int = 0) -> dict:
    key_list = jax.random.split(jax.random.key(seed), 4)
    return {
        "psi": bell_draw(key_list[0], (SLOTS_ALL, G, G * G), 1.0, 6.0, ((0, 64), (1, 4)), jnp.float32),
        "potential": jnp.clip(jax.random.uniform(key_list[1], (G, G * G), jnp.float32, -3.0, 3.0) * shard_levels(key_list[1], (G, G * G), ((0, 4),), -0.4, 0.0), -3.0, 3.0),
        "orbital_slot": draw_orbital_slot(jax.random.fold_in(key_list[3], 71), 0),
    }


highest = lax.Precision.HIGHEST
coupling_z = 4.0
coupling_xy = 1.0


def magic_weights(tap_count):
    half_len = tap_count // 2
    offsets = np.arange(1 - half_len, half_len + 1) * 1.0
    weights = np.ones(tap_count)
    for index_a in range(tap_count):
        for index_b in range(tap_count):
            if index_b != index_a:
                weights[index_a] *= (0.25 - offsets[index_b]) / (offsets[index_a] - offsets[index_b])
    return weights


def second_weights(reach_cells):
    factor = math.factorial(reach_cells) ** 2
    weights = np.zeros(2 * reach_cells + 1)
    for distance in range(1, reach_cells + 1):
        entry_value = 2.0 * (-1) ** (distance + 1) * factor / (distance * distance * math.factorial(reach_cells - distance) * math.factorial(reach_cells + distance))
        weights[reach_cells + distance] = entry_value
        weights[reach_cells - distance] = entry_value
    weights[reach_cells] = -weights.sum()
    return -0.5 * weights


def banded(row_count, col_count, row_start, col_start, weights, offset_low):
    row_index = np.arange(row_count)[:, None] + row_start
    col_index = np.arange(col_count)[None, :] + col_start
    position = row_index - col_index - offset_low
    inside = (position >= 0) & (position < len(weights))
    return np.where(inside, weights[np.clip(position, 0, len(weights) - 1)], 0.0)


def apply_orbital(coeffs, potential_cube, forward, kinetic):
    grid_values = jnp.einsum("zyx,zp->pyx", coeffs, forward, precision=highest)
    grid_values = jnp.einsum("zyx,yp->zpx", grid_values, forward, precision=highest)
    grid_values = jnp.einsum("zyx,xp->zyp", grid_values, forward, precision=highest)
    weighted = grid_values * potential_cube
    applied = jnp.einsum("pyx,zp->zyx", weighted, forward, precision=highest)
    applied = jnp.einsum("zpx,yp->zyx", applied, forward, precision=highest)
    applied = jnp.einsum("zyp,xp->zyx", applied, forward, precision=highest)
    applied = applied + jnp.einsum("zyx,zp->pyx", coeffs, kinetic, precision=highest)
    applied = applied + jnp.einsum("zyx,yp->zpx", coeffs, kinetic, precision=highest)
    applied = applied + jnp.einsum("zyx,xp->zyp", coeffs, kinetic, precision=highest)
    return applied


def relax_orbital(residual_cube, denominator):
    iterate = residual_cube / denominator
    for sweep_index in range(SWEEPS):
        padded = jnp.pad(iterate, 1)
        along_z = padded[2:, 1:-1, 1:-1] + padded[:-2, 1:-1, 1:-1]
        along_y = padded[1:-1, 2:, 1:-1] + padded[1:-1, :-2, 1:-1]
        along_x = padded[1:-1, 1:-1, 2:] + padded[1:-1, 1:-1, :-2]
        iterate = (residual_cube + coupling_xy * (along_y + along_x) + coupling_z * along_z) / denominator
    return iterate


def reference(psi, potential, orbital_slot):
    magic = magic_weights(MTAPS)
    kinetic_row = second_weights(KREACH)
    forward = jnp.asarray(banded(G, G, 0, 0, magic, 1 - MTAPS // 2), dtype=jnp.float32)
    kinetic = jnp.asarray(banded(G, G, 0, 0, kinetic_row, -KREACH), dtype=jnp.float32)
    potential_cube = potential.reshape(G, G, G)
    chosen = jnp.take(psi, orbital_slot, axis=0)
    applied = lax.map(lambda coeffs: apply_orbital(coeffs.reshape(G, G, G), potential_cube, forward, kinetic).reshape(G, G * G), chosen)
    chosen_flat = chosen.reshape(ORBS, G * G * G)
    applied_flat = applied.reshape(ORBS, G * G * G)
    multipliers = jnp.einsum("ia,ja->ij", chosen_flat, applied_flat, precision=highest) / float(G ** 3)
    residual = applied_flat - jnp.einsum("ji,ja->ia", multipliers, chosen_flat, precision=highest)
    residual = residual.reshape(ORBS, G, G * G)
    denominator = 2.0 * coupling_z + 4.0 * coupling_xy + 1.0 + jnp.abs(jnp.diagonal(multipliers))
    direction = lax.map(lambda pair: relax_orbital(pair[0].reshape(G, G, G), pair[1]).reshape(G, G * G), (residual, denominator))
    return (residual, direction, multipliers)
```

```python
import math

import jax
import jax.numpy as jnp
import ml_dtypes
import numpy as np
from jax import lax
from jax.experimental import pallas as pl
from jax.experimental.pallas import tpu as pltpu
from jax.sharding import PartitionSpec as P

G = 64
MTAPS = 16
KREACH = 14
SWEEPS = 4
ORB, BOX = 64, 4
SLOTS, ORBS, OWN = 8, 256, 4
DEPTH = 16
PLANE = G * G
LANES = 256
TILES = PLANE // LANES
FPAD, KPAD = 2, 4

coupling_z = 4.0
coupling_xy = 1.0

F32, BF16 = jnp.float32, jnp.bfloat16
ANY = pl.BlockSpec(memory_space=pl.ANY)
VMEM = pl.BlockSpec(memory_space=pltpu.VMEM)
VLIMIT = 56 * 2**20


def magic_weights(tap_count):
    half_len = tap_count // 2
    offsets = np.arange(1 - half_len, half_len + 1) * 1.0
    weights = np.ones(tap_count)
    for index_a in range(tap_count):
        for index_b in range(tap_count):
            if index_b != index_a:
                weights[index_a] *= (0.25 - offsets[index_b]) / (
                    offsets[index_a] - offsets[index_b]
                )
    return weights


def second_weights(reach_cells):
    factor = math.factorial(reach_cells) ** 2
    weights = np.zeros(2 * reach_cells + 1)
    for distance in range(1, reach_cells + 1):
        entry_value = (
            2.0
            * (-1) ** (distance + 1)
            * factor
            / (
                distance
                * distance
                * math.factorial(reach_cells - distance)
                * math.factorial(reach_cells + distance)
            )
        )
        weights[reach_cells + distance] = entry_value
        weights[reach_cells - distance] = entry_value
    weights[reach_cells] = -weights.sum()
    return -0.5 * weights


def banded(row_count, col_count, row_start, col_start, weights, offset_low):
    row_index = np.arange(row_count)[:, None] + row_start
    col_index = np.arange(col_count)[None, :] + col_start
    position = row_index - col_index - offset_low
    inside = (position >= 0) & (position < len(weights))
    return np.where(inside, weights[np.clip(position, 0, len(weights) - 1)], 0.0)


def halves(table):
    table = np.asarray(table, np.float32)
    high = table.astype(ml_dtypes.bfloat16)
    low = (table - high.astype(np.float32)).astype(ml_dtypes.bfloat16)
    return high, low


def tables():
    magic = magic_weights(MTAPS)
    kinetic_row = second_weights(KREACH)
    forward = banded(G, G, 0, 0, magic, 1 - MTAPS // 2)
    kinetic = banded(G, G, 0, 0, kinetic_row, -KREACH)
    rows = LANES // G

    def beside(high, low):
        return np.concatenate([high, high, low], 1)

    z_in = beside(*halves(np.concatenate([forward.T, kinetic], 0)))
    z_out = beside(*halves(forward))
    into, back, kin = [], [], []
    for step in range(-FPAD, FPAD + 1):
        block = banded(rows, rows, rows * step, 0, magic, 1 - MTAPS // 2)
        into.append(np.kron(block, forward))
        block = banded(rows, rows, -rows * step, 0, magic, 1 - MTAPS // 2).T
        back.append(np.kron(block, forward.T))
    for step in range(-KPAD, KPAD + 1):
        block = np.kron(banded(rows, rows, rows * step, 0, kinetic_row, -KREACH), np.eye(G))
        if step == 0:
            block = block + np.kron(np.eye(rows), kinetic)
        kin.append(block)
    return [z_in, z_out] + [np.stack(halves(np.stack(m))) for m in (into, back, kin)]


def split(values):
    high = values.astype(BF16)
    return high, (values - high.astype(F32)).astype(BF16)


def mm(left, right):
    return jnp.dot(left, right, preferred_element_type=F32)


def place():
    orb = lax.axis_index("orb")
    box = lax.axis_index("box")
    return orb, box, orb // 16, (orb // 2) % 8, orb % 2


def shifted(orb, step):
    x, z, core = orb // 16, (orb // 2) % 8, orb % 2
    dx, dz, dc = step // 16, (step // 2) % 8, step % 2
    return ((x + dx) % 4) * 16 + ((z + dz) % 8) * 2 + (core + dc) % 2


def remote(src, dst, send, recv, orb, box):
    return pltpu.make_async_remote_copy(
        src_ref=src,
        dst_ref=dst,
        send_sem=send,
        recv_sem=recv,
        device_id={"orb": orb, "box": box},
        device_id_type=pl.DeviceIdType.MESH,
    )


def wait_for(ref, sem):
    pltpu.make_async_copy(ref, ref, sem).wait()


def tile_of(orb):
    return pl.ds(pl.multiple_of((orb // 32) * 8, 8), 8), pl.ds(
        pl.multiple_of((orb % 32) * 128, 128), 128
    )


def exchange_kernel(psi, pot, pieces, cube, vfull, own, p_send, p_recv, y_send, y_recv, v_send, v_recv):
    orb, box, _, _, _ = place()
    slab = pl.ds(pl.multiple_of(box * DEPTH, DEPTH), DEPTH)
    for step in range(1, BOX):
        to = (box + step) % BOX
        remote(psi.at[pl.ds(2 * to, 2)], cube.at[:, slab, :], y_send, y_recv, orb, to).start()
        remote(pot, vfull.at[slab, :], v_send, v_recv, orb, to).start()
    mine = pltpu.make_async_copy(psi.at[pl.ds(2 * box, 2)], cube.at[:, slab, :], own.at[0])
    mine.start()
    vmine = pltpu.make_async_copy(pot, vfull.at[slab, :], own.at[1])
    vmine.start()
    target = pl.ds(pl.multiple_of(orb * SLOTS, SLOTS), SLOTS)
    z_rows, lanes = tile_of(orb)
    pmine = pltpu.make_async_copy(psi.at[:, z_rows, lanes], pieces.at[target], own.at[2])
    pmine.start()

    def send(step, carry):
        to = shifted(orb, step)
        z_rows, lanes = tile_of(to)
        remote(psi.at[:, z_rows, lanes], pieces.at[target], p_send, p_recv, to, box).start()
        return carry

    lax.fori_loop(1, ORB, send, 0)
    mine.wait()
    vmine.wait()
    pmine.wait()
    third = cube.at[:, pl.ds(0, 3 * DEPTH), :]
    wait_for(third, y_send)
    wait_for(third, y_recv)
    wait_for(vfull.at[pl.ds(0, 3 * DEPTH)], v_send)
    wait_for(vfull.at[pl.ds(0, 3 * DEPTH)], v_recv)
    wait_for(pieces.at[pl.ds(0, SLOTS * (ORB - 1))], p_send)
    wait_for(pieces.at[pl.ds(0, SLOTS * (ORB - 1))], p_recv)


def apply_kernel(cube, vfull, z_in, z_out, into, back, kin, out, c_hi, c_lo, t_hi, t_lo, s_hi, s_lo, kz):
    for buf, pad in ((c_hi, KPAD), (c_lo, KPAD), (t_hi, FPAD), (t_lo, FPAD), (s_hi, FPAD), (s_lo, FPAD)):
        edge = jnp.zeros((pad, 2 * G, LANES), BF16)
        buf[pl.ds(0, pad)] = edge
        buf[pl.ds(TILES + pad, pad)] = edge

    def along_z(t, carry):
        lanes = pl.ds(pl.multiple_of(t * LANES, LANES), LANES)
        for s in range(2):
            rows = pl.ds(s * G, G)
            high, low = split(cube[s, :, lanes])
            c_hi[t + KPAD, rows, :] = high
            c_lo[t + KPAD, rows, :] = low
            both = mm(z_in[...], jnp.concatenate([high, low, high], 0))
            kz[t, rows, :] = both[G:]
            high, low = split(both[:G])
            t_hi[t + FPAD, rows, :] = high
            t_lo[t + FPAD, rows, :] = low
        return carry

    lax.fori_loop(0, TILES, along_z, 0)
    group = 2

    def spread(hi, lo, table, count, first, acc):
        for d in range(count):
            high = hi[pl.ds(first + d, group)].reshape(group * 2 * G, LANES)
            low = lo[pl.ds(first + d, group)].reshape(group * 2 * G, LANES)
            term = mm(high, table[0, d]) + mm(low, table[0, d]) + mm(high, table[1, d])
            acc = term if acc is None else acc + term
        return acc

    def middle(i, carry):
        first = i * group
        grid = spread(t_hi, t_lo, into, 2 * FPAD + 1, first, None)
        for j in range(group):
            lanes = pl.ds(pl.multiple_of((first + j) * LANES, LANES), LANES)
            local = vfull[:, lanes]
            for s in range(2):
                low_row = (j * 2 + s) * G
                high, low = split(grid[low_row : low_row + G] * local)
                done = mm(z_out[...], jnp.concatenate([high, low, high], 0))
                high, low = split(done)
                s_hi[first + j + FPAD, pl.ds(s * G, G), :] = high
                s_lo[first + j + FPAD, pl.ds(s * G, G), :] = low
        return carry

    lax.fori_loop(0, TILES // group, middle, 0)

    def last(i, carry):
        first = i * group
        acc = kz[pl.ds(first, group)].reshape(group * 2 * G, LANES)
        acc = spread(c_hi, c_lo, kin, 2 * KPAD + 1, first, acc)
        acc = spread(s_hi, s_lo, back, 2 * FPAD + 1, first, acc)
        for j in range(group):
            lanes = pl.ds(pl.multiple_of((first + j) * LANES, LANES), LANES)
            for s in range(2):
                low_row = (j * 2 + s) * G
                out[s, :, lanes] = acc[low_row : low_row + G]
        return carry

    lax.fori_loop(0, TILES // group, last, 0)


def scatter_kernel(applied, pieces, own, send_sem, recv_sem):
    orb, box, _, _, _ = place()
    target = pl.ds(orb * SLOTS + 2 * box, 2)

    def source(to_orb, to_box):
        z_rows = pl.ds(pl.multiple_of(to_box * DEPTH + (to_orb // 32) * 8, 8), 8)
        return applied.at[:, z_rows, pl.ds(pl.multiple_of((to_orb % 32) * 128, 128), 128)]

    mine = pltpu.make_async_copy(source(orb, box), pieces.at[target], own)
    mine.start()

    def send(step, carry):
        to_orb = shifted(orb, step // BOX)
        to_box = (box + step % BOX) % BOX
        remote(source(to_orb, to_box), pieces.at[target], send_sem, recv_sem, to_orb, to_box).start()
        return carry

    lax.fori_loop(1, ORB * BOX, send, 0)
    mine.wait()
    rest = pieces.at[pl.ds(0, SLOTS * ORB - 2)]
    wait_for(rest, send_sem)
    wait_for(rest, recv_sem)


def reduce_kernel(
    psi_pieces, app_pieces, slots, mult, ext,
    part, rs, bb, resid, c_hi, c_lo, a_hi, a_lo, sems, own,
):
    orb, box, x, z, core = place()
    pieces2 = psi_pieces.reshape(SLOTS * ORB * 8, 128)
    applied2 = app_pieces.reshape(SLOTS * ORB * 8, 128)
    resid2 = resid.reshape(ORBS * 8, 128)
    pick = (
        lax.broadcasted_iota(jnp.int32, (ORBS, SLOTS * ORB), 1) == slots[...]
    ).astype(F32).astype(BF16)
    for k in range(8):
        lanes = pl.ds(k * 128, 128)
        for ref, hi, lo in ((pieces2, c_hi, c_lo), (applied2, a_hi, a_lo)):
            high, low = split(ref[pl.ds(k, SLOTS * ORB, stride=8), :])
            hi[:, lanes] = mm(pick, high).astype(BF16)
            lo[:, lanes] = mm(pick, low).astype(BF16)

    def dot_nt(left, right):
        return lax.dot_general(left, right, (((1,), (1,)), ((), ())), preferred_element_type=F32)

    scale = 1.0 / float(G**3)
    total = dot_nt(c_hi[...], a_hi[...]) + dot_nt(c_lo[...], a_hi[...]) + dot_nt(c_hi[...], a_lo[...])
    part[...] = (total * scale).reshape(16, 16, ORBS)

    a_me = x * 4 + box
    b_me = z * 2 + core

    def a_peer(step):
        return ((x + step // 4) % 4) * 16 + z * 2 + core, (box + step % 4) % 4

    def b_peer(step):
        return x * 16 + ((z + step // 2) % 8) * 2 + (core + step % 2) % 2, box

    def send_rows(step, carry):
        to_orb, to_box = a_peer(step)
        a_to = (to_orb // 16) * 4 + to_box
        remote(part.at[a_to], rs.at[a_me], sems.at[0], sems.at[1], to_orb, to_box).start()
        return carry

    lax.fori_loop(1, 16, send_rows, 0)
    rs[a_me] = part[a_me]
    wait_for(rs.at[pl.ds(0, 15)], sems.at[1])
    bb[b_me] = jnp.sum(rs[...], axis=0)

    def send_sum(step, carry):
        to_orb, to_box = b_peer(step)
        remote(bb.at[b_me], bb.at[b_me], sems.at[2], sems.at[3], to_orb, to_box).start()
        return carry

    lax.fori_loop(1, 16, send_sum, 0)
    wait_for(bb.at[pl.ds(0, 15)], sems.at[3])
    mult[a_me] = jnp.sum(bb[...], axis=0)

    def send_total(step, carry):
        to_orb, to_box = a_peer(step)
        remote(mult.at[a_me], mult.at[a_me], sems.at[4], sems.at[5], to_orb, to_box).start()
        return carry

    lax.fori_loop(1, 16, send_total, 0)
    wait_for(mult.at[pl.ds(0, 15)], sems.at[5])
    m_hi, m_lo = split(mult[...].reshape(ORBS, ORBS).T)
    for k in range(8):
        lanes = pl.ds(k * 128, 128)
        fix = mm(m_hi, c_hi[:, lanes]) + mm(m_hi, c_lo[:, lanes]) + mm(m_lo, c_hi[:, lanes])
        value = a_hi[:, lanes].astype(F32) + a_lo[:, lanes].astype(F32) - fix
        resid2[pl.ds(k, ORBS, stride=8), :] = value

    z_rows = pl.ds(pl.multiple_of(8 + (orb // 32) * 8, 8), 8)
    lanes = pl.ds(pl.multiple_of((orb % 32) * 128, 128), 128)
    landing = ext.at[:, z_rows, lanes]
    mine = pltpu.make_async_copy(resid.at[pl.ds(orb * OWN, OWN)], landing, own)
    mine.start()

    def send_resid(step, carry):
        to = shifted(orb, step)
        remote(resid.at[pl.ds(to * OWN, OWN)], landing, sems.at[6], sems.at[7], to, box).start()
        return carry

    lax.fori_loop(1, ORB, send_resid, 0)
    mine.wait()
    wait_for(resid.at[pl.ds(0, OWN * (ORB - 1))], sems.at[7])
    up = remote(ext.at[:, pl.ds(20, 4), :], ext.at[:, pl.ds(4, 4), :], sems.at[8], sems.at[9], orb, (box + 1) % BOX)
    down = remote(ext.at[:, pl.ds(8, 4), :], ext.at[:, pl.ds(24, 4), :], sems.at[10], sems.at[11], orb, (box + 3) % BOX)
    up.start()
    down.start()
    wait_for(part.at[pl.ds(0, 15)], sems.at[0])
    wait_for(bb.at[pl.ds(0, 15)], sems.at[2])
    wait_for(mult.at[pl.ds(0, 15)], sems.at[4])
    wait_for(resid.at[pl.ds(0, OWN * (ORB - 1))], sems.at[6])
    up.wait()
    down.wait()


def relax_kernel(ext, mult, resid_out, direct_out):
    orb = lax.axis_index("orb")
    box = lax.axis_index("box")
    lane = lax.broadcasted_iota(jnp.int32, (32, PLANE), 1)
    row = lax.broadcasted_iota(jnp.int32, (32, PLANE), 0)
    inside = ((row >= 8) | (box > 0)) & ((row < 24) | (box < BOX - 1))
    col = lane % G
    for n in range(OWN):
        which = orb * OWN + n
        line = mult[pl.ds(which, 1), :]
        keep = lax.broadcasted_iota(jnp.int32, (1, ORBS), 1) == which
        diagonal = jnp.sum(jnp.where(keep, line, 0.0), axis=1, keepdims=True)
        denominator = 2.0 * coupling_z + 4.0 * coupling_xy + 1.0 + jnp.abs(diagonal)
        inverse = 1.0 / denominator
        resid = jnp.where(inside, ext[n], 0.0)
        resid_out[n] = resid[8:24]
        now = resid * inverse
        for _ in range(SWEEPS):
            side = jnp.where(col != 0, pltpu.roll(now, 1, 1), 0.0)
            side = side + jnp.where(col != G - 1, pltpu.roll(now, PLANE - 1, 1), 0.0)
            side = side + jnp.where(lane >= G, pltpu.roll(now, G, 1), 0.0)
            side = side + jnp.where(lane < PLANE - G, pltpu.roll(now, PLANE - G, 1), 0.0)
            along_z = pltpu.roll(now, 1, 0) + pltpu.roll(now, 31, 0)
            now = jnp.where(inside, (resid + coupling_xy * side + coupling_z * along_z) * inverse, 0.0)
        direct_out[n] = now[8:24]


DMA = pltpu.SemaphoreType.DMA


def shape(*dims, dtype=F32):
    return jax.ShapeDtypeStruct(dims, dtype)


def local(psi, potential, orbital_slot):
    z_in, z_out, into, back, kin = [jnp.asarray(t) for t in tables()]
    params = pltpu.CompilerParams(has_side_effects=True, vmem_limit_bytes=VLIMIT)
    pieces, cube, vfull = pl.pallas_call(
        exchange_kernel,
        out_shape=[shape(SLOTS * ORB, 8, 128), shape(2, G, PLANE), shape(G, PLANE)],
        in_specs=[ANY] * 2,
        out_specs=[ANY] * 3,
        scratch_shapes=[DMA((3,))] + [DMA] * 6,
        compiler_params=params,
        name="exchange",
    )(psi, potential)
    bf = lambda pad: pltpu.VMEM((TILES + 2 * pad, 2 * G, LANES), BF16)
    applied = pl.pallas_call(
        apply_kernel,
        out_shape=shape(2, G, PLANE),
        in_specs=[VMEM] * 7,
        out_specs=VMEM,
        scratch_shapes=[bf(KPAD), bf(KPAD), bf(FPAD), bf(FPAD), bf(FPAD), bf(FPAD), pltpu.VMEM((TILES, 2 * G, LANES), F32)],
        compiler_params=pltpu.CompilerParams(vmem_limit_bytes=VLIMIT),
        name="filters",
    )(cube, vfull, z_in, z_out, into, back, kin)
    app_pieces = pl.pallas_call(
        scatter_kernel,
        out_shape=shape(SLOTS * ORB, 8, 128),
        in_specs=[ANY],
        out_specs=ANY,
        scratch_shapes=[DMA] * 3,
        compiler_params=params,
        name="scatter",
    )(applied)
    table = lambda: pltpu.VMEM((ORBS, 1024), BF16)
    mult, ext = pl.pallas_call(
        reduce_kernel,
        out_shape=[shape(16, 16, ORBS), shape(OWN, 32, PLANE)],
        in_specs=[VMEM] * 3,
        out_specs=[VMEM, VMEM],
        scratch_shapes=[
            pltpu.VMEM((16, 16, ORBS), F32),
            pltpu.VMEM((16, 16, ORBS), F32),
            pltpu.VMEM((16, 16, ORBS), F32),
            pltpu.VMEM((ORBS, 8, 128), F32),
            table(), table(), table(), table(),
            DMA((12,)),
            DMA,
        ],
        compiler_params=params,
        name="reduce",
    )(pieces, app_pieces, orbital_slot.reshape(ORBS, 1))
    mult = mult.reshape(ORBS, ORBS)
    residual, direction = pl.pallas_call(
        relax_kernel,
        out_shape=[shape(OWN, DEPTH, PLANE)] * 2,
        in_specs=[VMEM] * 2,
        out_specs=[VMEM] * 2,
        compiler_params=pltpu.CompilerParams(vmem_limit_bytes=VLIMIT),
        name="relax",
    )(ext, mult)
    return residual, direction, mult


def solution(mesh):
    in_specs = (P("orb", "box", None), P("box", None), P())
    out_specs = (P("orb", "box", None), P("orb", "box", None), P())
    return jax.shard_map(local, mesh=mesh, in_specs=in_specs, out_specs=out_specs, check_vma=False)
```

```python
import math

import jax
import jax.numpy as jnp
import ml_dtypes
import numpy as np
from jax import lax
from jax.experimental import pallas as pl
from jax.experimental.pallas import tpu as pltpu
from jax.sharding import PartitionSpec as P

G = 64
MTAPS = 16
KREACH = 14
SWEEPS = 4
ORB, BOX = 64, 4
SLOTS, ORBS, OWN = 8, 256, 4
DEPTH = 16
PLANE = G * G
LANES = 256
TILES = PLANE // LANES
FPAD, KPAD = 2, 4

coupling_z = 4.0
coupling_xy = 1.0

F32, BF16 = jnp.float32, jnp.bfloat16
ANY = pl.BlockSpec(memory_space=pl.ANY)
VMEM = pl.BlockSpec(memory_space=pltpu.VMEM)
VLIMIT = 56 * 2**20


def magic_weights(tap_count):
    half_len = tap_count // 2
    offsets = np.arange(1 - half_len, half_len + 1) * 1.0
    weights = np.ones(tap_count)
    for index_a in range(tap_count):
        for index_b in range(tap_count):
            if index_b != index_a:
                weights[index_a] *= (0.25 - offsets[index_b]) / (
                    offsets[index_a] - offsets[index_b]
                )
    return weights


def second_weights(reach_cells):
    factor = math.factorial(reach_cells) ** 2
    weights = np.zeros(2 * reach_cells + 1)
    for distance in range(1, reach_cells + 1):
        entry_value = (
            2.0
            * (-1) ** (distance + 1)
            * factor
            / (
                distance
                * distance
                * math.factorial(reach_cells - distance)
                * math.factorial(reach_cells + distance)
            )
        )
        weights[reach_cells + distance] = entry_value
        weights[reach_cells - distance] = entry_value
    weights[reach_cells] = -weights.sum()
    return -0.5 * weights


def banded(row_count, col_count, row_start, col_start, weights, offset_low):
    row_index = np.arange(row_count)[:, None] + row_start
    col_index = np.arange(col_count)[None, :] + col_start
    position = row_index - col_index - offset_low
    inside = (position >= 0) & (position < len(weights))
    return np.where(inside, weights[np.clip(position, 0, len(weights) - 1)], 0.0)


def halves(table):
    table = np.asarray(table, np.float32)
    high = table.astype(ml_dtypes.bfloat16)
    low = (table - high.astype(np.float32)).astype(ml_dtypes.bfloat16)
    return high, low


def tables():
    magic = magic_weights(MTAPS)
    kinetic_row = second_weights(KREACH)
    forward = banded(G, G, 0, 0, magic, 1 - MTAPS // 2)
    kinetic = banded(G, G, 0, 0, kinetic_row, -KREACH)
    rows = LANES // G

    def beside(high, low):
        return np.concatenate([high, high, low], 1)

    z_in = beside(*halves(np.concatenate([forward.T, kinetic], 0)))
    z_out = beside(*halves(forward))
    into, back, kin = [], [], []
    for step in range(-FPAD, FPAD + 1):
        block = banded(rows, rows, rows * step, 0, magic, 1 - MTAPS // 2)
        into.append(np.kron(block, forward))
        block = banded(rows, rows, -rows * step, 0, magic, 1 - MTAPS // 2).T
        back.append(np.kron(block, forward.T))
    for step in range(-KPAD, KPAD + 1):
        block = np.kron(banded(rows, rows, rows * step, 0, kinetic_row, -KREACH), np.eye(G))
        if step == 0:
            block = block + np.kron(np.eye(rows), kinetic)
        kin.append(block)
    return [z_in, z_out] + [np.stack(halves(np.stack(m))) for m in (into, back, kin)]


def split(values):
    high = values.astype(BF16)
    return high, (values - high.astype(F32)).astype(BF16)


def mm(left, right):
    return jnp.dot(left, right, preferred_element_type=F32)


def place():
    orb = lax.axis_index("orb")
    box = lax.axis_index("box")
    return orb, box, orb // 16, (orb // 2) % 8, orb % 2


def shifted(orb, step):
    x, z, core = orb // 16, (orb // 2) % 8, orb % 2
    dx, dz, dc = step // 16, (step // 2) % 8, step % 2
    return ((x + dx) % 4) * 16 + ((z + dz) % 8) * 2 + (core + dc) % 2


def remote(src, dst, send, recv, orb, box):
    return pltpu.make_async_remote_copy(
        src_ref=src,
        dst_ref=dst,
        send_sem=send,
        recv_sem=recv,
        device_id={"orb": orb, "box": box},
        device_id_type=pl.DeviceIdType.MESH,
    )


def wait_for(ref, sem):
    pltpu.make_async_copy(ref, ref, sem).wait()


def tile_of(orb):
    return pl.ds(pl.multiple_of((orb // 32) * 8, 8), 8), pl.ds(
        pl.multiple_of((orb % 32) * 128, 128), 128
    )


CHUNKS = 4


def greet(orb, box, x, z, core, plane_sem):
    barrier = pltpu.get_barrier_semaphore()

    def signal(sem, to_orb, to_box):
        pl.semaphore_signal(
            sem, inc=1, device_id={"orb": to_orb, "box": to_box}, device_id_type=pl.DeviceIdType.MESH
        )

    def along_z(step, carry):
        signal(barrier, x * 16 + ((z + step) % 8) * 2 + core, box)
        return carry

    def across(sem):
        def body(step, carry):
            signal(sem, ((x + step // 2) % 4) * 16 + z * 2 + (core + step % 2) % 2, box)
            return carry

        return body

    def beside(sem):
        for step in range(1, BOX):
            signal(sem, orb, (box + step) % BOX)

    beside(barrier)
    lax.fori_loop(1, 8, along_z, 0)
    lax.fori_loop(1, 8, across(barrier), 0)
    pl.semaphore_wait(barrier, 7 + 7 + 3)
    lax.fori_loop(1, 8, across(plane_sem), 0)
    return beside


def filters(cube, vfull, z_in, z_out, into, back, kin, out, c_hi, c_lo, t_hi, t_lo, s_hi, s_lo, kz, arrived, tabled):
    for buf, pad in ((c_hi, KPAD), (c_lo, KPAD), (t_hi, FPAD), (t_lo, FPAD), (s_hi, FPAD), (s_lo, FPAD)):
        edge = jnp.zeros((pad, 2 * G, LANES), BF16)
        buf[pl.ds(0, pad)] = edge
        buf[pl.ds(TILES + pad, pad)] = edge

    def along_z(t, carry):
        lanes = pl.ds(pl.multiple_of(t * LANES, LANES), LANES)
        for s in range(2):
            rows = pl.ds(s * G, G)
            high, low = split(cube[s, :, lanes])
            c_hi[t + KPAD, rows, :] = high
            c_lo[t + KPAD, rows, :] = low
            both = mm(z_in[...], jnp.concatenate([high, low, high], 0))
            kz[t, rows, :] = both[G:]
            high, low = split(both[:G])
            t_hi[t + FPAD, rows, :] = high
            t_lo[t + FPAD, rows, :] = low
        return carry

    tabled()
    per = TILES // CHUNKS
    for chunk in range(CHUNKS):
        arrived(chunk)
        lax.fori_loop(chunk * per, (chunk + 1) * per, along_z, 0)
    group = 2

    def spread(hi, lo, table, count, first, acc):
        for d in range(count):
            high = hi[pl.ds(first + d, group)].reshape(group * 2 * G, LANES)
            low = lo[pl.ds(first + d, group)].reshape(group * 2 * G, LANES)
            term = mm(high, table[0, d]) + mm(low, table[0, d]) + mm(high, table[1, d])
            acc = term if acc is None else acc + term
        return acc

    def middle(i, carry):
        first = i * group
        grid = spread(t_hi, t_lo, into, 2 * FPAD + 1, first, None)
        for j in range(group):
            lanes = pl.ds(pl.multiple_of((first + j) * LANES, LANES), LANES)
            local = vfull[:, lanes]
            for s in range(2):
                low_row = (j * 2 + s) * G
                high, low = split(grid[low_row : low_row + G] * local)
                done = mm(z_out[...], jnp.concatenate([high, low, high], 0))
                high, low = split(done)
                s_hi[first + j + FPAD, pl.ds(s * G, G), :] = high
                s_lo[first + j + FPAD, pl.ds(s * G, G), :] = low
        return carry

    lax.fori_loop(0, TILES // group, middle, 0)

    def last(i, carry):
        first = i * group
        acc = kz[pl.ds(first, group)].reshape(group * 2 * G, LANES)
        acc = spread(c_hi, c_lo, kin, 2 * KPAD + 1, first, acc)
        acc = spread(s_hi, s_lo, back, 2 * FPAD + 1, first, acc)
        for j in range(group):
            lanes = pl.ds(pl.multiple_of((first + j) * LANES, LANES), LANES)
            for s in range(2):
                low_row = (j * 2 + s) * G
                out[s, :, lanes] = acc[low_row : low_row + G]
        return carry

    lax.fori_loop(0, TILES // group, last, 0)


def dot_nt(left, right):
    return lax.dot_general(left, right, (((1,), (1,)), ((), ())), preferred_element_type=F32)


def relax(resid, mult, which, box, resid_out, direct_out):
    lane = lax.broadcasted_iota(jnp.int32, (32, PLANE), 1)
    row = lax.broadcasted_iota(jnp.int32, (32, PLANE), 0)
    inside = ((row >= 8) | (box > 0)) & ((row < 24) | (box < BOX - 1))
    col = lane % G
    line = mult[which // 16, pl.ds(which % 16, 1), :]
    keep = lax.broadcasted_iota(jnp.int32, (1, ORBS), 1) == which
    diagonal = jnp.sum(jnp.where(keep, line, 0.0), axis=1, keepdims=True)
    denominator = 2.0 * coupling_z + 4.0 * coupling_xy + 1.0 + jnp.abs(diagonal)
    inverse = 1.0 / denominator
    resid = jnp.where(inside, resid, 0.0)
    resid_out[...] = resid[8:24]
    now = resid * inverse
    for _ in range(SWEEPS):
        side = jnp.where(col != 0, pltpu.roll(now, 1, 1), 0.0)
        side = side + jnp.where(col != G - 1, pltpu.roll(now, PLANE - 1, 1), 0.0)
        side = side + jnp.where(lane >= G, pltpu.roll(now, G, 1), 0.0)
        side = side + jnp.where(lane < PLANE - G, pltpu.roll(now, PLANE - G, 1), 0.0)
        along_z = pltpu.roll(now, 1, 0) + pltpu.roll(now, 31, 0)
        now = jnp.where(inside, (resid + coupling_xy * side + coupling_z * along_z) * inverse, 0.0)
    direct_out[...] = now[8:24]


def step_kernel(
    psi, pot, slots, z_in_h, z_out_h, into_h, back_h, kin_h,
    resid_out, direct_out, mult,
    pieces, app_pieces, cube, vfull, applied,
    z_in, z_out, into, back, kin,
    f_c_hi, f_c_lo, f_t_hi, f_t_lo, f_s_hi, f_s_lo, kz,
    part, rs, bb, resid, c_hi, c_lo, a_hi, a_lo, ext,
    own, y_send, y_recv, v_sem, p_sem, a_sem, r_sem, f_send, f_recv, h_send, h_recv, tab, plane_sem, all_sem,
):
    orb, box, x, z, core = place()
    table_copies = [
        pltpu.make_async_copy(src, dst, tab.at[i])
        for i, (src, dst) in enumerate(
            ((z_in_h, z_in), (z_out_h, z_out), (into_h, into), (back_h, back), (kin_h, kin))
        )
    ]
    for copy in table_copies:
        copy.start()
    slab = pl.ds(pl.multiple_of(box * DEPTH, DEPTH), DEPTH)
    width = PLANE // CHUNKS
    v_mine = pltpu.make_async_copy(pot, vfull.at[slab, :], own.at[0])
    v_mine.start()
    target = pl.ds(pl.multiple_of(orb * SLOTS, SLOTS), SLOTS)
    z_rows, lanes = tile_of(orb)
    p_mine = pltpu.make_async_copy(psi.at[:, z_rows, lanes], pieces.at[target], own.at[1])
    p_mine.start()
    c_mine = pltpu.make_async_copy(psi.at[pl.ds(2 * box, 2)], cube.at[:, slab, :], own.at[2])
    c_mine.start()

    beside = greet(orb, box, x, z, core, plane_sem)
    for chunk in range(CHUNKS):
        cols = pl.ds(chunk * width, width)
        for step in range(1, BOX):
            to = (box + step) % BOX
            remote(
                psi.at[pl.ds(2 * to, 2), :, cols], cube.at[:, slab, cols],
                y_send.at[chunk], y_recv.at[chunk], orb, to,
            ).start()
    for step in range(1, BOX):
        remote(pot, vfull.at[slab, :], v_sem.at[0], v_sem.at[1], orb, (box + step) % BOX).start()
    pl.semaphore_wait(plane_sem, 7)

    def send_psi(step, carry):
        to = shifted(orb, step)
        z_rows, lanes = tile_of(to)
        remote(psi.at[:, z_rows, lanes], pieces.at[target], p_sem.at[0], p_sem.at[1], to, box).start()
        return carry

    lax.fori_loop(1, ORB, send_psi, 0)
    beside(all_sem)

    def tabled():
        for copy in table_copies:
            copy.wait()

    def arrived(chunk):
        if chunk == 0:
            c_mine.wait()
        third = cube.at[:, pl.ds(0, 3 * DEPTH), pl.ds(chunk * width, width)]
        wait_for(third, y_recv.at[chunk])
        if chunk == CHUNKS - 1:
            v_mine.wait()
            wait_for(vfull.at[pl.ds(0, 3 * DEPTH)], v_sem.at[1])

    filters(
        cube, vfull, z_in, z_out, into, back, kin, applied,
        f_c_hi, f_c_lo, f_t_hi, f_t_lo, f_s_hi, f_s_lo, kz, arrived, tabled,
    )
    pl.semaphore_wait(all_sem, BOX - 1)

    a_target = pl.ds(orb * SLOTS + 2 * box, 2)

    def source(to_orb, to_box):
        z_rows = pl.ds(pl.multiple_of(to_box * DEPTH + (to_orb // 32) * 8, 8), 8)
        return applied.at[:, z_rows, pl.ds(pl.multiple_of((to_orb % 32) * 128, 128), 128)]

    a_mine = pltpu.make_async_copy(source(orb, box), app_pieces.at[a_target], own.at[3])
    a_mine.start()

    def send_applied(step, carry):
        to_orb = shifted(orb, step // BOX)
        to_box = (box + step % BOX) % BOX
        remote(
            source(to_orb, to_box), app_pieces.at[a_target], a_sem.at[0], a_sem.at[1], to_orb, to_box
        ).start()
        return carry

    lax.fori_loop(1, ORB * BOX, send_applied, 0)

    pieces2 = pieces.reshape(SLOTS * ORB * 8, 128)
    applied2 = app_pieces.reshape(SLOTS * ORB * 8, 128)
    resid2 = resid.reshape(ORBS * 8, 128)
    pick = (
        lax.broadcasted_iota(jnp.int32, (ORBS, SLOTS * ORB), 1) == slots[...]
    ).astype(F32).astype(BF16)

    def choose(ref, hi, lo):
        for k in range(8):
            lanes = pl.ds(k * 128, 128)
            high, low = split(ref[pl.ds(k, SLOTS * ORB, stride=8), :])
            hi[:, lanes] = mm(pick, high).astype(BF16)
            lo[:, lanes] = mm(pick, low).astype(BF16)

    p_mine.wait()
    wait_for(pieces.at[pl.ds(0, SLOTS * (ORB - 1))], p_sem.at[1])
    choose(pieces2, c_hi, c_lo)
    a_mine.wait()
    wait_for(app_pieces.at[pl.ds(0, SLOTS * ORB - 2)], a_sem.at[1])
    choose(applied2, a_hi, a_lo)

    scale = 1.0 / float(G**3)
    total = dot_nt(c_hi[...], a_hi[...]) + dot_nt(c_lo[...], a_hi[...]) + dot_nt(c_hi[...], a_lo[...])
    part[...] = (total * scale).reshape(16, 16, ORBS)

    a_me = x * 4 + box
    b_me = z * 2 + core

    def a_peer(step):
        return ((x + step // 4) % 4) * 16 + z * 2 + core, (box + step % 4) % 4

    def b_peer(step):
        return x * 16 + ((z + step // 2) % 8) * 2 + (core + step % 2) % 2, box

    def send_rows(step, carry):
        to_orb, to_box = a_peer(step)
        a_to = (to_orb // 16) * 4 + to_box
        remote(part.at[a_to], rs.at[a_me], r_sem.at[0], r_sem.at[1], to_orb, to_box).start()
        return carry

    lax.fori_loop(1, 16, send_rows, 0)
    rs[a_me] = part[a_me]
    wait_for(rs.at[pl.ds(0, 15)], r_sem.at[1])
    bb[b_me] = jnp.sum(rs[...], axis=0)

    def send_sum(step, carry):
        to_orb, to_box = b_peer(step)
        remote(bb.at[b_me], bb.at[b_me], r_sem.at[2], r_sem.at[3], to_orb, to_box).start()
        return carry

    lax.fori_loop(1, 16, send_sum, 0)
    wait_for(bb.at[pl.ds(0, 15)], r_sem.at[3])
    mult[a_me] = jnp.sum(bb[...], axis=0)

    def send_total(step, carry):
        to_orb, to_box = a_peer(step)
        remote(mult.at[a_me], mult.at[a_me], r_sem.at[4], r_sem.at[5], to_orb, to_box).start()
        return carry

    lax.fori_loop(1, 16, send_total, 0)
    wait_for(mult.at[pl.ds(0, 15)], r_sem.at[5])
    m_hi, m_lo = split(mult[...].reshape(ORBS, ORBS).T)
    for k in range(8):
        lanes = pl.ds(k * 128, 128)
        fix = mm(m_hi, c_hi[:, lanes]) + mm(m_hi, c_lo[:, lanes]) + mm(m_lo, c_hi[:, lanes])
        value = a_hi[:, lanes].astype(F32) + a_lo[:, lanes].astype(F32) - fix
        resid2[pl.ds(k, ORBS, stride=8), :] = value

    z_rows = pl.ds(pl.multiple_of(8 + (orb // 32) * 8, 8), 8)
    lanes = pl.ds(pl.multiple_of((orb % 32) * 128, 128), 128)
    r_mine = []
    for n in range(OWN):
        landing = ext.at[pl.ds(n, 1), z_rows, lanes]
        copy = pltpu.make_async_copy(resid.at[pl.ds(orb * OWN + n, 1)], landing, own.at[4 + n])
        copy.start()
        r_mine.append(copy)

        def send_resid(step, carry, n=n, landing=landing):
            to = shifted(orb, step)
            remote(resid.at[pl.ds(to * OWN + n, 1)], landing, f_send, f_recv.at[n], to, box).start()
            return carry

        lax.fori_loop(1, ORB, send_resid, 0)

    def halo(n):
        one = pl.ds(n, 1)
        up = remote(
            ext.at[one, pl.ds(20, 4), :], ext.at[one, pl.ds(4, 4), :],
            h_send.at[2 * n], h_recv.at[2 * n], orb, (box + 1) % BOX,
        )
        down = remote(
            ext.at[one, pl.ds(8, 4), :], ext.at[one, pl.ds(24, 4), :],
            h_send.at[2 * n + 1], h_recv.at[2 * n + 1], orb, (box + 3) % BOX,
        )
        up.start()
        down.start()
        return up, down

    def finish(n, pair):
        for copy in pair:
            copy.wait()
        relax(ext[n], mult, orb * OWN + n, box, resid_out.at[n], direct_out.at[n])

    pair = None
    for n in range(OWN):
        r_mine[n].wait()
        wait_for(resid.at[pl.ds(0, ORB - 1)], f_recv.at[n])
        following = halo(n)
        if pair is not None:
            finish(n - 1, pair)
        pair = following
    for chunk in range(CHUNKS):
        wait_for(cube.at[:, pl.ds(0, 3 * DEPTH), pl.ds(chunk * width, width)], y_send.at[chunk])
    wait_for(vfull.at[pl.ds(0, 3 * DEPTH)], v_sem.at[0])
    wait_for(pieces.at[pl.ds(0, SLOTS * (ORB - 1))], p_sem.at[0])
    wait_for(app_pieces.at[pl.ds(0, SLOTS * ORB - 2)], a_sem.at[0])
    wait_for(part.at[pl.ds(0, 15)], r_sem.at[0])
    wait_for(bb.at[pl.ds(0, 15)], r_sem.at[2])
    wait_for(mult.at[pl.ds(0, 15)], r_sem.at[4])
    wait_for(resid.at[pl.ds(0, OWN * (ORB - 1))], f_send)
    finish(OWN - 1, pair)


DMA = pltpu.SemaphoreType.DMA
REGULAR = pltpu.SemaphoreType.REGULAR


def shape(*dims, dtype=F32):
    return jax.ShapeDtypeStruct(dims, dtype)


def local(psi, potential, orbital_slot):
    consts = [jnp.asarray(t) for t in tables()]
    v32 = lambda *dims: pltpu.VMEM(dims, F32)
    v16 = lambda *dims: pltpu.VMEM(dims, BF16)
    padded = lambda pad: v16(TILES + 2 * pad, 2 * G, LANES)
    residual, direction, mult = pl.pallas_call(
        step_kernel,
        out_shape=[shape(OWN, DEPTH, PLANE), shape(OWN, DEPTH, PLANE), shape(16, 16, ORBS)],
        in_specs=[ANY, ANY, VMEM] + [ANY] * 5,
        out_specs=[VMEM] * 3,
        scratch_shapes=[
            v32(SLOTS * ORB, 8, 128), v32(SLOTS * ORB, 8, 128),
            v32(2, G, PLANE), v32(G, PLANE), v32(2, G, PLANE),
        ]
        + [v16(*t.shape) for t in consts]
        + [padded(KPAD)] * 2 + [padded(FPAD)] * 4 + [v32(TILES, 2 * G, LANES)]
        + [v32(16, 16, ORBS)] * 3 + [v32(ORBS, 8, 128)]
        + [v16(ORBS, 1024)] * 4 + [v32(OWN, 32, PLANE)]
        + [
            DMA((8,)), DMA((CHUNKS,)), DMA((CHUNKS,)), DMA((2,)), DMA((2,)), DMA((2,)), DMA((6,)),
            DMA, DMA((OWN,)), DMA((2 * OWN,)), DMA((2 * OWN,)), DMA((5,)), REGULAR, REGULAR,
        ],
        compiler_params=pltpu.CompilerParams(
            has_side_effects=True, vmem_limit_bytes=VLIMIT, collective_id=0
        ),
        name="orbital_step",
    )(psi, potential, orbital_slot.reshape(ORBS, 1), *consts)
    return residual, direction, mult.reshape(ORBS, ORBS)


def solution(mesh):
    in_specs = (P("orb", "box", None), P("box", None), P())
    out_specs = (P("orb", "box", None), P("orb", "box", None), P())
    return jax.shard_map(local, mesh=mesh, in_specs=in_specs, out_specs=out_specs, check_vma=False)
```

```python
import math

import jax
import jax.numpy as jnp
import ml_dtypes
import numpy as np
from jax import lax
from jax.experimental import pallas as pl
from jax.experimental.pallas import tpu as pltpu
from jax.sharding import PartitionSpec as P

G = 64
MTAPS = 16
KREACH = 14
SWEEPS = 4
ORB, BOX = 64, 4
SLOTS, ORBS, OWN = 8, 256, 4
DEPTH = 16
PLANE = G * G
LANES = 256
TILES = PLANE // LANES
FPAD, KPAD = 2, 4

coupling_z = 4.0
coupling_xy = 1.0

F32, BF16 = jnp.float32, jnp.bfloat16
ANY = pl.BlockSpec(memory_space=pl.ANY)
VMEM = pl.BlockSpec(memory_space=pltpu.VMEM)
VLIMIT = 56 * 2**20


def magic_weights(tap_count):
    half_len = tap_count // 2
    offsets = np.arange(1 - half_len, half_len + 1) * 1.0
    weights = np.ones(tap_count)
    for index_a in range(tap_count):
        for index_b in range(tap_count):
            if index_b != index_a:
                weights[index_a] *= (0.25 - offsets[index_b]) / (
                    offsets[index_a] - offsets[index_b]
                )
    return weights


def second_weights(reach_cells):
    factor = math.factorial(reach_cells) ** 2
    weights = np.zeros(2 * reach_cells + 1)
    for distance in range(1, reach_cells + 1):
        entry_value = (
            2.0
            * (-1) ** (distance + 1)
            * factor
            / (
                distance
                * distance
                * math.factorial(reach_cells - distance)
                * math.factorial(reach_cells + distance)
            )
        )
        weights[reach_cells + distance] = entry_value
        weights[reach_cells - distance] = entry_value
    weights[reach_cells] = -weights.sum()
    return -0.5 * weights


def banded(row_count, col_count, row_start, col_start, weights, offset_low):
    row_index = np.arange(row_count)[:, None] + row_start
    col_index = np.arange(col_count)[None, :] + col_start
    position = row_index - col_index - offset_low
    inside = (position >= 0) & (position < len(weights))
    return np.where(inside, weights[np.clip(position, 0, len(weights) - 1)], 0.0)


def halves(table):
    table = np.asarray(table, np.float32)
    high = table.astype(ml_dtypes.bfloat16)
    low = (table - high.astype(np.float32)).astype(ml_dtypes.bfloat16)
    return high, low


def tables():
    magic = magic_weights(MTAPS)
    kinetic_row = second_weights(KREACH)
    forward = banded(G, G, 0, 0, magic, 1 - MTAPS // 2)
    kinetic = banded(G, G, 0, 0, kinetic_row, -KREACH)
    rows = LANES // G

    def beside(high, low):
        return np.concatenate([high, high, low], 1)

    z_in = beside(*halves(np.concatenate([forward.T, kinetic], 0)))
    z_out = beside(*halves(forward))
    into, back, kin = [], [], []
    for step in range(-FPAD, FPAD + 1):
        block = banded(rows, rows, rows * step, 0, magic, 1 - MTAPS // 2)
        into.append(np.kron(block, forward))
        block = banded(rows, rows, -rows * step, 0, magic, 1 - MTAPS // 2).T
        back.append(np.kron(block, forward.T))
    for step in range(-KPAD, KPAD + 1):
        block = np.kron(banded(rows, rows, rows * step, 0, kinetic_row, -KREACH), np.eye(G))
        if step == 0:
            block = block + np.kron(np.eye(rows), kinetic)
        kin.append(block)
    return [z_in, z_out] + [np.stack(halves(np.stack(m))) for m in (into, back, kin)]


def split(values):
    high = values.astype(BF16)
    return high, (values - high.astype(F32)).astype(BF16)


def mm(left, right):
    return jnp.dot(left, right, preferred_element_type=F32)


def place():
    orb = lax.axis_index("orb")
    box = lax.axis_index("box")
    return orb, box, orb // 16, (orb // 2) % 8, orb % 2


def shifted(orb, step):
    x, z, core = orb // 16, (orb // 2) % 8, orb % 2
    dx, dz, dc = step // 16, (step // 2) % 8, step % 2
    return ((x + dx) % 4) * 16 + ((z + dz) % 8) * 2 + (core + dc) % 2


def remote(src, dst, send, recv, orb, box):
    return pltpu.make_async_remote_copy(
        src_ref=src,
        dst_ref=dst,
        send_sem=send,
        recv_sem=recv,
        device_id={"orb": orb, "box": box},
        device_id_type=pl.DeviceIdType.MESH,
    )


def wait_for(ref, sem):
    pltpu.make_async_copy(ref, ref, sem).wait()


def tile_of(orb):
    return pl.ds(pl.multiple_of((orb // 32) * 8, 8), 8), pl.ds(
        pl.multiple_of((orb % 32) * 128, 128), 128
    )


CHUNKS = 4


def greet(orb, box, x, z, core, plane_sem):
    barrier = pltpu.get_barrier_semaphore()

    def signal(sem, to_orb, to_box):
        pl.semaphore_signal(
            sem, inc=1, device_id={"orb": to_orb, "box": to_box}, device_id_type=pl.DeviceIdType.MESH
        )

    def along_z(step, carry):
        signal(barrier, x * 16 + ((z + step) % 8) * 2 + core, box)
        return carry

    def across(sem):
        def body(step, carry):
            signal(sem, ((x + step // 2) % 4) * 16 + z * 2 + (core + step % 2) % 2, box)
            return carry

        return body

    def beside(sem):
        for step in range(1, BOX):
            signal(sem, orb, (box + step) % BOX)

    beside(barrier)
    lax.fori_loop(1, 8, along_z, 0)
    lax.fori_loop(1, 8, across(barrier), 0)
    pl.semaphore_wait(barrier, 7 + 7 + 3)
    lax.fori_loop(1, 8, across(plane_sem), 0)
    return beside


def filters(cube, vfull, z_in, z_out, into, back, kin, out, c_hi, c_lo, t_hi, t_lo, s_hi, s_lo, kz, arrived, tabled):
    for buf, pad in ((c_hi, KPAD), (c_lo, KPAD), (t_hi, FPAD), (t_lo, FPAD), (s_hi, FPAD), (s_lo, FPAD)):
        edge = jnp.zeros((pad, 2 * G, LANES), BF16)
        buf[pl.ds(0, pad)] = edge
        buf[pl.ds(TILES + pad, pad)] = edge

    def along_z(t, carry):
        lanes = pl.ds(pl.multiple_of(t * LANES, LANES), LANES)
        for s in range(2):
            rows = pl.ds(s * G, G)
            high, low = split(cube[s, :, lanes])
            c_hi[t + KPAD, rows, :] = high
            c_lo[t + KPAD, rows, :] = low
            both = mm(z_in[...], jnp.concatenate([high, low, high], 0))
            kz[t, rows, :] = both[G:]
            high, low = split(both[:G])
            t_hi[t + FPAD, rows, :] = high
            t_lo[t + FPAD, rows, :] = low
        return carry

    group = 2

    def spread(hi, lo, table, count, first, acc):
        for d in range(count):
            high = hi[pl.ds(first + d, group)].reshape(group * 2 * G, LANES)
            low = lo[pl.ds(first + d, group)].reshape(group * 2 * G, LANES)
            term = mm(high, table[0, d]) + mm(low, table[0, d]) + mm(high, table[1, d])
            acc = term if acc is None else acc + term
        return acc

    def middle(i, carry):
        first = i * group
        grid = spread(t_hi, t_lo, into, 2 * FPAD + 1, first, None)
        for j in range(group):
            lanes = pl.ds(pl.multiple_of((first + j) * LANES, LANES), LANES)
            local = vfull[:, lanes]
            for s in range(2):
                low_row = (j * 2 + s) * G
                high, low = split(grid[low_row : low_row + G] * local)
                done = mm(z_out[...], jnp.concatenate([high, low, high], 0))
                high, low = split(done)
                s_hi[first + j + FPAD, pl.ds(s * G, G), :] = high
                s_lo[first + j + FPAD, pl.ds(s * G, G), :] = low
        return carry

    def kinetic(i, carry):
        first = i * group
        acc = kz[pl.ds(first, group)].reshape(group * 2 * G, LANES)
        acc = spread(c_hi, c_lo, kin, 2 * KPAD + 1, first, acc)
        kz[pl.ds(first, group)] = acc.reshape(group, 2 * G, LANES)
        return carry

    tabled()
    per = TILES // CHUNKS
    for chunk in range(CHUNKS - 1):
        arrived(chunk)
        lax.fori_loop(chunk * per, (chunk + 1) * per, along_z, 0)
    early = (TILES - per - KPAD) // group
    lax.fori_loop(0, early, kinetic, 0)
    lax.fori_loop(0, early, middle, 0)
    arrived(CHUNKS - 1)
    lax.fori_loop(TILES - per, TILES, along_z, 0)
    lax.fori_loop(early, TILES // group, middle, 0)
    lax.fori_loop(early, TILES // group, kinetic, 0)

    def last(i, carry):
        first = i * group
        acc = kz[pl.ds(first, group)].reshape(group * 2 * G, LANES)
        acc = spread(s_hi, s_lo, back, 2 * FPAD + 1, first, acc)
        for j in range(group):
            lanes = pl.ds(pl.multiple_of((first + j) * LANES, LANES), LANES)
            for s in range(2):
                low_row = (j * 2 + s) * G
                out[s, :, lanes] = acc[low_row : low_row + G]
        return carry

    lax.fori_loop(0, TILES // group, last, 0)


def dot_nt(left, right):
    return lax.dot_general(left, right, (((1,), (1,)), ((), ())), preferred_element_type=F32)


def relax(resid, mult, which, box, resid_out, direct_out):
    lane = lax.broadcasted_iota(jnp.int32, (32, PLANE), 1)
    row = lax.broadcasted_iota(jnp.int32, (32, PLANE), 0)
    inside = ((row >= 8) | (box > 0)) & ((row < 24) | (box < BOX - 1))
    col = lane % G
    line = mult[which // 8, pl.ds(which % 8, 1), :]
    keep = lax.broadcasted_iota(jnp.int32, (1, ORBS), 1) == which
    diagonal = jnp.sum(jnp.where(keep, line, 0.0), axis=1, keepdims=True)
    denominator = 2.0 * coupling_z + 4.0 * coupling_xy + 1.0 + jnp.abs(diagonal)
    inverse = 1.0 / denominator
    resid = jnp.where(inside, resid, 0.0)
    resid_out[...] = resid[8:24]
    now = resid * inverse
    for _ in range(SWEEPS):
        side = jnp.where(col != 0, pltpu.roll(now, 1, 1), 0.0)
        side = side + jnp.where(col != G - 1, pltpu.roll(now, PLANE - 1, 1), 0.0)
        side = side + jnp.where(lane >= G, pltpu.roll(now, G, 1), 0.0)
        side = side + jnp.where(lane < PLANE - G, pltpu.roll(now, PLANE - G, 1), 0.0)
        along_z = pltpu.roll(now, 1, 0) + pltpu.roll(now, 31, 0)
        now = jnp.where(inside, (resid + coupling_xy * side + coupling_z * along_z) * inverse, 0.0)
    direct_out[...] = now[8:24]


def step_kernel(
    psi, pot, slots, z_in_h, z_out_h, into_h, back_h, kin_h,
    resid_out, direct_out, mult,
    pieces, app_pieces, cube, vfull, applied,
    z_in, z_out, into, back, kin,
    f_c_hi, f_c_lo, f_t_hi, f_t_lo, f_s_hi, f_s_lo, kz,
    part, rs, bb, resid, c_hi, c_lo, a_hi, a_lo, ext,
    own, y_send, y_recv, v_sem, p_sem, a_sem, r_sem, f_send, f_recv, h_send, h_recv, tab, plane_sem, all_sem,
):
    orb, box, x, z, core = place()
    table_copies = [
        pltpu.make_async_copy(src, dst, tab.at[i])
        for i, (src, dst) in enumerate(
            ((z_in_h, z_in), (z_out_h, z_out), (into_h, into), (back_h, back), (kin_h, kin))
        )
    ]
    for copy in table_copies:
        copy.start()
    slab = pl.ds(pl.multiple_of(box * DEPTH, DEPTH), DEPTH)
    width = PLANE // CHUNKS
    v_mine = pltpu.make_async_copy(pot, vfull.at[slab, :], own.at[0])
    v_mine.start()
    target = pl.ds(pl.multiple_of(orb * SLOTS, SLOTS), SLOTS)
    z_rows, lanes = tile_of(orb)
    p_mine = pltpu.make_async_copy(psi.at[:, z_rows, lanes], pieces.at[target], own.at[1])
    p_mine.start()
    c_mine = pltpu.make_async_copy(psi.at[pl.ds(2 * box, 2)], cube.at[:, slab, :], own.at[2])
    c_mine.start()

    beside = greet(orb, box, x, z, core, plane_sem)
    for chunk in range(CHUNKS):
        cols = pl.ds(chunk * width, width)
        for step in range(1, BOX):
            to = (box + step) % BOX
            remote(
                psi.at[pl.ds(2 * to, 2), :, cols], cube.at[:, slab, cols],
                y_send.at[chunk], y_recv.at[chunk], orb, to,
            ).start()
            if chunk == CHUNKS - 2:
                remote(pot, vfull.at[slab, :], v_sem.at[0], v_sem.at[1], orb, to).start()
    pl.semaphore_wait(plane_sem, 7)

    def send_psi(step, carry):
        to = shifted(orb, step)
        z_rows, lanes = tile_of(to)
        remote(psi.at[:, z_rows, lanes], pieces.at[target], p_sem.at[0], p_sem.at[1], to, box).start()
        return carry

    lax.fori_loop(1, ORB, send_psi, 0)
    beside(all_sem)

    def tabled():
        for copy in table_copies:
            copy.wait()

    def arrived(chunk):
        if chunk == 0:
            c_mine.wait()
        third = cube.at[:, pl.ds(0, 3 * DEPTH), pl.ds(chunk * width, width)]
        wait_for(third, y_recv.at[chunk])
        if chunk == CHUNKS - 2:
            v_mine.wait()
            wait_for(vfull.at[pl.ds(0, 3 * DEPTH)], v_sem.at[1])

    filters(
        cube, vfull, z_in, z_out, into, back, kin, applied,
        f_c_hi, f_c_lo, f_t_hi, f_t_lo, f_s_hi, f_s_lo, kz, arrived, tabled,
    )
    pl.semaphore_wait(all_sem, BOX - 1)

    a_target = pl.ds(orb * SLOTS + 2 * box, 2)

    def source(to_orb, to_box):
        z_rows = pl.ds(pl.multiple_of(to_box * DEPTH + (to_orb // 32) * 8, 8), 8)
        return applied.at[:, z_rows, pl.ds(pl.multiple_of((to_orb % 32) * 128, 128), 128)]

    a_mine = pltpu.make_async_copy(source(orb, box), app_pieces.at[a_target], own.at[3])
    a_mine.start()

    def send_applied(step, carry):
        to_orb = shifted(orb, step // BOX)
        to_box = (box + step % BOX) % BOX
        remote(
            source(to_orb, to_box), app_pieces.at[a_target], a_sem.at[0], a_sem.at[1], to_orb, to_box
        ).start()
        return carry

    lax.fori_loop(1, ORB * BOX, send_applied, 0)

    pieces2 = pieces.reshape(SLOTS * ORB * 8, 128)
    applied2 = app_pieces.reshape(SLOTS * ORB * 8, 128)
    resid2 = resid.reshape(ORBS * 8, 128)
    wanted = jnp.broadcast_to(slots[...].astype(F32), (ORBS, ORBS)).T
    column = lax.broadcasted_iota(jnp.int32, (ORBS, ORBS), 1).astype(F32)
    pick = jnp.concatenate(
        [(column + float(k * ORBS) == wanted).astype(F32) for k in range(SLOTS * ORB // ORBS)], 1
    ).astype(BF16)

    def choose(ref, hi, lo):
        for k in range(8):
            lanes = pl.ds(k * 128, 128)
            high, low = split(ref[pl.ds(k, SLOTS * ORB, stride=8), :])
            hi[:, lanes] = mm(pick, high).astype(BF16)
            lo[:, lanes] = mm(pick, low).astype(BF16)

    p_mine.wait()
    wait_for(pieces.at[pl.ds(0, SLOTS * (ORB - 1))], p_sem.at[1])
    choose(pieces2, c_hi, c_lo)
    a_mine.wait()
    wait_for(app_pieces.at[pl.ds(0, SLOTS * ORB - 2)], a_sem.at[1])
    choose(applied2, a_hi, a_lo)

    scale = 1.0 / float(G**3)
    total = dot_nt(c_hi[...], a_hi[...]) + dot_nt(c_lo[...], a_hi[...]) + dot_nt(c_hi[...], a_lo[...])
    part[...] = (total * scale).reshape(32, 8, ORBS)

    a_me = (x * 4 + box) * 2 + core

    def a_peer(step):
        to_orb = ((x + step // 8) % 4) * 16 + z * 2 + (core + step % 2) % 2
        return to_orb, (box + (step // 2) % 4) % 4

    for step in range(1, 32):
        to_orb, to_box = a_peer(step)
        a_to = ((to_orb // 16) * 4 + to_box) * 2 + to_orb % 2
        remote(part.at[a_to], rs.at[a_me], r_sem.at[0], r_sem.at[1], to_orb, to_box).start()
    rs[a_me] = part[a_me]
    wait_for(rs.at[pl.ds(0, 31)], r_sem.at[1])
    bb[z] = jnp.sum(rs[...], axis=0)
    for step in range(1, 8):
        to_orb = x * 16 + ((z + step) % 8) * 2 + core
        remote(bb.at[z], bb.at[z], r_sem.at[2], r_sem.at[3], to_orb, box).start()
    wait_for(bb.at[pl.ds(0, 7)], r_sem.at[3])
    mult[a_me] = jnp.sum(bb[...], axis=0)
    for step in range(1, 32):
        to_orb, to_box = a_peer(step)
        remote(mult.at[a_me], mult.at[a_me], r_sem.at[4], r_sem.at[5], to_orb, to_box).start()
    wait_for(mult.at[pl.ds(0, 31)], r_sem.at[5])
    m_hi, m_lo = split(mult[...].reshape(ORBS, ORBS).T)
    for k in range(8):
        lanes = pl.ds(k * 128, 128)
        fix = mm(m_hi, c_hi[:, lanes]) + mm(m_hi, c_lo[:, lanes]) + mm(m_lo, c_hi[:, lanes])
        value = a_hi[:, lanes].astype(F32) + a_lo[:, lanes].astype(F32) - fix
        resid2[pl.ds(k, ORBS, stride=8), :] = value

    z_rows = pl.ds(pl.multiple_of(8 + (orb // 32) * 8, 8), 8)
    lanes = pl.ds(pl.multiple_of((orb % 32) * 128, 128), 128)
    r_mine = []
    for n in range(OWN):
        landing = ext.at[pl.ds(n, 1), z_rows, lanes]
        copy = pltpu.make_async_copy(resid.at[pl.ds(orb * OWN + n, 1)], landing, own.at[4 + n])
        copy.start()
        r_mine.append(copy)

        def send_resid(step, carry, n=n, landing=landing):
            to = shifted(orb, step)
            remote(resid.at[pl.ds(to * OWN + n, 1)], landing, f_send, f_recv.at[n], to, box).start()
            return carry

        lax.fori_loop(1, ORB, send_resid, 0)

    def halo(n):
        one = pl.ds(n, 1)
        up = remote(
            ext.at[one, pl.ds(20, 4), :], ext.at[one, pl.ds(4, 4), :],
            h_send.at[2 * n], h_recv.at[2 * n], orb, (box + 1) % BOX,
        )
        down = remote(
            ext.at[one, pl.ds(8, 4), :], ext.at[one, pl.ds(24, 4), :],
            h_send.at[2 * n + 1], h_recv.at[2 * n + 1], orb, (box + 3) % BOX,
        )
        up.start()
        down.start()
        return up, down

    def finish(n, pair):
        for copy in pair:
            copy.wait()
        relax(ext[n], mult, orb * OWN + n, box, resid_out.at[n], direct_out.at[n])

    pair = None
    for n in range(OWN):
        r_mine[n].wait()
        wait_for(resid.at[pl.ds(0, ORB - 1)], f_recv.at[n])
        following = halo(n)
        if pair is not None:
            finish(n - 1, pair)
        pair = following
    for chunk in range(CHUNKS):
        wait_for(cube.at[:, pl.ds(0, 3 * DEPTH), pl.ds(chunk * width, width)], y_send.at[chunk])
    wait_for(vfull.at[pl.ds(0, 3 * DEPTH)], v_sem.at[0])
    wait_for(pieces.at[pl.ds(0, SLOTS * (ORB - 1))], p_sem.at[0])
    wait_for(app_pieces.at[pl.ds(0, SLOTS * ORB - 2)], a_sem.at[0])
    wait_for(part.at[pl.ds(0, 31)], r_sem.at[0])
    wait_for(bb.at[pl.ds(0, 7)], r_sem.at[2])
    wait_for(mult.at[pl.ds(0, 31)], r_sem.at[4])
    wait_for(resid.at[pl.ds(0, OWN * (ORB - 1))], f_send)
    finish(OWN - 1, pair)


DMA = pltpu.SemaphoreType.DMA
REGULAR = pltpu.SemaphoreType.REGULAR


def shape(*dims, dtype=F32):
    return jax.ShapeDtypeStruct(dims, dtype)


def local(psi, potential, orbital_slot):
    consts = [jnp.asarray(t) for t in tables()]
    v32 = lambda *dims: pltpu.VMEM(dims, F32)
    v16 = lambda *dims: pltpu.VMEM(dims, BF16)
    padded = lambda pad: v16(TILES + 2 * pad, 2 * G, LANES)
    residual, direction, mult = pl.pallas_call(
        step_kernel,
        out_shape=[v32(OWN, DEPTH, PLANE), v32(OWN, DEPTH, PLANE), v32(32, 8, ORBS)],
        in_specs=[ANY, ANY, VMEM] + [ANY] * 5,
        out_specs=[VMEM] * 3,
        scratch_shapes=[
            v32(SLOTS * ORB, 8, 128), v32(SLOTS * ORB, 8, 128),
            v32(2, G, PLANE), v32(G, PLANE), v32(2, G, PLANE),
        ]
        + [v16(*t.shape) for t in consts]
        + [padded(KPAD)] * 2 + [padded(FPAD)] * 4 + [v32(TILES, 2 * G, LANES)]
        + [v32(32, 8, ORBS)] * 2 + [v32(8, 8, ORBS)] + [v32(ORBS, 8, 128)]
        + [v16(ORBS, 1024)] * 4 + [v32(OWN, 32, PLANE)]
        + [
            DMA((8,)), DMA((CHUNKS,)), DMA((CHUNKS,)), DMA((2,)), DMA((2,)), DMA((2,)), DMA((6,)),
            DMA, DMA((OWN,)), DMA((2 * OWN,)), DMA((2 * OWN,)), DMA((5,)), REGULAR, REGULAR,
        ],
        compiler_params=pltpu.CompilerParams(
            has_side_effects=True, vmem_limit_bytes=VLIMIT, collective_id=0
        ),
        name="orbital_step",
    )(psi, potential, orbital_slot.reshape(1, ORBS), *consts)
    return residual, direction, mult.reshape(ORBS, ORBS)


def solution(mesh):
    in_specs = (P("orb", "box", None), P("box", None), P())
    out_specs = (P("orb", "box", None), P("orb", "box", None), P())
    return jax.shard_map(local, mesh=mesh, in_specs=in_specs, out_specs=out_specs, check_vma=False)
```

```python
import math

import jax
import jax.numpy as jnp
import ml_dtypes
import numpy as np
from jax import lax
from jax.experimental import pallas as pl
from jax.experimental.pallas import tpu as pltpu
from jax.sharding import PartitionSpec as P

G = 64
MTAPS = 16
KREACH = 14
SWEEPS = 4
ORB, BOX = 64, 4
SLOTS, ORBS, OWN = 8, 256, 4
DEPTH = 16
PLANE = G * G
LANES = 256
TILES = PLANE // LANES
FPAD, KPAD = 2, 4

coupling_z = 4.0
coupling_xy = 1.0

F32, BF16 = jnp.float32, jnp.bfloat16
ANY = pl.BlockSpec(memory_space=pl.ANY)
VMEM = pl.BlockSpec(memory_space=pltpu.VMEM)
VLIMIT = 56 * 2**20


def magic_weights(tap_count):
    half_len = tap_count // 2
    offsets = np.arange(1 - half_len, half_len + 1) * 1.0
    weights = np.ones(tap_count)
    for index_a in range(tap_count):
        for index_b in range(tap_count):
            if index_b != index_a:
                weights[index_a] *= (0.25 - offsets[index_b]) / (
                    offsets[index_a] - offsets[index_b]
                )
    return weights


def second_weights(reach_cells):
    factor = math.factorial(reach_cells) ** 2
    weights = np.zeros(2 * reach_cells + 1)
    for distance in range(1, reach_cells + 1):
        entry_value = (
            2.0
            * (-1) ** (distance + 1)
            * factor
            / (
                distance
                * distance
                * math.factorial(reach_cells - distance)
                * math.factorial(reach_cells + distance)
            )
        )
        weights[reach_cells + distance] = entry_value
        weights[reach_cells - distance] = entry_value
    weights[reach_cells] = -weights.sum()
    return -0.5 * weights


def banded(row_count, col_count, row_start, col_start, weights, offset_low):
    row_index = np.arange(row_count)[:, None] + row_start
    col_index = np.arange(col_count)[None, :] + col_start
    position = row_index - col_index - offset_low
    inside = (position >= 0) & (position < len(weights))
    return np.where(inside, weights[np.clip(position, 0, len(weights) - 1)], 0.0)


def halves(table):
    table = np.asarray(table, np.float32)
    high = table.astype(ml_dtypes.bfloat16)
    low = (table - high.astype(np.float32)).astype(ml_dtypes.bfloat16)
    return high, low


def tables():
    magic = magic_weights(MTAPS)
    kinetic_row = second_weights(KREACH)
    forward = banded(G, G, 0, 0, magic, 1 - MTAPS // 2)
    kinetic = banded(G, G, 0, 0, kinetic_row, -KREACH)
    rows = LANES // G

    def beside(high, low):
        return np.concatenate([high, high, low], 1)

    z_in = beside(*halves(np.concatenate([forward.T, kinetic], 0)))
    z_out = beside(*halves(forward))
    into, back, kin = [], [], []
    for step in range(-FPAD, FPAD + 1):
        block = banded(rows, rows, rows * step, 0, magic, 1 - MTAPS // 2)
        into.append(np.kron(block, forward))
        block = banded(rows, rows, -rows * step, 0, magic, 1 - MTAPS // 2).T
        back.append(np.kron(block, forward.T))
    for step in range(-KPAD, KPAD + 1):
        block = np.kron(banded(rows, rows, rows * step, 0, kinetic_row, -KREACH), np.eye(G))
        if step == 0:
            block = block + np.kron(np.eye(rows), kinetic)
        kin.append(block)
    return [z_in, z_out] + [np.stack(halves(np.stack(m))) for m in (into, back, kin)]


def split(values):
    high = values.astype(BF16)
    return high, (values - high.astype(F32)).astype(BF16)


def mm(left, right):
    return jnp.dot(left, right, preferred_element_type=F32)


def place():
    orb = lax.axis_index("orb")
    box = lax.axis_index("box")
    return orb, box, orb // 16, (orb // 2) % 8, orb % 2


def shifted(orb, step):
    x, z, core = orb // 16, (orb // 2) % 8, orb % 2
    dx, dz, dc = step // 16, (step // 2) % 8, step % 2
    return ((x + dx) % 4) * 16 + ((z + dz) % 8) * 2 + (core + dc) % 2


def remote(src, dst, send, recv, orb, box):
    return pltpu.make_async_remote_copy(
        src_ref=src,
        dst_ref=dst,
        send_sem=send,
        recv_sem=recv,
        device_id={"orb": orb, "box": box},
        device_id_type=pl.DeviceIdType.MESH,
    )


def wait_for(ref, sem):
    pltpu.make_async_copy(ref, ref, sem).wait()


def tile_of(orb):
    return pl.ds(pl.multiple_of((orb // 32) * 8, 8), 8), pl.ds(
        pl.multiple_of((orb % 32) * 128, 128), 128
    )


CHUNKS = 4


def greet(orb, box, x, z, core, plane_sem):
    barrier = pltpu.get_barrier_semaphore()

    def signal(sem, to_orb, to_box):
        pl.semaphore_signal(
            sem, inc=1, device_id={"orb": to_orb, "box": to_box}, device_id_type=pl.DeviceIdType.MESH
        )

    def along_z(step, carry):
        signal(barrier, x * 16 + ((z + step) % 8) * 2 + core, box)
        return carry

    def across(sem):
        def body(step, carry):
            signal(sem, ((x + step // 2) % 4) * 16 + z * 2 + (core + step % 2) % 2, box)
            return carry

        return body

    def beside(sem):
        for step in range(1, BOX):
            signal(sem, orb, (box + step) % BOX)

    beside(barrier)
    lax.fori_loop(1, 8, along_z, 0)
    lax.fori_loop(1, 8, across(barrier), 0)
    pl.semaphore_wait(barrier, 7 + 7 + 3)
    lax.fori_loop(1, 8, across(plane_sem), 0)
    return beside


def filters(cube, vfull, z_in, z_out, into, back, kin, out, c_hi, c_lo, t_hi, t_lo, s_hi, s_lo, kz, arrived, tabled):
    for buf, pad in ((c_hi, KPAD), (c_lo, KPAD), (t_hi, FPAD), (t_lo, FPAD), (s_hi, FPAD), (s_lo, FPAD)):
        edge = jnp.zeros((pad, 2 * G, LANES), BF16)
        buf[pl.ds(0, pad)] = edge
        buf[pl.ds(TILES + pad, pad)] = edge

    def along_z(t, carry):
        lanes = pl.ds(pl.multiple_of(t * LANES, LANES), LANES)
        for s in range(2):
            rows = pl.ds(s * G, G)
            high, low = split(cube[s, :, lanes])
            c_hi[t + KPAD, rows, :] = high
            c_lo[t + KPAD, rows, :] = low
            both = mm(z_in[...], jnp.concatenate([high, low, high], 0))
            kz[t, rows, :] = both[G:]
            high, low = split(both[:G])
            t_hi[t + FPAD, rows, :] = high
            t_lo[t + FPAD, rows, :] = low
        return carry

    group = 2

    def spread(hi, lo, table, count, first, acc):
        for d in range(count):
            high = hi[pl.ds(first + d, group)].reshape(group * 2 * G, LANES)
            low = lo[pl.ds(first + d, group)].reshape(group * 2 * G, LANES)
            term = mm(high, table[0, d]) + mm(low, table[0, d]) + mm(high, table[1, d])
            acc = term if acc is None else acc + term
        return acc

    def middle(i, carry):
        first = i * group
        grid = spread(t_hi, t_lo, into, 2 * FPAD + 1, first, None)
        for j in range(group):
            lanes = pl.ds(pl.multiple_of((first + j) * LANES, LANES), LANES)
            local = vfull[:, lanes]
            for s in range(2):
                low_row = (j * 2 + s) * G
                high, low = split(grid[low_row : low_row + G] * local)
                done = mm(z_out[...], jnp.concatenate([high, low, high], 0))
                high, low = split(done)
                s_hi[first + j + FPAD, pl.ds(s * G, G), :] = high
                s_lo[first + j + FPAD, pl.ds(s * G, G), :] = low
        return carry

    def kinetic(i, carry):
        first = i * group
        acc = kz[pl.ds(first, group)].reshape(group * 2 * G, LANES)
        acc = spread(c_hi, c_lo, kin, 2 * KPAD + 1, first, acc)
        kz[pl.ds(first, group)] = acc.reshape(group, 2 * G, LANES)
        return carry

    tabled()
    per = TILES // CHUNKS
    for chunk in range(CHUNKS - 1):
        arrived(chunk)
        lax.fori_loop(chunk * per, (chunk + 1) * per, along_z, 0)
    early = (TILES - per - KPAD) // group
    lax.fori_loop(0, early, kinetic, 0)
    lax.fori_loop(0, early, middle, 0)
    arrived(CHUNKS - 1)
    lax.fori_loop(TILES - per, TILES, along_z, 0)
    lax.fori_loop(early, TILES // group, middle, 0)
    lax.fori_loop(early, TILES // group, kinetic, 0)

    def last(i, carry):
        first = i * group
        acc = kz[pl.ds(first, group)].reshape(group * 2 * G, LANES)
        acc = spread(s_hi, s_lo, back, 2 * FPAD + 1, first, acc)
        for j in range(group):
            lanes = pl.ds(pl.multiple_of((first + j) * LANES, LANES), LANES)
            for s in range(2):
                low_row = (j * 2 + s) * G
                out[s, :, lanes] = acc[low_row : low_row + G]
        return carry

    lax.fori_loop(0, TILES // group, last, 0)


def dot_nt(left, right):
    return lax.dot_general(left, right, (((1,), (1,)), ((), ())), preferred_element_type=F32)


def inverse_of(mult_t, which):
    line = mult_t[which // 8, pl.ds(which % 8, 1), :]
    keep = lax.broadcasted_iota(jnp.int32, (1, ORBS), 1) == which
    diagonal = jnp.sum(jnp.where(keep, line, 0.0), axis=1, keepdims=True)
    return 1.0 / (2.0 * coupling_z + 4.0 * coupling_xy + 1.0 + jnp.abs(diagonal))


def relax(resid, inverse, box, direct_out):
    lane = lax.broadcasted_iota(jnp.int32, (32, 128), 1)
    row = lax.broadcasted_iota(jnp.int32, (32, 128), 0)
    inside = ((row >= 8) | (box > 0)) & ((row < 24) | (box < BOX - 1))
    factor = jnp.where(inside, jnp.broadcast_to(inverse, (32, 128)), 0.0)
    first_col, last_col, first_row = lane % G == 0, lane % G == G - 1, lane < G
    count = PLANE // 128
    start = [jnp.where(inside, resid[:, k * 128 : (k + 1) * 128], 0.0) for k in range(count)]
    now = [part * factor for part in start]
    for _ in range(SWEEPS):
        turned = [pltpu.roll(part, G, 1) for part in now]
        pairs = [turned[0]] + [turned[k - 1] + turned[k] for k in range(1, count)] + [turned[-1]]
        following = []
        for k in range(count):
            side = jnp.where(first_row, pairs[k], pairs[k + 1])
            side = side + jnp.where(first_col, 0.0, pltpu.roll(now[k], 1, 1))
            side = side + jnp.where(last_col, 0.0, pltpu.roll(now[k], 127, 1))
            along_z = pltpu.roll(now[k], 1, 0) + pltpu.roll(now[k], 31, 0)
            following.append((start[k] + coupling_xy * side + coupling_z * along_z) * factor)
        now = following
    for k in range(count):
        direct_out[:, k * 128 : (k + 1) * 128] = now[k][8:24]


def finish_kernel(resid, direct, mult, ext, inverse, resid_out, direct_out, mult_out, last, sems):
    box = lax.axis_index("box")
    done = pl.ds(0, OWN - 1)
    copies = [
        pltpu.make_async_copy(direct, direct_out.at[done], sems.at[0]),
        pltpu.make_async_copy(resid, resid_out.at[done], sems.at[1]),
        pltpu.make_async_copy(ext.at[pl.ds(8, DEPTH)], resid_out.at[OWN - 1], sems.at[2]),
        pltpu.make_async_copy(mult, mult_out, sems.at[3]),
    ]
    for copy in copies:
        copy.start()
    relax(ext[...], inverse[0:1, 0:1], box, last)
    copies.append(pltpu.make_async_copy(last, direct_out.at[OWN - 1], sems.at[4]))
    copies[-1].start()
    for copy in copies:
        copy.wait()


def step_kernel(
    psi, pot, slots, z_in_h, z_out_h, into_h, back_h, kin_h,
    resid_out, direct_out, mult_out, ext_out, inverse_out,
    pieces, app_pieces, cube, vfull, applied,
    z_in, z_out, into, back, kin,
    f_c_hi, f_c_lo, f_t_hi, f_t_lo, f_s_hi, f_s_lo, kz,
    part, rs, bb, mult, resid, c_hi, c_lo, a_hi, a_lo, a_sum, m_side, ext,
    own, y_send, y_recv, v_sem, p_sem, a_sem, r_sem, f_send, f_recv, h_send, h_recv, tab, plane_sem, all_sem,
):
    orb, box, x, z, core = place()
    table_copies = [
        pltpu.make_async_copy(src, dst, tab.at[i])
        for i, (src, dst) in enumerate(
            ((z_in_h, z_in), (z_out_h, z_out), (into_h, into), (back_h, back), (kin_h, kin))
        )
    ]
    for copy in table_copies:
        copy.start()
    slab = pl.ds(pl.multiple_of(box * DEPTH, DEPTH), DEPTH)
    width = PLANE // CHUNKS
    v_mine = pltpu.make_async_copy(pot, vfull.at[slab, :], own.at[0])
    v_mine.start()
    target = pl.ds(pl.multiple_of(orb * SLOTS, SLOTS), SLOTS)
    z_rows, lanes = tile_of(orb)
    p_mine = pltpu.make_async_copy(psi.at[:, z_rows, lanes], pieces.at[target], own.at[1])
    p_mine.start()
    c_mine = pltpu.make_async_copy(psi.at[pl.ds(2 * box, 2)], cube.at[:, slab, :], own.at[2])
    c_mine.start()

    beside = greet(orb, box, x, z, core, plane_sem)
    for chunk in range(CHUNKS):
        cols = pl.ds(chunk * width, width)
        for step in range(1, BOX):
            to = (box + step) % BOX
            remote(
                psi.at[pl.ds(2 * to, 2), :, cols], cube.at[:, slab, cols],
                y_send.at[chunk], y_recv.at[chunk], orb, to,
            ).start()
            if chunk == CHUNKS - 2:
                remote(pot, vfull.at[slab, :], v_sem.at[0], v_sem.at[1], orb, to).start()
    pl.semaphore_wait(plane_sem, 7)

    def send_psi(step, carry):
        to = shifted(orb, step)
        z_rows, lanes = tile_of(to)
        remote(psi.at[:, z_rows, lanes], pieces.at[target], p_sem.at[0], p_sem.at[1], to, box).start()
        return carry

    lax.fori_loop(1, ORB, send_psi, 0)
    beside(all_sem)

    def tabled():
        for copy in table_copies:
            copy.wait()

    def arrived(chunk):
        if chunk == 0:
            c_mine.wait()
        third = cube.at[:, pl.ds(0, 3 * DEPTH), pl.ds(chunk * width, width)]
        wait_for(third, y_recv.at[chunk])
        if chunk == CHUNKS - 2:
            v_mine.wait()
            wait_for(vfull.at[pl.ds(0, 3 * DEPTH)], v_sem.at[1])

    filters(
        cube, vfull, z_in, z_out, into, back, kin, applied,
        f_c_hi, f_c_lo, f_t_hi, f_t_lo, f_s_hi, f_s_lo, kz, arrived, tabled,
    )
    pl.semaphore_wait(all_sem, BOX - 1)

    a_target = pl.ds(orb * SLOTS + 2 * box, 2)

    def source(to_orb, to_box):
        z_rows = pl.ds(pl.multiple_of(to_box * DEPTH + (to_orb // 32) * 8, 8), 8)
        return applied.at[:, z_rows, pl.ds(pl.multiple_of((to_orb % 32) * 128, 128), 128)]

    a_mine = pltpu.make_async_copy(source(orb, box), app_pieces.at[a_target], own.at[3])
    a_mine.start()

    def send_applied(step, carry):
        to_orb = shifted(orb, step // BOX)
        to_box = (box + step % BOX) % BOX
        remote(
            source(to_orb, to_box), app_pieces.at[a_target], a_sem.at[0], a_sem.at[1], to_orb, to_box
        ).start()
        return carry

    lax.fori_loop(1, ORB * BOX, send_applied, 0)

    pieces2 = pieces.reshape(SLOTS * ORB * 8, 128)
    applied2 = app_pieces.reshape(SLOTS * ORB * 8, 128)
    resid2 = resid.reshape(ORBS * 8, 128)
    wanted = jnp.broadcast_to(slots[...].astype(F32), (ORBS, ORBS)).T
    column = lax.broadcasted_iota(jnp.int32, (ORBS, ORBS), 1).astype(F32)
    pick = jnp.concatenate(
        [(column + float(k * ORBS) == wanted).astype(F32) for k in range(SLOTS * ORB // ORBS)], 1
    ).astype(BF16)

    def choose(ref, hi, lo, both=None):
        for k in range(8):
            lanes = pl.ds(k * 128, 128)
            high, low = split(ref[pl.ds(k, SLOTS * ORB, stride=8), :])
            high, low = mm(pick, high), mm(pick, low)
            hi[:, lanes] = high.astype(BF16)
            lo[:, lanes] = low.astype(BF16)
            if both is not None:
                both[pl.ds(k * ORBS, ORBS), :] = high + low

    p_mine.wait()
    wait_for(pieces.at[pl.ds(0, SLOTS * (ORB - 1))], p_sem.at[1])
    choose(pieces2, c_hi, c_lo)
    a_mine.wait()
    wait_for(app_pieces.at[pl.ds(0, SLOTS * ORB - 2)], a_sem.at[1])
    choose(applied2, a_hi, a_lo, a_sum)

    scale = 1.0 / float(G**3)
    total = dot_nt(a_hi[...], c_hi[...]) + dot_nt(a_hi[...], c_lo[...]) + dot_nt(a_lo[...], c_hi[...])
    part[...] = (total * scale).reshape(32, 8, ORBS)

    a_me = (x * 4 + box) * 2 + core

    def a_peer(step):
        to_orb = ((x + step // 8) % 4) * 16 + z * 2 + (core + step % 2) % 2
        return to_orb, (box + (step // 2) % 4) % 4

    for step in range(1, 32):
        to_orb, to_box = a_peer(step)
        a_to = ((to_orb // 16) * 4 + to_box) * 2 + to_orb % 2
        remote(part.at[a_to], rs.at[a_me], r_sem.at[0], r_sem.at[1], to_orb, to_box).start()
    rs[a_me] = part[a_me]
    wait_for(rs.at[pl.ds(0, 31)], r_sem.at[1])
    bb[z] = jnp.sum(rs[...], axis=0)
    for step in range(1, 8):
        to_orb = x * 16 + ((z + step) % 8) * 2 + core
        remote(bb.at[z], bb.at[z], r_sem.at[2], r_sem.at[3], to_orb, box).start()
    wait_for(bb.at[pl.ds(0, 7)], r_sem.at[3])
    mult[a_me] = jnp.sum(bb[...], axis=0)
    for step in range(1, 32):
        to_orb, to_box = a_peer(step)
        remote(mult.at[a_me], mult.at[a_me], r_sem.at[4], r_sem.at[5], to_orb, to_box).start()
    wait_for(mult.at[pl.ds(0, 31)], r_sem.at[5])
    z_rows = pl.ds(pl.multiple_of(8 + (orb // 32) * 8, 8), 8)
    lanes = pl.ds(pl.multiple_of((orb % 32) * 128, 128), 128)
    r_mine = []
    mult2 = mult.reshape(ORBS, ORBS)
    for h in range(2):
        m_side[pl.ds(h * ORBS, ORBS), :] = mult2[:, pl.ds(h * 128, 128)]
    for n in range(OWN):
        sides = [m_side[pl.ds(h * ORBS + n, ORB, stride=OWN), :] for h in range(2)]
        m_hi, m_lo = split(jnp.concatenate(sides, 1))
        fix = mm(m_hi, c_hi[...]) + mm(m_hi, c_lo[...]) + mm(m_lo, c_hi[...])
        for k in range(8):
            value = a_sum[pl.ds(k * ORBS + n, ORB, stride=OWN), :] - fix[:, k * 128 : (k + 1) * 128]
            resid2[pl.ds(n * 8 + k, ORB, stride=OWN * 8), :] = value
        landing = ext.at[pl.ds(n, 1), z_rows, lanes]
        copy = pltpu.make_async_copy(resid.at[pl.ds(orb * OWN + n, 1)], landing, own.at[4 + n])
        copy.start()
        r_mine.append(copy)

        def send_resid(step, carry, n=n, landing=landing):
            to = shifted(orb, step)
            remote(resid.at[pl.ds(to * OWN + n, 1)], landing, f_send, f_recv.at[n], to, box).start()
            return carry

        lax.fori_loop(1, ORB, send_resid, 0)

    def halo(n):
        one = pl.ds(n, 1)
        up = remote(
            ext.at[one, pl.ds(20, 4), :], ext.at[one, pl.ds(4, 4), :],
            h_send.at[2 * n], h_recv.at[2 * n], orb, (box + 1) % BOX,
        )
        down = remote(
            ext.at[one, pl.ds(8, 4), :], ext.at[one, pl.ds(24, 4), :],
            h_send.at[2 * n + 1], h_recv.at[2 * n + 1], orb, (box + 3) % BOX,
        )
        up.start()
        down.start()
        return up, down

    def finish(n, pair):
        for copy in pair:
            copy.wait()
        resid_out[n] = ext[n, 8:24, :]
        relax(ext[n], inverse_of(mult, orb * OWN + n), box, direct_out.at[n])

    mult_out[...] = mult2[...].T
    inverse_out[...] = jnp.broadcast_to(inverse_of(mult, orb * OWN + OWN - 1), (8, 128))
    pair = None
    for n in range(OWN):
        r_mine[n].wait()
        wait_for(resid.at[pl.ds(0, ORB - 1)], f_recv.at[n])
        following = halo(n)
        if pair is not None:
            finish(n - 1, pair)
        pair = following
    for chunk in range(CHUNKS):
        wait_for(cube.at[:, pl.ds(0, 3 * DEPTH), pl.ds(chunk * width, width)], y_send.at[chunk])
    wait_for(vfull.at[pl.ds(0, 3 * DEPTH)], v_sem.at[0])
    wait_for(pieces.at[pl.ds(0, SLOTS * (ORB - 1))], p_sem.at[0])
    wait_for(app_pieces.at[pl.ds(0, SLOTS * ORB - 2)], a_sem.at[0])
    wait_for(part.at[pl.ds(0, 31)], r_sem.at[0])
    wait_for(bb.at[pl.ds(0, 7)], r_sem.at[2])
    wait_for(mult.at[pl.ds(0, 31)], r_sem.at[4])
    wait_for(resid.at[pl.ds(0, OWN * (ORB - 1))], f_send)
    for copy in pair:
        copy.wait()
    ext_out[...] = ext[OWN - 1]


DMA = pltpu.SemaphoreType.DMA
REGULAR = pltpu.SemaphoreType.REGULAR


def shape(*dims, dtype=F32):
    return jax.ShapeDtypeStruct(dims, dtype)


def local(psi, potential, orbital_slot):
    consts = [jnp.asarray(t) for t in tables()]
    v32 = lambda *dims: pltpu.VMEM(dims, F32)
    v16 = lambda *dims: pltpu.VMEM(dims, BF16)
    padded = lambda pad: v16(TILES + 2 * pad, 2 * G, LANES)
    residual, direction, mult, ext, inverse = pl.pallas_call(
        step_kernel,
        out_shape=[
            v32(OWN - 1, DEPTH, PLANE), v32(OWN - 1, DEPTH, PLANE), v32(ORBS, ORBS),
            v32(32, PLANE), v32(8, 128),
        ],
        in_specs=[ANY, ANY, VMEM] + [ANY] * 5,
        out_specs=[VMEM] * 5,
        scratch_shapes=[
            v32(SLOTS * ORB, 8, 128), v32(SLOTS * ORB, 8, 128),
            v32(2, G, PLANE), v32(G, PLANE), v32(2, G, PLANE),
        ]
        + [v16(*t.shape) for t in consts]
        + [padded(KPAD)] * 2 + [padded(FPAD)] * 4 + [v32(TILES, 2 * G, LANES)]
        + [v32(32, 8, ORBS)] * 2 + [v32(8, 8, ORBS)] + [v32(32, 8, ORBS)] + [v32(ORBS, 8, 128)]
        + [v16(ORBS, 1024)] * 4 + [v32(8 * ORBS, 128), v32(2 * ORBS, 128)] + [v32(OWN, 32, PLANE)]
        + [
            DMA((8,)), DMA((CHUNKS,)), DMA((CHUNKS,)), DMA((2,)), DMA((2,)), DMA((2,)), DMA((6,)),
            DMA, DMA((OWN,)), DMA((2 * OWN,)), DMA((2 * OWN,)), DMA((5,)), REGULAR, REGULAR,
        ],
        compiler_params=pltpu.CompilerParams(
            has_side_effects=True, vmem_limit_bytes=VLIMIT, collective_id=0
        ),
        name="orbital_step",
    )(psi, potential, orbital_slot.reshape(1, ORBS), *consts)
    return pl.pallas_call(
        finish_kernel,
        out_shape=[shape(OWN, DEPTH, PLANE), shape(OWN, DEPTH, PLANE), shape(ORBS, ORBS)],
        in_specs=[VMEM] * 5,
        out_specs=[ANY] * 3,
        scratch_shapes=[v32(DEPTH, PLANE), DMA((5,))],
        compiler_params=pltpu.CompilerParams(vmem_limit_bytes=16 * 2**20),
        name="last_orbital",
    )(residual, direction, mult, ext, inverse)


def solution(mesh):
    in_specs = (P("orb", "box", None), P("box", None), P())
    out_specs = (P("orb", "box", None), P("orb", "box", None), P())
    return jax.shard_map(local, mesh=mesh, in_specs=in_specs, out_specs=out_specs, check_vma=False)
```

```python
import math

import jax
import jax.numpy as jnp
import ml_dtypes
import numpy as np
from jax import lax
from jax.experimental import pallas as pl
from jax.experimental.pallas import tpu as pltpu
from jax.sharding import PartitionSpec as P

G = 64
MTAPS = 16
KREACH = 14
SWEEPS = 4
ORB, BOX = 64, 4
SLOTS, ORBS, OWN = 8, 256, 4
DEPTH = 16
PLANE = G * G
LANES = 256
TILES = PLANE // LANES
FPAD, KPAD = 2, 4

coupling_z = 4.0
coupling_xy = 1.0

F32, BF16 = jnp.float32, jnp.bfloat16
ANY = pl.BlockSpec(memory_space=pl.ANY)
VMEM = pl.BlockSpec(memory_space=pltpu.VMEM)
VLIMIT = 56 * 2**20


def magic_weights(tap_count):
    half_len = tap_count // 2
    offsets = np.arange(1 - half_len, half_len + 1) * 1.0
    weights = np.ones(tap_count)
    for index_a in range(tap_count):
        for index_b in range(tap_count):
            if index_b != index_a:
                weights[index_a] *= (0.25 - offsets[index_b]) / (
                    offsets[index_a] - offsets[index_b]
                )
    return weights


def second_weights(reach_cells):
    factor = math.factorial(reach_cells) ** 2
    weights = np.zeros(2 * reach_cells + 1)
    for distance in range(1, reach_cells + 1):
        entry_value = (
            2.0
            * (-1) ** (distance + 1)
            * factor
            / (
                distance
                * distance
                * math.factorial(reach_cells - distance)
                * math.factorial(reach_cells + distance)
            )
        )
        weights[reach_cells + distance] = entry_value
        weights[reach_cells - distance] = entry_value
    weights[reach_cells] = -weights.sum()
    return -0.5 * weights


def banded(row_count, col_count, row_start, col_start, weights, offset_low):
    row_index = np.arange(row_count)[:, None] + row_start
    col_index = np.arange(col_count)[None, :] + col_start
    position = row_index - col_index - offset_low
    inside = (position >= 0) & (position < len(weights))
    return np.where(inside, weights[np.clip(position, 0, len(weights) - 1)], 0.0)


def halves(table):
    table = np.asarray(table, np.float32)
    high = table.astype(ml_dtypes.bfloat16)
    low = (table - high.astype(np.float32)).astype(ml_dtypes.bfloat16)
    return high, low


def tables():
    magic = magic_weights(MTAPS)
    kinetic_row = second_weights(KREACH)
    forward = banded(G, G, 0, 0, magic, 1 - MTAPS // 2)
    kinetic = banded(G, G, 0, 0, kinetic_row, -KREACH)
    rows = LANES // G

    def beside(high, low):
        return np.concatenate([high, high, low], 1)

    z_in = beside(*halves(np.concatenate([forward.T, kinetic], 0)))
    z_out = beside(*halves(forward))
    into, back, kin = [], [], []
    for step in range(-FPAD, FPAD + 1):
        block = banded(rows, rows, rows * step, 0, magic, 1 - MTAPS // 2)
        into.append(np.kron(block, forward))
        block = banded(rows, rows, -rows * step, 0, magic, 1 - MTAPS // 2).T
        back.append(np.kron(block, forward.T))
    for step in range(-KPAD, KPAD + 1):
        block = np.kron(banded(rows, rows, rows * step, 0, kinetic_row, -KREACH), np.eye(G))
        if step == 0:
            block = block + np.kron(np.eye(rows), kinetic)
        kin.append(block)
    return [z_in, z_out] + [np.stack(halves(np.stack(m))) for m in (into, back, kin)]


def split(values):
    high = values.astype(BF16)
    return high, (values - high.astype(F32)).astype(BF16)


def mm(left, right):
    return jnp.dot(left, right, preferred_element_type=F32)


def place():
    orb = lax.axis_index("orb")
    box = lax.axis_index("box")
    return orb, box, orb // 16, (orb // 2) % 8, orb % 2


def shifted(orb, step):
    x, z, core = orb // 16, (orb // 2) % 8, orb % 2
    dx, dz, dc = step // 16, (step // 2) % 8, step % 2
    return ((x + dx) % 4) * 16 + ((z + dz) % 8) * 2 + (core + dc) % 2


def remote(src, dst, send, recv, orb, box):
    return pltpu.make_async_remote_copy(
        src_ref=src,
        dst_ref=dst,
        send_sem=send,
        recv_sem=recv,
        device_id={"orb": orb, "box": box},
        device_id_type=pl.DeviceIdType.MESH,
    )


def wait_for(ref, sem):
    pltpu.make_async_copy(ref, ref, sem).wait()


def tile_of(orb):
    return pl.ds(pl.multiple_of((orb // 32) * 8, 8), 8), pl.ds(
        pl.multiple_of((orb % 32) * 128, 128), 128
    )


CHUNKS = 4
GROUPS = ((0, 2), (2, 1), (3, 1))


def greet(orb, box, x, z, core, plane_sem, meanwhile):
    barrier = pltpu.get_barrier_semaphore()

    def signal(sem, to_orb, to_box):
        pl.semaphore_signal(
            sem, inc=1, device_id={"orb": to_orb, "box": to_box}, device_id_type=pl.DeviceIdType.MESH
        )

    def along_z(step, carry):
        signal(barrier, x * 16 + ((z + step) % 8) * 2 + core, box)
        return carry

    def across(sem):
        def body(step, carry):
            signal(sem, ((x + step // 2) % 4) * 16 + z * 2 + (core + step % 2) % 2, box)
            return carry

        return body

    def beside(sem):
        for step in range(1, BOX):
            signal(sem, orb, (box + step) % BOX)

    lax.fori_loop(1, 8, along_z, 0)
    lax.fori_loop(1, 8, across(barrier), 0)
    beside(barrier)
    meanwhile()
    pl.semaphore_wait(barrier, 7 + 7 + 3)
    lax.fori_loop(1, 8, across(plane_sem), 0)
    return beside


def filters(cube, vfull, z_in, z_out, into, back, kin, out, c_hi, c_lo, t_hi, t_lo, s_hi, s_lo, kz, arrived, tabled):
    for buf, pad in ((c_hi, KPAD), (c_lo, KPAD), (t_hi, FPAD), (t_lo, FPAD), (s_hi, FPAD), (s_lo, FPAD)):
        edge = jnp.zeros((pad, 2 * G, LANES), BF16)
        buf[pl.ds(0, pad)] = edge
        buf[pl.ds(TILES + pad, pad)] = edge

    def along_z(t, carry):
        lanes = pl.ds(pl.multiple_of(t * LANES, LANES), LANES)
        for s in range(2):
            rows = pl.ds(s * G, G)
            high, low = split(cube[s, :, lanes])
            c_hi[t + KPAD, rows, :] = high
            c_lo[t + KPAD, rows, :] = low
            both = mm(z_in[...], jnp.concatenate([high, low, high], 0))
            kz[t, rows, :] = both[G:]
            high, low = split(both[:G])
            t_hi[t + FPAD, rows, :] = high
            t_lo[t + FPAD, rows, :] = low
        return carry

    group = 2

    def spread(hi, lo, table, count, first, acc):
        for d in range(count):
            high = hi[pl.ds(first + d, group)].reshape(group * 2 * G, LANES)
            low = lo[pl.ds(first + d, group)].reshape(group * 2 * G, LANES)
            term = mm(high, table[0, d]) + mm(low, table[0, d]) + mm(high, table[1, d])
            acc = term if acc is None else acc + term
        return acc

    def middle(i, carry):
        first = i * group
        grid = spread(t_hi, t_lo, into, 2 * FPAD + 1, first, None)
        for j in range(group):
            lanes = pl.ds(pl.multiple_of((first + j) * LANES, LANES), LANES)
            local = vfull[:, lanes]
            for s in range(2):
                low_row = (j * 2 + s) * G
                high, low = split(grid[low_row : low_row + G] * local)
                done = mm(z_out[...], jnp.concatenate([high, low, high], 0))
                high, low = split(done)
                s_hi[first + j + FPAD, pl.ds(s * G, G), :] = high
                s_lo[first + j + FPAD, pl.ds(s * G, G), :] = low
        return carry

    def kinetic(i, carry):
        first = i * group
        acc = kz[pl.ds(first, group)].reshape(group * 2 * G, LANES)
        acc = spread(c_hi, c_lo, kin, 2 * KPAD + 1, first, acc)
        kz[pl.ds(first, group)] = acc.reshape(group, 2 * G, LANES)
        return carry

    tabled()
    per = TILES // CHUNKS
    for chunk in range(CHUNKS - 1):
        arrived(chunk)
        lax.fori_loop(chunk * per, (chunk + 1) * per, along_z, 0)
    early = (TILES - per - KPAD) // group
    lax.fori_loop(0, early, kinetic, 0)
    lax.fori_loop(0, early, middle, 0)
    arrived(CHUNKS - 1)
    lax.fori_loop(TILES - per, TILES, along_z, 0)
    lax.fori_loop(early, TILES // group, middle, 0)
    lax.fori_loop(early, TILES // group, kinetic, 0)

    def last(i, carry):
        first = i * group
        acc = kz[pl.ds(first, group)].reshape(group * 2 * G, LANES)
        acc = spread(s_hi, s_lo, back, 2 * FPAD + 1, first, acc)
        for j in range(group):
            lanes = pl.ds(pl.multiple_of((first + j) * LANES, LANES), LANES)
            for s in range(2):
                low_row = (j * 2 + s) * G
                out[s, :, lanes] = acc[low_row : low_row + G]
        return carry

    lax.fori_loop(0, TILES // group, last, 0)


def dot_nt(left, right):
    return lax.dot_general(left, right, (((1,), (1,)), ((), ())), preferred_element_type=F32)


def inverse_of(mult_t, which):
    line = mult_t[which // 8, pl.ds(which % 8, 1), :]
    keep = lax.broadcasted_iota(jnp.int32, (1, ORBS), 1) == which
    diagonal = jnp.sum(jnp.where(keep, line, 0.0), axis=1, keepdims=True)
    return 1.0 / (2.0 * coupling_z + 4.0 * coupling_xy + 1.0 + jnp.abs(diagonal))


def relax(resid, inverse, box, direct_out):
    lane = lax.broadcasted_iota(jnp.int32, (32, 128), 1)
    row = lax.broadcasted_iota(jnp.int32, (32, 128), 0)
    inside = ((row >= 8) | (box > 0)) & ((row < 24) | (box < BOX - 1))
    factor = jnp.where(inside, jnp.broadcast_to(inverse, (32, 128)), 0.0)
    first_col, last_col, first_row = lane % G == 0, lane % G == G - 1, lane < G
    count = PLANE // 128
    start = [jnp.where(inside, resid[:, k * 128 : (k + 1) * 128], 0.0) for k in range(count)]
    now = [part * factor for part in start]
    for _ in range(SWEEPS):
        turned = [pltpu.roll(part, G, 1) for part in now]
        pairs = [turned[0]] + [turned[k - 1] + turned[k] for k in range(1, count)] + [turned[-1]]
        following = []
        for k in range(count):
            side = jnp.where(first_row, pairs[k], pairs[k + 1])
            side = side + jnp.where(first_col, 0.0, pltpu.roll(now[k], 1, 1))
            side = side + jnp.where(last_col, 0.0, pltpu.roll(now[k], 127, 1))
            along_z = pltpu.roll(now[k], 1, 0) + pltpu.roll(now[k], 31, 0)
            following.append((start[k] + coupling_xy * side + coupling_z * along_z) * factor)
        now = following
    for k in range(count):
        direct_out[:, k * 128 : (k + 1) * 128] = now[k][8:24]


def finish_kernel(resid, direct, mult, ext, inverse, resid_out, direct_out, mult_out, last, sems):
    box = lax.axis_index("box")
    done = pl.ds(0, OWN - 1)
    copies = [
        pltpu.make_async_copy(direct, direct_out.at[done], sems.at[0]),
        pltpu.make_async_copy(resid, resid_out.at[done], sems.at[1]),
        pltpu.make_async_copy(ext.at[pl.ds(8, DEPTH)], resid_out.at[OWN - 1], sems.at[2]),
        pltpu.make_async_copy(mult, mult_out, sems.at[3]),
    ]
    for copy in copies:
        copy.start()
    relax(ext[...], inverse[0:1, 0:1], box, last)
    copies.append(pltpu.make_async_copy(last, direct_out.at[OWN - 1], sems.at[4]))
    copies[-1].start()
    for copy in copies:
        copy.wait()


def step_kernel(
    psi, pot, slots, z_in_h, z_out_h, into_h, back_h, kin_h,
    resid_out, direct_out, mult_out, ext_out, inverse_out,
    pieces, app_pieces, cube, vfull, applied,
    z_in, z_out, into, back, kin,
    f_c_hi, f_c_lo, f_t_hi, f_t_lo, f_s_hi, f_s_lo, kz,
    part, rs, bb, mult, resid, c_hi, c_lo, a_hi, a_lo, a_sum, m_side, ext,
    own, y_send, y_recv, v_sem, p_sem, a_sem, r_sem, f_send, f_recv, h_send, h_recv, tab, plane_sem, all_sem,
):
    orb, box, x, z, core = place()
    table_copies = [
        pltpu.make_async_copy(src, dst, tab.at[i])
        for i, (src, dst) in enumerate(
            ((z_in_h, z_in), (z_out_h, z_out), (into_h, into), (back_h, back), (kin_h, kin))
        )
    ]
    slab = pl.ds(pl.multiple_of(box * DEPTH, DEPTH), DEPTH)
    width = PLANE // CHUNKS
    v_mine = pltpu.make_async_copy(pot, vfull.at[slab, :], own.at[0])
    target = pl.ds(pl.multiple_of(orb * SLOTS, SLOTS), SLOTS)
    z_rows, lanes = tile_of(orb)
    p_mine = pltpu.make_async_copy(psi.at[:, z_rows, lanes], pieces.at[target], own.at[1])
    c_mine = pltpu.make_async_copy(psi.at[pl.ds(2 * box, 2)], cube.at[:, slab, :], own.at[2])

    def meanwhile():
        for copy in [*table_copies, v_mine, p_mine, c_mine]:
            copy.start()

    beside = greet(orb, box, x, z, core, plane_sem, meanwhile)
    for chunk in range(CHUNKS):
        cols = pl.ds(chunk * width, width)
        for step in range(1, BOX):
            to = (box + step) % BOX
            remote(
                psi.at[pl.ds(2 * to, 2), :, cols], cube.at[:, slab, cols],
                y_send.at[chunk], y_recv.at[chunk], orb, to,
            ).start()
            if chunk == CHUNKS - 2:
                remote(pot, vfull.at[slab, :], v_sem.at[0], v_sem.at[1], orb, to).start()
    pl.semaphore_wait(plane_sem, 7)

    def send_psi(step, carry):
        to = shifted(orb, step)
        z_rows, lanes = tile_of(to)
        remote(psi.at[:, z_rows, lanes], pieces.at[target], p_sem.at[0], p_sem.at[1], to, box).start()
        return carry

    lax.fori_loop(1, ORB, send_psi, 0)
    beside(all_sem)

    def tabled():
        for copy in table_copies:
            copy.wait()

    def arrived(chunk):
        if chunk == 0:
            c_mine.wait()
        third = cube.at[:, pl.ds(0, 3 * DEPTH), pl.ds(chunk * width, width)]
        wait_for(third, y_recv.at[chunk])
        if chunk == CHUNKS - 2:
            v_mine.wait()
            wait_for(vfull.at[pl.ds(0, 3 * DEPTH)], v_sem.at[1])

    filters(
        cube, vfull, z_in, z_out, into, back, kin, applied,
        f_c_hi, f_c_lo, f_t_hi, f_t_lo, f_s_hi, f_s_lo, kz, arrived, tabled,
    )
    pl.semaphore_wait(all_sem, BOX - 1)

    a_target = pl.ds(orb * SLOTS + 2 * box, 2)

    def source(to_orb, to_box):
        z_rows = pl.ds(pl.multiple_of(to_box * DEPTH + (to_orb // 32) * 8, 8), 8)
        return applied.at[:, z_rows, pl.ds(pl.multiple_of((to_orb % 32) * 128, 128), 128)]

    a_mine = pltpu.make_async_copy(source(orb, box), app_pieces.at[a_target], own.at[3])
    a_mine.start()

    def send_applied(step, carry):
        to_orb = shifted(orb, step // BOX)
        to_box = (box + step % BOX) % BOX
        remote(
            source(to_orb, to_box), app_pieces.at[a_target], a_sem.at[0], a_sem.at[1], to_orb, to_box
        ).start()
        return carry

    lax.fori_loop(1, ORB * BOX, send_applied, 0)

    pieces2 = pieces.reshape(SLOTS * ORB * 8, 128)
    applied2 = app_pieces.reshape(SLOTS * ORB * 8, 128)
    resid2 = resid.reshape(ORBS * 8, 128)
    wanted = jnp.broadcast_to(slots[...].astype(F32), (ORBS, ORBS)).T
    column = lax.broadcasted_iota(jnp.int32, (ORBS, ORBS), 1).astype(F32)
    pick = jnp.concatenate(
        [(column + float(k * ORBS) == wanted).astype(F32) for k in range(SLOTS * ORB // ORBS)], 1
    ).astype(BF16)

    def choose(ref, hi, lo, both=None):
        for k in range(8):
            lanes = pl.ds(k * 128, 128)
            high, low = split(ref[pl.ds(k, SLOTS * ORB, stride=8), :])
            high, low = mm(pick, high), mm(pick, low)
            hi[:, lanes] = high.astype(BF16)
            lo[:, lanes] = low.astype(BF16)
            if both is not None:
                both[pl.ds(k * ORBS, ORBS), :] = high + low

    p_mine.wait()
    wait_for(pieces.at[pl.ds(0, SLOTS * (ORB - 1))], p_sem.at[1])
    choose(pieces2, c_hi, c_lo)
    a_mine.wait()
    wait_for(app_pieces.at[pl.ds(0, SLOTS * ORB - 2)], a_sem.at[1])
    choose(applied2, a_hi, a_lo, a_sum)

    scale = 1.0 / float(G**3)
    total = dot_nt(a_hi[...], c_hi[...]) + dot_nt(a_hi[...], c_lo[...]) + dot_nt(a_lo[...], c_hi[...])
    part[...] = (total * scale).reshape(32, 8, ORBS)

    a_me = (x * 4 + box) * 2 + core

    def a_peer(step):
        to_orb = ((x + step // 8) % 4) * 16 + z * 2 + (core + step % 2) % 2
        return to_orb, (box + (step // 2) % 4) % 4

    for step in range(1, 32):
        to_orb, to_box = a_peer(step)
        a_to = ((to_orb // 16) * 4 + to_box) * 2 + to_orb % 2
        remote(part.at[a_to], rs.at[a_me], r_sem.at[0], r_sem.at[1], to_orb, to_box).start()
    rs[a_me] = part[a_me]
    wait_for(rs.at[pl.ds(0, 31)], r_sem.at[1])
    bb[z] = jnp.sum(rs[...], axis=0)
    for step in range(1, 8):
        to_orb = x * 16 + ((z + step) % 8) * 2 + core
        remote(bb.at[z], bb.at[z], r_sem.at[2], r_sem.at[3], to_orb, box).start()
    wait_for(bb.at[pl.ds(0, 7)], r_sem.at[3])
    mult[a_me] = jnp.sum(bb[...], axis=0)
    for step in range(1, 32):
        to_orb, to_box = a_peer(step)
        remote(mult.at[a_me], mult.at[a_me], r_sem.at[4], r_sem.at[5], to_orb, to_box).start()
    wait_for(mult.at[pl.ds(0, 31)], r_sem.at[5])
    z_rows = pl.ds(pl.multiple_of(8 + (orb // 32) * 8, 8), 8)
    lanes = pl.ds(pl.multiple_of((orb % 32) * 128, 128), 128)
    r_mine = []
    mult2 = mult.reshape(ORBS, ORBS)
    for h in range(2):
        m_side[pl.ds(h * ORBS, ORBS), :] = mult2[:, pl.ds(h * 128, 128)]
    for g, (first, count) in enumerate(GROUPS):
        members = range(first, first + count)
        sides = [
            jnp.concatenate([m_side[pl.ds(h * ORBS + n, ORB, stride=OWN), :] for n in members], 0)
            for h in range(2)
        ]
        m_hi, m_lo = split(jnp.concatenate(sides, 1))
        fix = mm(m_hi, c_hi[...]) + mm(m_hi, c_lo[...]) + mm(m_lo, c_hi[...])
        for i, n in enumerate(members):
            for k in range(8):
                part_fix = fix[i * ORB : (i + 1) * ORB, k * 128 : (k + 1) * 128]
                value = a_sum[pl.ds(k * ORBS + n, ORB, stride=OWN), :] - part_fix
                resid2[pl.ds(n * 8 + k, ORB, stride=OWN * 8), :] = value
        landing = ext.at[pl.ds(first, count), z_rows, lanes]
        copy = pltpu.make_async_copy(resid.at[pl.ds(orb * OWN + first, count)], landing, own.at[4 + g])
        copy.start()
        r_mine.append(copy)

        def send_resid(step, carry, g=g, first=first, count=count, landing=landing):
            to = shifted(orb, step)
            remote(
                resid.at[pl.ds(to * OWN + first, count)], landing, f_send, f_recv.at[g], to, box
            ).start()
            return carry

        lax.fori_loop(1, ORB, send_resid, 0)

    def halo(g):
        r_mine[g].wait()
        first, count = GROUPS[g]
        wait_for(resid.at[pl.ds(0, count * (ORB - 1))], f_recv.at[g])
        some = pl.ds(first, count)
        up = remote(
            ext.at[some, pl.ds(20, 4), :], ext.at[some, pl.ds(4, 4), :],
            h_send.at[2 * g], h_recv.at[2 * g], orb, (box + 1) % BOX,
        )
        down = remote(
            ext.at[some, pl.ds(8, 4), :], ext.at[some, pl.ds(24, 4), :],
            h_send.at[2 * g + 1], h_recv.at[2 * g + 1], orb, (box + 3) % BOX,
        )
        up.start()
        down.start()
        return up, down

    def finish(g, pair):
        for copy in pair:
            copy.wait()
        first, count = GROUPS[g]
        for n in range(first, first + count):
            resid_out[n] = ext[n, 8:24, :]
            relax(ext[n], inverse_of(mult, orb * OWN + n), box, direct_out.at[n])

    mult_out[...] = mult2[...].T
    inverse_out[...] = jnp.broadcast_to(inverse_of(mult, orb * OWN + OWN - 1), (8, 128))
    pair = halo(0)
    for g in range(1, len(GROUPS)):
        following = halo(g)
        finish(g - 1, pair)
        pair = following
    for chunk in range(CHUNKS):
        wait_for(cube.at[:, pl.ds(0, 3 * DEPTH), pl.ds(chunk * width, width)], y_send.at[chunk])
    wait_for(vfull.at[pl.ds(0, 3 * DEPTH)], v_sem.at[0])
    wait_for(pieces.at[pl.ds(0, SLOTS * (ORB - 1))], p_sem.at[0])
    wait_for(app_pieces.at[pl.ds(0, SLOTS * ORB - 2)], a_sem.at[0])
    wait_for(part.at[pl.ds(0, 31)], r_sem.at[0])
    wait_for(bb.at[pl.ds(0, 7)], r_sem.at[2])
    wait_for(mult.at[pl.ds(0, 31)], r_sem.at[4])
    wait_for(resid.at[pl.ds(0, OWN * (ORB - 1))], f_send)
    for copy in pair:
        copy.wait()
    ext_out[...] = ext[OWN - 1]


DMA = pltpu.SemaphoreType.DMA
REGULAR = pltpu.SemaphoreType.REGULAR


def shape(*dims, dtype=F32):
    return jax.ShapeDtypeStruct(dims, dtype)


def local(psi, potential, orbital_slot):
    consts = [jnp.asarray(t) for t in tables()]
    v32 = lambda *dims: pltpu.VMEM(dims, F32)
    v16 = lambda *dims: pltpu.VMEM(dims, BF16)
    padded = lambda pad: v16(TILES + 2 * pad, 2 * G, LANES)
    residual, direction, mult, ext, inverse = pl.pallas_call(
        step_kernel,
        out_shape=[
            v32(OWN - 1, DEPTH, PLANE), v32(OWN - 1, DEPTH, PLANE), v32(ORBS, ORBS),
            v32(32, PLANE), v32(8, 128),
        ],
        in_specs=[ANY, ANY, VMEM] + [ANY] * 5,
        out_specs=[VMEM] * 5,
        scratch_shapes=[
            v32(SLOTS * ORB, 8, 128), v32(SLOTS * ORB, 8, 128),
            v32(2, G, PLANE), v32(G, PLANE), v32(2, G, PLANE),
        ]
        + [v16(*t.shape) for t in consts]
        + [padded(KPAD)] * 2 + [padded(FPAD)] * 4 + [v32(TILES, 2 * G, LANES)]
        + [v32(32, 8, ORBS)] * 2 + [v32(8, 8, ORBS)] + [v32(32, 8, ORBS)] + [v32(ORBS, 8, 128)]
        + [v16(ORBS, 1024)] * 4 + [v32(8 * ORBS, 128), v32(2 * ORBS, 128)] + [v32(OWN, 32, PLANE)]
        + [
            DMA((8,)), DMA((CHUNKS,)), DMA((CHUNKS,)), DMA((2,)), DMA((2,)), DMA((2,)), DMA((6,)),
            DMA, DMA((OWN,)), DMA((2 * OWN,)), DMA((2 * OWN,)), DMA((5,)), REGULAR, REGULAR,
        ],
        compiler_params=pltpu.CompilerParams(
            has_side_effects=True, vmem_limit_bytes=VLIMIT, collective_id=0
        ),
        name="orbital_step",
    )(psi, potential, orbital_slot.reshape(1, ORBS), *consts)
    return pl.pallas_call(
        finish_kernel,
        out_shape=[shape(OWN, DEPTH, PLANE), shape(OWN, DEPTH, PLANE), shape(ORBS, ORBS)],
        in_specs=[VMEM] * 5,
        out_specs=[ANY] * 3,
        scratch_shapes=[v32(DEPTH, PLANE), DMA((5,))],
        compiler_params=pltpu.CompilerParams(vmem_limit_bytes=16 * 2**20),
        name="last_orbital",
    )(residual, direction, mult, ext, inverse)


def solution(mesh):
    in_specs = (P("orb", "box", None), P("box", None), P())
    out_specs = (P("orb", "box", None), P("orb", "box", None), P())
    return jax.shard_map(local, mesh=mesh, in_specs=in_specs, out_specs=out_specs, check_vma=False)
```

```python
import math

import jax
import jax.numpy as jnp
import ml_dtypes
import numpy as np
from jax import lax
from jax.experimental import pallas as pl
from jax.experimental.pallas import tpu as pltpu
from jax.sharding import PartitionSpec as P

G = 64
MTAPS = 16
KREACH = 14
SWEEPS = 4
ORB, BOX = 64, 4
SLOTS, ORBS, OWN = 8, 256, 4
DEPTH = 16
PLANE = G * G
LANES = 256
TILES = PLANE // LANES
FPAD, KPAD = 2, 4

coupling_z = 4.0
coupling_xy = 1.0

F32, BF16 = jnp.float32, jnp.bfloat16
ANY = pl.BlockSpec(memory_space=pl.ANY)
VMEM = pl.BlockSpec(memory_space=pltpu.VMEM)
VLIMIT = 56 * 2**20


def magic_weights(tap_count):
    half_len = tap_count // 2
    offsets = np.arange(1 - half_len, half_len + 1) * 1.0
    weights = np.ones(tap_count)
    for index_a in range(tap_count):
        for index_b in range(tap_count):
            if index_b != index_a:
                weights[index_a] *= (0.25 - offsets[index_b]) / (
                    offsets[index_a] - offsets[index_b]
                )
    return weights


def second_weights(reach_cells):
    factor = math.factorial(reach_cells) ** 2
    weights = np.zeros(2 * reach_cells + 1)
    for distance in range(1, reach_cells + 1):
        entry_value = (
            2.0
            * (-1) ** (distance + 1)
            * factor
            / (
                distance
                * distance
                * math.factorial(reach_cells - distance)
                * math.factorial(reach_cells + distance)
            )
        )
        weights[reach_cells + distance] = entry_value
        weights[reach_cells - distance] = entry_value
    weights[reach_cells] = -weights.sum()
    return -0.5 * weights


def banded(row_count, col_count, row_start, col_start, weights, offset_low):
    row_index = np.arange(row_count)[:, None] + row_start
    col_index = np.arange(col_count)[None, :] + col_start
    position = row_index - col_index - offset_low
    inside = (position >= 0) & (position < len(weights))
    return np.where(inside, weights[np.clip(position, 0, len(weights) - 1)], 0.0)


def halves(table):
    table = np.asarray(table, np.float32)
    high = table.astype(ml_dtypes.bfloat16)
    low = (table - high.astype(np.float32)).astype(ml_dtypes.bfloat16)
    return high, low


def tables():
    magic = magic_weights(MTAPS)
    kinetic_row = second_weights(KREACH)
    forward = banded(G, G, 0, 0, magic, 1 - MTAPS // 2)
    kinetic = banded(G, G, 0, 0, kinetic_row, -KREACH)
    rows = LANES // G

    def beside(high, low):
        return np.concatenate([high, high, low], 1)

    z_in = beside(*halves(np.concatenate([forward.T, kinetic], 0)))
    z_out = beside(*halves(forward))
    into, back, kin = [], [], []
    for step in range(-FPAD, FPAD + 1):
        block = banded(rows, rows, rows * step, 0, magic, 1 - MTAPS // 2)
        into.append(np.kron(block, forward))
        block = banded(rows, rows, -rows * step, 0, magic, 1 - MTAPS // 2).T
        back.append(np.kron(block, forward.T))
    for step in range(-KPAD, KPAD + 1):
        block = np.kron(banded(rows, rows, rows * step, 0, kinetic_row, -KREACH), np.eye(G))
        if step == 0:
            block = block + np.kron(np.eye(rows), kinetic)
        kin.append(block)
    return [z_in, z_out] + [np.stack(halves(np.stack(m))) for m in (into, back, kin)]


def split(values):
    high = values.astype(BF16)
    return high, (values - high.astype(F32)).astype(BF16)


def mm(left, right):
    return jnp.dot(left, right, preferred_element_type=F32)


def place():
    orb = lax.axis_index("orb")
    box = lax.axis_index("box")
    return orb, box, orb // 16, (orb // 2) % 8, orb % 2


def shifted(orb, step):
    x, z, core = orb // 16, (orb // 2) % 8, orb % 2
    dx, dz, dc = step // 16, (step // 2) % 8, step % 2
    return ((x + dx) % 4) * 16 + ((z + dz) % 8) * 2 + (core + dc) % 2


def remote(src, dst, send, recv, orb, box):
    return pltpu.make_async_remote_copy(
        src_ref=src,
        dst_ref=dst,
        send_sem=send,
        recv_sem=recv,
        device_id={"orb": orb, "box": box},
        device_id_type=pl.DeviceIdType.MESH,
    )


def wait_for(ref, sem):
    pltpu.make_async_copy(ref, ref, sem).wait()


def tile_of(orb):
    return pl.ds(pl.multiple_of((orb // 32) * 8, 8), 8), pl.ds(
        pl.multiple_of((orb % 32) * 128, 128), 128
    )


CHUNKS = 4
GROUPS = ((0, 2), (2, 1), (3, 1))


def greet(orb, box, x, z, core, plane_sem, meanwhile):
    barrier = pltpu.get_barrier_semaphore()

    def signal(sem, to_orb, to_box):
        pl.semaphore_signal(
            sem, inc=1, device_id={"orb": to_orb, "box": to_box}, device_id_type=pl.DeviceIdType.MESH
        )

    def along_z(step, carry):
        signal(barrier, x * 16 + ((z + step) % 8) * 2 + core, box)
        return carry

    def across(sem):
        def body(step, carry):
            signal(sem, ((x + step // 2) % 4) * 16 + z * 2 + (core + step % 2) % 2, box)
            return carry

        return body

    def beside(sem):
        for step in range(1, BOX):
            signal(sem, orb, (box + step) % BOX)

    lax.fori_loop(1, 8, along_z, 0)
    lax.fori_loop(1, 8, across(barrier), 0)
    beside(barrier)
    meanwhile()
    pl.semaphore_wait(barrier, 7 + 7 + 3)
    lax.fori_loop(1, 8, across(plane_sem), 0)
    return beside


def filters(cube, vfull, z_in, z_out, into, back, kin, out, c_hi, c_lo, t_hi, t_lo, s_hi, s_lo, kz, arrived, tabled, ready, order, leave):
    for buf, pad in ((c_hi, KPAD), (c_lo, KPAD), (t_hi, FPAD), (t_lo, FPAD), (s_hi, FPAD), (s_lo, FPAD)):
        edge = jnp.zeros((pad, 2 * G, LANES), BF16)
        buf[pl.ds(0, pad)] = edge
        buf[pl.ds(TILES + pad, pad)] = edge

    def along_z(t, carry):
        lanes = pl.ds(pl.multiple_of(t * LANES, LANES), LANES)
        for s in range(2):
            rows = pl.ds(s * G, G)
            high, low = split(cube[s, :, lanes])
            c_hi[t + KPAD, rows, :] = high
            c_lo[t + KPAD, rows, :] = low
            both = mm(z_in[...], jnp.concatenate([high, low, high], 0))
            kz[t, rows, :] = both[G:]
            high, low = split(both[:G])
            t_hi[t + FPAD, rows, :] = high
            t_lo[t + FPAD, rows, :] = low
        return carry

    group = 2

    def spread(hi, lo, table, count, first, acc):
        for d in range(count):
            high = hi[pl.ds(first + d, group)].reshape(group * 2 * G, LANES)
            low = lo[pl.ds(first + d, group)].reshape(group * 2 * G, LANES)
            term = mm(high, table[0, d]) + mm(low, table[0, d]) + mm(high, table[1, d])
            acc = term if acc is None else acc + term
        return acc

    def middle(i, carry):
        first = i * group
        grid = spread(t_hi, t_lo, into, 2 * FPAD + 1, first, None)
        for j in range(group):
            lanes = pl.ds(pl.multiple_of((first + j) * LANES, LANES), LANES)
            local = vfull[:, lanes]
            for s in range(2):
                low_row = (j * 2 + s) * G
                high, low = split(grid[low_row : low_row + G] * local)
                done = mm(z_out[...], jnp.concatenate([high, low, high], 0))
                high, low = split(done)
                s_hi[first + j + FPAD, pl.ds(s * G, G), :] = high
                s_lo[first + j + FPAD, pl.ds(s * G, G), :] = low
        return carry

    def kinetic(i, carry):
        first = i * group
        acc = kz[pl.ds(first, group)].reshape(group * 2 * G, LANES)
        acc = spread(c_hi, c_lo, kin, 2 * KPAD + 1, first, acc)
        kz[pl.ds(first, group)] = acc.reshape(group, 2 * G, LANES)
        return carry

    tabled()
    per = TILES // CHUNKS
    for chunk in range(CHUNKS - 1):
        arrived(chunk)
        lax.fori_loop(chunk * per, (chunk + 1) * per, along_z, 0)
    early = (TILES - per - KPAD) // group
    lax.fori_loop(0, early, kinetic, 0)
    lax.fori_loop(0, early, middle, 0)
    arrived(CHUNKS - 1)
    lax.fori_loop(TILES - per, TILES, along_z, 0)
    lax.fori_loop(early, TILES // group, middle, 0)
    lax.fori_loop(early, TILES // group, kinetic, 0)

    def last(i, carry):
        first = order(i) * group
        acc = kz[pl.ds(first, group)].reshape(group * 2 * G, LANES)
        acc = spread(s_hi, s_lo, back, 2 * FPAD + 1, first, acc)
        for j in range(group):
            lanes = pl.ds(pl.multiple_of((first + j) * LANES, LANES), LANES)
            for s in range(2):
                low_row = (j * 2 + s) * G
                out[s, :, lanes] = acc[low_row : low_row + G]
        leave(first)
        return carry

    ready()
    lax.fori_loop(0, TILES // group, last, 0)


def dot_nt(left, right):
    return lax.dot_general(left, right, (((1,), (1,)), ((), ())), preferred_element_type=F32)


def inverse_of(mult_t, which):
    line = mult_t[which // 8, pl.ds(which % 8, 1), :]
    keep = lax.broadcasted_iota(jnp.int32, (1, ORBS), 1) == which
    diagonal = jnp.sum(jnp.where(keep, line, 0.0), axis=1, keepdims=True)
    return 1.0 / (2.0 * coupling_z + 4.0 * coupling_xy + 1.0 + jnp.abs(diagonal))


def relax(resid, inverse, box, direct_out):
    lane = lax.broadcasted_iota(jnp.int32, (32, 128), 1)
    row = lax.broadcasted_iota(jnp.int32, (32, 128), 0)
    inside = ((row >= 8) | (box > 0)) & ((row < 24) | (box < BOX - 1))
    factor = jnp.where(inside, jnp.broadcast_to(inverse, (32, 128)), 0.0)
    first_col, last_col, first_row = lane % G == 0, lane % G == G - 1, lane < G
    count = PLANE // 128
    start = [jnp.where(inside, resid[:, k * 128 : (k + 1) * 128], 0.0) for k in range(count)]
    now = [part * factor for part in start]
    for _ in range(SWEEPS):
        turned = [pltpu.roll(part, G, 1) for part in now]
        pairs = [turned[0]] + [turned[k - 1] + turned[k] for k in range(1, count)] + [turned[-1]]
        following = []
        for k in range(count):
            side = jnp.where(first_row, pairs[k], pairs[k + 1])
            side = side + jnp.where(first_col, 0.0, pltpu.roll(now[k], 1, 1))
            side = side + jnp.where(last_col, 0.0, pltpu.roll(now[k], 127, 1))
            along_z = pltpu.roll(now[k], 1, 0) + pltpu.roll(now[k], 31, 0)
            following.append((start[k] + coupling_xy * side + coupling_z * along_z) * factor)
        now = following
    for k in range(count):
        direct_out[:, k * 128 : (k + 1) * 128] = now[k][8:24]


def finish_kernel(resid, direct, mult, ext, inverse, resid_out, direct_out, mult_out, last, sems):
    box = lax.axis_index("box")
    done = pl.ds(0, OWN - 1)
    copies = [
        pltpu.make_async_copy(direct, direct_out.at[done], sems.at[0]),
        pltpu.make_async_copy(resid, resid_out.at[done], sems.at[1]),
        pltpu.make_async_copy(ext.at[pl.ds(8, DEPTH)], resid_out.at[OWN - 1], sems.at[2]),
        pltpu.make_async_copy(mult, mult_out, sems.at[3]),
    ]
    for copy in copies:
        copy.start()
    relax(ext[...], inverse[0:1, 0:1], box, last)
    copies.append(pltpu.make_async_copy(last, direct_out.at[OWN - 1], sems.at[4]))
    copies[-1].start()
    for copy in copies:
        copy.wait()


def step_kernel(
    psi, pot, slots, z_in_h, z_out_h, into_h, back_h, kin_h,
    resid_out, direct_out, mult_out, ext_out, inverse_out,
    pieces, app_pieces, cube, vfull, applied,
    z_in, z_out, into, back, kin,
    f_c_hi, f_c_lo, f_t_hi, f_t_lo, f_s_hi, f_s_lo, kz,
    part, rs, bb, mult, resid, c_hi, c_lo, a_hi, a_lo, a_sum, m_side, ext,
    own, y_send, y_recv, v_sem, p_sem, a_sem, r_sem, f_send, f_recv, h_send, h_recv, tab, plane_sem, all_sem,
):
    orb, box, x, z, core = place()
    table_copies = [
        pltpu.make_async_copy(src, dst, tab.at[i])
        for i, (src, dst) in enumerate(
            ((z_in_h, z_in), (z_out_h, z_out), (into_h, into), (back_h, back), (kin_h, kin))
        )
    ]
    slab = pl.ds(pl.multiple_of(box * DEPTH, DEPTH), DEPTH)
    width = PLANE // CHUNKS
    v_mine = pltpu.make_async_copy(pot, vfull.at[slab, :], own.at[0])
    target = pl.ds(pl.multiple_of(orb * SLOTS, SLOTS), SLOTS)
    z_rows, lanes = tile_of(orb)
    p_mine = pltpu.make_async_copy(psi.at[:, z_rows, lanes], pieces.at[target], own.at[1])
    c_mine = pltpu.make_async_copy(psi.at[pl.ds(2 * box, 2)], cube.at[:, slab, :], own.at[2])

    def meanwhile():
        for copy in [*table_copies, v_mine, p_mine, c_mine]:
            copy.start()

    beside = greet(orb, box, x, z, core, plane_sem, meanwhile)
    for chunk in range(CHUNKS):
        cols = pl.ds(chunk * width, width)
        for step in range(1, BOX):
            to = (box + step) % BOX
            remote(
                psi.at[pl.ds(2 * to, 2), :, cols], cube.at[:, slab, cols],
                y_send.at[chunk], y_recv.at[chunk], orb, to,
            ).start()
            if chunk == CHUNKS - 2:
                remote(pot, vfull.at[slab, :], v_sem.at[0], v_sem.at[1], orb, to).start()
    pl.semaphore_wait(plane_sem, 7)

    def send_psi(step, carry):
        to = shifted(orb, step)
        z_rows, lanes = tile_of(to)
        remote(psi.at[:, z_rows, lanes], pieces.at[target], p_sem.at[0], p_sem.at[1], to, box).start()
        return carry

    lax.fori_loop(1, ORB, send_psi, 0)
    beside(all_sem)

    def tabled():
        for copy in table_copies:
            copy.wait()

    def arrived(chunk):
        if chunk == 0:
            c_mine.wait()
        third = cube.at[:, pl.ds(0, 3 * DEPTH), pl.ds(chunk * width, width)]
        wait_for(third, y_recv.at[chunk])
        if chunk == CHUNKS - 2:
            v_mine.wait()
            wait_for(vfull.at[pl.ds(0, 3 * DEPTH)], v_sem.at[1])

    a_target = pl.ds(orb * SLOTS + 2 * box, 2)

    def source(to_orb, to_box):
        z_rows = pl.ds(pl.multiple_of(to_box * DEPTH + (to_orb // 32) * 8, 8), 8)
        return applied.at[:, z_rows, pl.ds(pl.multiple_of((to_orb % 32) * 128, 128), 128)]

    def ready():
        pl.semaphore_wait(all_sem, BOX - 1)

    def order(i):
        return (z // 2 + (1 + i) * (1 + 2 * core)) % 4 + 4 * ((i // 4 + x) % 2)

    def leave(first):
        def send_applied(step, carry):
            to_orb = ((step // BOX) % 2) * 32 + 2 * first + step // (2 * BOX)
            to_box = (box + step % BOX) % BOX

            @pl.when((to_orb != orb) | (to_box != box))
            def _():
                remote(
                    source(to_orb, to_box), app_pieces.at[a_target], a_sem.at[0], a_sem.at[1], to_orb, to_box
                ).start()

            return carry

        lax.fori_loop(0, 8 * BOX, send_applied, 0)

    filters(
        cube, vfull, z_in, z_out, into, back, kin, applied,
        f_c_hi, f_c_lo, f_t_hi, f_t_lo, f_s_hi, f_s_lo, kz, arrived, tabled, ready, order, leave,
    )
    a_mine = pltpu.make_async_copy(source(orb, box), app_pieces.at[a_target], own.at[3])
    a_mine.start()

    pieces2 = pieces.reshape(SLOTS * ORB * 8, 128)
    applied2 = app_pieces.reshape(SLOTS * ORB * 8, 128)
    resid2 = resid.reshape(ORBS * 8, 128)
    wanted = jnp.broadcast_to(slots[...].astype(F32), (ORBS, ORBS)).T
    column = lax.broadcasted_iota(jnp.int32, (ORBS, ORBS), 1).astype(F32)
    pick = jnp.concatenate(
        [(column + float(k * ORBS) == wanted).astype(F32) for k in range(SLOTS * ORB // ORBS)], 1
    ).astype(BF16)

    def choose(ref, hi, lo, both=None):
        for k in range(8):
            lanes = pl.ds(k * 128, 128)
            high, low = split(ref[pl.ds(k, SLOTS * ORB, stride=8), :])
            high, low = mm(pick, high), mm(pick, low)
            hi[:, lanes] = high.astype(BF16)
            lo[:, lanes] = low.astype(BF16)
            if both is not None:
                both[pl.ds(k * ORBS, ORBS), :] = high + low

    p_mine.wait()
    wait_for(pieces.at[pl.ds(0, SLOTS * (ORB - 1))], p_sem.at[1])
    choose(pieces2, c_hi, c_lo)
    a_mine.wait()
    wait_for(app_pieces.at[pl.ds(0, SLOTS * ORB - 2)], a_sem.at[1])
    choose(applied2, a_hi, a_lo, a_sum)

    scale = 1.0 / float(G**3)
    total = dot_nt(a_hi[...], c_hi[...]) + dot_nt(a_hi[...], c_lo[...]) + dot_nt(a_lo[...], c_hi[...])
    part[...] = (total * scale).reshape(32, 8, ORBS)

    a_me = (x * 4 + box) * 2 + core

    def a_peer(step):
        to_orb = ((x + step // 8) % 4) * 16 + z * 2 + (core + step % 2) % 2
        return to_orb, (box + (step // 2) % 4) % 4

    for step in range(1, 32):
        to_orb, to_box = a_peer(step)
        a_to = ((to_orb // 16) * 4 + to_box) * 2 + to_orb % 2
        remote(part.at[a_to], rs.at[a_me], r_sem.at[0], r_sem.at[1], to_orb, to_box).start()
    rs[a_me] = part[a_me]
    wait_for(rs.at[pl.ds(0, 31)], r_sem.at[1])
    bb[z] = jnp.sum(rs[...], axis=0)
    for step in range(1, 8):
        to_orb = x * 16 + ((z + step) % 8) * 2 + core
        remote(bb.at[z], bb.at[z], r_sem.at[2], r_sem.at[3], to_orb, box).start()
    wait_for(bb.at[pl.ds(0, 7)], r_sem.at[3])
    mult[a_me] = jnp.sum(bb[...], axis=0)
    for step in range(1, 32):
        to_orb, to_box = a_peer(step)
        remote(mult.at[a_me], mult.at[a_me], r_sem.at[4], r_sem.at[5], to_orb, to_box).start()
    wait_for(mult.at[pl.ds(0, 31)], r_sem.at[5])
    z_rows = pl.ds(pl.multiple_of(8 + (orb // 32) * 8, 8), 8)
    lanes = pl.ds(pl.multiple_of((orb % 32) * 128, 128), 128)
    r_mine = []
    mult2 = mult.reshape(ORBS, ORBS)
    for h in range(2):
        m_side[pl.ds(h * ORBS, ORBS), :] = mult2[:, pl.ds(h * 128, 128)]
    for g, (first, count) in enumerate(GROUPS):
        members = range(first, first + count)
        sides = [
            jnp.concatenate([m_side[pl.ds(h * ORBS + n, ORB, stride=OWN), :] for n in members], 0)
            for h in range(2)
        ]
        m_hi, m_lo = split(jnp.concatenate(sides, 1))
        fix = mm(m_hi, c_hi[...]) + mm(m_hi, c_lo[...]) + mm(m_lo, c_hi[...])
        for i, n in enumerate(members):
            for k in range(8):
                part_fix = fix[i * ORB : (i + 1) * ORB, k * 128 : (k + 1) * 128]
                value = a_sum[pl.ds(k * ORBS + n, ORB, stride=OWN), :] - part_fix
                resid2[pl.ds(n * 8 + k, ORB, stride=OWN * 8), :] = value
        landing = ext.at[pl.ds(first, count), z_rows, lanes]
        copy = pltpu.make_async_copy(resid.at[pl.ds(orb * OWN + first, count)], landing, own.at[4 + g])
        copy.start()
        r_mine.append(copy)

        def send_resid(step, carry, g=g, first=first, count=count, landing=landing):
            to = shifted(orb, step)
            remote(
                resid.at[pl.ds(to * OWN + first, count)], landing, f_send, f_recv.at[g], to, box
            ).start()
            return carry

        lax.fori_loop(1, ORB, send_resid, 0)

    def halo(g):
        r_mine[g].wait()
        first, count = GROUPS[g]
        wait_for(resid.at[pl.ds(0, count * (ORB - 1))], f_recv.at[g])
        some = pl.ds(first, count)
        up = remote(
            ext.at[some, pl.ds(20, 4), :], ext.at[some, pl.ds(4, 4), :],
            h_send.at[2 * g], h_recv.at[2 * g], orb, (box + 1) % BOX,
        )
        down = remote(
            ext.at[some, pl.ds(8, 4), :], ext.at[some, pl.ds(24, 4), :],
            h_send.at[2 * g + 1], h_recv.at[2 * g + 1], orb, (box + 3) % BOX,
        )
        up.start()
        down.start()
        return up, down

    def finish(g, pair):
        for copy in pair:
            copy.wait()
        first, count = GROUPS[g]
        for n in range(first, first + count):
            resid_out[n] = ext[n, 8:24, :]
            relax(ext[n], inverse_of(mult, orb * OWN + n), box, direct_out.at[n])

    mult_out[...] = mult2[...].T
    inverse_out[...] = jnp.broadcast_to(inverse_of(mult, orb * OWN + OWN - 1), (8, 128))
    pair = halo(0)
    for g in range(1, len(GROUPS)):
        following = halo(g)
        finish(g - 1, pair)
        pair = following
    for chunk in range(CHUNKS):
        wait_for(cube.at[:, pl.ds(0, 3 * DEPTH), pl.ds(chunk * width, width)], y_send.at[chunk])
    wait_for(vfull.at[pl.ds(0, 3 * DEPTH)], v_sem.at[0])
    wait_for(pieces.at[pl.ds(0, SLOTS * (ORB - 1))], p_sem.at[0])
    wait_for(app_pieces.at[pl.ds(0, SLOTS * ORB - 2)], a_sem.at[0])
    wait_for(part.at[pl.ds(0, 31)], r_sem.at[0])
    wait_for(bb.at[pl.ds(0, 7)], r_sem.at[2])
    wait_for(mult.at[pl.ds(0, 31)], r_sem.at[4])
    wait_for(resid.at[pl.ds(0, OWN * (ORB - 1))], f_send)
    for copy in pair:
        copy.wait()
    ext_out[...] = ext[OWN - 1]


DMA = pltpu.SemaphoreType.DMA
REGULAR = pltpu.SemaphoreType.REGULAR


def shape(*dims, dtype=F32):
    return jax.ShapeDtypeStruct(dims, dtype)


def local(psi, potential, orbital_slot):
    consts = [jnp.asarray(t) for t in tables()]
    v32 = lambda *dims: pltpu.VMEM(dims, F32)
    v16 = lambda *dims: pltpu.VMEM(dims, BF16)
    padded = lambda pad: v16(TILES + 2 * pad, 2 * G, LANES)
    residual, direction, mult, ext, inverse = pl.pallas_call(
        step_kernel,
        out_shape=[
            v32(OWN - 1, DEPTH, PLANE), v32(OWN - 1, DEPTH, PLANE), v32(ORBS, ORBS),
            v32(32, PLANE), v32(8, 128),
        ],
        in_specs=[ANY, ANY, VMEM] + [ANY] * 5,
        out_specs=[VMEM] * 5,
        scratch_shapes=[
            v32(SLOTS * ORB, 8, 128), v32(SLOTS * ORB, 8, 128),
            v32(2, G, PLANE), v32(G, PLANE), v32(2, G, PLANE),
        ]
        + [v16(*t.shape) for t in consts]
        + [padded(KPAD)] * 2 + [padded(FPAD)] * 4 + [v32(TILES, 2 * G, LANES)]
        + [v32(32, 8, ORBS)] * 2 + [v32(8, 8, ORBS)] + [v32(32, 8, ORBS)] + [v32(ORBS, 8, 128)]
        + [v16(ORBS, 1024)] * 4 + [v32(8 * ORBS, 128), v32(2 * ORBS, 128)] + [v32(OWN, 32, PLANE)]
        + [
            DMA((8,)), DMA((CHUNKS,)), DMA((CHUNKS,)), DMA((2,)), DMA((2,)), DMA((2,)), DMA((6,)),
            DMA, DMA((OWN,)), DMA((2 * OWN,)), DMA((2 * OWN,)), DMA((5,)), REGULAR, REGULAR,
        ],
        compiler_params=pltpu.CompilerParams(
            has_side_effects=True, vmem_limit_bytes=VLIMIT, collective_id=0
        ),
        name="orbital_step",
    )(psi, potential, orbital_slot.reshape(1, ORBS), *consts)
    return pl.pallas_call(
        finish_kernel,
        out_shape=[shape(OWN, DEPTH, PLANE), shape(OWN, DEPTH, PLANE), shape(ORBS, ORBS)],
        in_specs=[VMEM] * 5,
        out_specs=[ANY] * 3,
        scratch_shapes=[v32(DEPTH, PLANE), DMA((5,))],
        compiler_params=pltpu.CompilerParams(vmem_limit_bytes=16 * 2**20),
        name="last_orbital",
    )(residual, direction, mult, ext, inverse)


def solution(mesh):
    in_specs = (P("orb", "box", None), P("box", None), P())
    out_specs = (P("orb", "box", None), P("orb", "box", None), P())
    return jax.shard_map(local, mesh=mesh, in_specs=in_specs, out_specs=out_specs, check_vma=False)
```

```python
import math

import jax
import jax.numpy as jnp
import ml_dtypes
import numpy as np
from jax import lax
from jax.experimental import pallas as pl
from jax.experimental.pallas import tpu as pltpu
from jax.sharding import PartitionSpec as P

G = 64
MTAPS = 16
KREACH = 14
SWEEPS = 4
ORB, BOX = 64, 4
SLOTS, ORBS, OWN = 8, 256, 4
DEPTH = 16
PLANE = G * G
LANES = 256
TILES = PLANE // LANES
FPAD, KPAD = 2, 4

coupling_z = 4.0
coupling_xy = 1.0

F32, BF16 = jnp.float32, jnp.bfloat16
ANY = pl.BlockSpec(memory_space=pl.ANY)
VMEM = pl.BlockSpec(memory_space=pltpu.VMEM)
VLIMIT = 56 * 2**20


def magic_weights(tap_count):
    half_len = tap_count // 2
    offsets = np.arange(1 - half_len, half_len + 1) * 1.0
    weights = np.ones(tap_count)
    for index_a in range(tap_count):
        for index_b in range(tap_count):
            if index_b != index_a:
                weights[index_a] *= (0.25 - offsets[index_b]) / (
                    offsets[index_a] - offsets[index_b]
                )
    return weights


def second_weights(reach_cells):
    factor = math.factorial(reach_cells) ** 2
    weights = np.zeros(2 * reach_cells + 1)
    for distance in range(1, reach_cells + 1):
        entry_value = (
            2.0
            * (-1) ** (distance + 1)
            * factor
            / (
                distance
                * distance
                * math.factorial(reach_cells - distance)
                * math.factorial(reach_cells + distance)
            )
        )
        weights[reach_cells + distance] = entry_value
        weights[reach_cells - distance] = entry_value
    weights[reach_cells] = -weights.sum()
    return -0.5 * weights


def banded(row_count, col_count, row_start, col_start, weights, offset_low):
    row_index = np.arange(row_count)[:, None] + row_start
    col_index = np.arange(col_count)[None, :] + col_start
    position = row_index - col_index - offset_low
    inside = (position >= 0) & (position < len(weights))
    return np.where(inside, weights[np.clip(position, 0, len(weights) - 1)], 0.0)


def halves(table):
    table = np.asarray(table, np.float32)
    high = table.astype(ml_dtypes.bfloat16)
    low = (table - high.astype(np.float32)).astype(ml_dtypes.bfloat16)
    return high, low


def tables():
    magic = magic_weights(MTAPS)
    kinetic_row = second_weights(KREACH)
    forward = banded(G, G, 0, 0, magic, 1 - MTAPS // 2)
    kinetic = banded(G, G, 0, 0, kinetic_row, -KREACH)
    rows = LANES // G

    def beside(high, low):
        return np.concatenate([high, high, low], 1)

    z_in = beside(*halves(np.concatenate([forward.T, kinetic], 0)))
    z_out = beside(*halves(forward))
    into, back, kin = [], [], []
    for step in range(-FPAD, FPAD + 1):
        block = banded(rows, rows, rows * step, 0, magic, 1 - MTAPS // 2)
        into.append(np.kron(block, forward))
        block = banded(rows, rows, -rows * step, 0, magic, 1 - MTAPS // 2).T
        back.append(np.kron(block, forward.T))
    for step in range(-KPAD, KPAD + 1):
        block = np.kron(banded(rows, rows, rows * step, 0, kinetic_row, -KREACH), np.eye(G))
        if step == 0:
            block = block + np.kron(np.eye(rows), kinetic)
        kin.append(block)
    return [z_in, z_out] + [np.stack(halves(np.stack(m))) for m in (into, back, kin)]


def split(values):
    high = values.astype(BF16)
    return high, (values - high.astype(F32)).astype(BF16)


def mm(left, right):
    return jnp.dot(left, right, preferred_element_type=F32)


def place():
    orb = lax.axis_index("orb")
    box = lax.axis_index("box")
    return orb, box, orb // 16, (orb // 2) % 8, orb % 2


def shifted(orb, step):
    x, z, core = orb // 16, (orb // 2) % 8, orb % 2
    dx, dz, dc = step // 16, (step // 2) % 8, step % 2
    x, z = (x + dx * (1 + 2 * core)) % 4, (z + dz * (1 + 6 * core)) % 8
    return x * 16 + z * 2 + (core + dc) % 2


def remote(src, dst, send, recv, orb, box):
    return pltpu.make_async_remote_copy(
        src_ref=src,
        dst_ref=dst,
        send_sem=send,
        recv_sem=recv,
        device_id={"orb": orb, "box": box},
        device_id_type=pl.DeviceIdType.MESH,
    )


def wait_for(ref, sem):
    pltpu.make_async_copy(ref, ref, sem).wait()


def tile_of(orb):
    return pl.ds(pl.multiple_of((orb // 32) * 8, 8), 8), pl.ds(
        pl.multiple_of((orb % 32) * 128, 128), 128
    )


CHUNKS = 4
GROUPS = ((0, 2), (2, 1), (3, 1))


def greet(orb, box, x, z, core, plane_sem, meanwhile):
    barrier = pltpu.get_barrier_semaphore()

    def signal(sem, to_orb, to_box):
        pl.semaphore_signal(
            sem, inc=1, device_id={"orb": to_orb, "box": to_box}, device_id_type=pl.DeviceIdType.MESH
        )

    def along_z(step, carry):
        signal(barrier, x * 16 + ((z + step) % 8) * 2 + core, box)
        return carry

    def across(sem):
        def body(step, carry):
            signal(sem, ((x + step // 2) % 4) * 16 + z * 2 + (core + step % 2) % 2, box)
            return carry

        return body

    def beside(sem):
        for step in range(1, BOX):
            signal(sem, orb, (box + step) % BOX)

    lax.fori_loop(1, 8, along_z, 0)
    lax.fori_loop(1, 8, across(barrier), 0)
    beside(barrier)
    meanwhile()
    pl.semaphore_wait(barrier, 7 + 7 + 3)
    lax.fori_loop(1, 8, across(plane_sem), 0)
    return beside


def filters(cube, vfull, z_in, z_out, into, back, kin, out, c_hi, c_lo, t_hi, t_lo, s_hi, s_lo, kz, arrived, tabled, ready, order, leave):
    for buf, pad in ((c_hi, KPAD), (c_lo, KPAD), (t_hi, FPAD), (t_lo, FPAD), (s_hi, FPAD), (s_lo, FPAD)):
        edge = jnp.zeros((pad, 2 * G, LANES), BF16)
        buf[pl.ds(0, pad)] = edge
        buf[pl.ds(TILES + pad, pad)] = edge

    def along_z(t, carry):
        lanes = pl.ds(pl.multiple_of(t * LANES, LANES), LANES)
        for s in range(2):
            rows = pl.ds(s * G, G)
            high, low = split(cube[s, :, lanes])
            c_hi[t + KPAD, rows, :] = high
            c_lo[t + KPAD, rows, :] = low
            both = mm(z_in[...], jnp.concatenate([high, low, high], 0))
            kz[t, rows, :] = both[G:]
            high, low = split(both[:G])
            t_hi[t + FPAD, rows, :] = high
            t_lo[t + FPAD, rows, :] = low
        return carry

    group = 2

    def spread(hi, lo, table, count, first, acc):
        for d in range(count):
            high = hi[pl.ds(first + d, group)].reshape(group * 2 * G, LANES)
            low = lo[pl.ds(first + d, group)].reshape(group * 2 * G, LANES)
            term = mm(high, table[0, d]) + mm(low, table[0, d]) + mm(high, table[1, d])
            acc = term if acc is None else acc + term
        return acc

    def middle(i, carry):
        first = i * group
        grid = spread(t_hi, t_lo, into, 2 * FPAD + 1, first, None)
        for j in range(group):
            lanes = pl.ds(pl.multiple_of((first + j) * LANES, LANES), LANES)
            local = vfull[:, lanes]
            for s in range(2):
                low_row = (j * 2 + s) * G
                high, low = split(grid[low_row : low_row + G] * local)
                done = mm(z_out[...], jnp.concatenate([high, low, high], 0))
                high, low = split(done)
                s_hi[first + j + FPAD, pl.ds(s * G, G), :] = high
                s_lo[first + j + FPAD, pl.ds(s * G, G), :] = low
        return carry

    def kinetic(i, carry):
        first = i * group
        acc = kz[pl.ds(first, group)].reshape(group * 2 * G, LANES)
        acc = spread(c_hi, c_lo, kin, 2 * KPAD + 1, first, acc)
        kz[pl.ds(first, group)] = acc.reshape(group, 2 * G, LANES)
        return carry

    tabled()
    per = TILES // CHUNKS
    for chunk in range(CHUNKS - 1):
        arrived(chunk)
        lax.fori_loop(chunk * per, (chunk + 1) * per, along_z, 0)
    early = (TILES - per - KPAD) // group
    lax.fori_loop(0, early, kinetic, 0)
    lax.fori_loop(0, early, middle, 0)
    arrived(CHUNKS - 1)
    lax.fori_loop(TILES - per, TILES, along_z, 0)
    lax.fori_loop(early, TILES // group, middle, 0)
    lax.fori_loop(early, TILES // group, kinetic, 0)

    def last(i, carry):
        first = order(i) * group
        acc = kz[pl.ds(first, group)].reshape(group * 2 * G, LANES)
        acc = spread(s_hi, s_lo, back, 2 * FPAD + 1, first, acc)
        for j in range(group):
            lanes = pl.ds(pl.multiple_of((first + j) * LANES, LANES), LANES)
            for s in range(2):
                low_row = (j * 2 + s) * G
                out[s, :, lanes] = acc[low_row : low_row + G]
        leave(first)
        return carry

    ready()
    lax.fori_loop(0, TILES // group, last, 0)


def dot_nt(left, right):
    return lax.dot_general(left, right, (((1,), (1,)), ((), ())), preferred_element_type=F32)


def inverse_of(mult_t, which):
    line = mult_t[which // 8, pl.ds(which % 8, 1), :]
    keep = lax.broadcasted_iota(jnp.int32, (1, ORBS), 1) == which
    diagonal = jnp.sum(jnp.where(keep, line, 0.0), axis=1, keepdims=True)
    return 1.0 / (2.0 * coupling_z + 4.0 * coupling_xy + 1.0 + jnp.abs(diagonal))


def relax(resid, inverse, box, direct_out):
    lane = lax.broadcasted_iota(jnp.int32, (32, 128), 1)
    row = lax.broadcasted_iota(jnp.int32, (32, 128), 0)
    inside = ((row >= 8) | (box > 0)) & ((row < 24) | (box < BOX - 1))
    factor = jnp.where(inside, jnp.broadcast_to(inverse, (32, 128)), 0.0)
    first_col, last_col, first_row = lane % G == 0, lane % G == G - 1, lane < G
    count = PLANE // 128
    start = [jnp.where(inside, resid[:, k * 128 : (k + 1) * 128], 0.0) for k in range(count)]
    now = [part * factor for part in start]
    for _ in range(SWEEPS):
        turned = [pltpu.roll(part, G, 1) for part in now]
        pairs = [turned[0]] + [turned[k - 1] + turned[k] for k in range(1, count)] + [turned[-1]]
        following = []
        for k in range(count):
            side = jnp.where(first_row, pairs[k], pairs[k + 1])
            side = side + jnp.where(first_col, 0.0, pltpu.roll(now[k], 1, 1))
            side = side + jnp.where(last_col, 0.0, pltpu.roll(now[k], 127, 1))
            along_z = pltpu.roll(now[k], 1, 0) + pltpu.roll(now[k], 31, 0)
            following.append((start[k] + coupling_xy * side + coupling_z * along_z) * factor)
        now = following
    for k in range(count):
        direct_out[:, k * 128 : (k + 1) * 128] = now[k][8:24]


def finish_kernel(resid, direct, mult, ext, inverse, resid_out, direct_out, mult_out, last, sems):
    box = lax.axis_index("box")
    done = pl.ds(0, OWN - 1)
    copies = [
        pltpu.make_async_copy(direct, direct_out.at[done], sems.at[0]),
        pltpu.make_async_copy(resid, resid_out.at[done], sems.at[1]),
        pltpu.make_async_copy(ext.at[pl.ds(8, DEPTH)], resid_out.at[OWN - 1], sems.at[2]),
        pltpu.make_async_copy(mult, mult_out, sems.at[3]),
    ]
    for copy in copies:
        copy.start()
    relax(ext[...], inverse[0:1, 0:1], box, last)
    copies.append(pltpu.make_async_copy(last, direct_out.at[OWN - 1], sems.at[4]))
    copies[-1].start()
    for copy in copies:
        copy.wait()


def step_kernel(
    psi, pot, slots, z_in_h, z_out_h, into_h, back_h, kin_h,
    resid_out, direct_out, mult_out, ext_out, inverse_out,
    pieces, app_pieces, cube, vfull, applied,
    z_in, z_out, into, back, kin,
    f_c_hi, f_c_lo, f_t_hi, f_t_lo, f_s_hi, f_s_lo, kz,
    part, rs, bb, mult, resid, c_hi, c_lo, a_hi, a_lo, a_sum, m_side, ext,
    own, y_send, y_recv, v_sem, p_sem, a_sem, r_sem, f_send, f_recv, h_send, h_recv, tab, plane_sem, all_sem,
):
    orb, box, x, z, core = place()
    table_copies = [
        pltpu.make_async_copy(src, dst, tab.at[i])
        for i, (src, dst) in enumerate(
            ((z_in_h, z_in), (z_out_h, z_out), (into_h, into), (back_h, back), (kin_h, kin))
        )
    ]
    slab = pl.ds(pl.multiple_of(box * DEPTH, DEPTH), DEPTH)
    width = PLANE // CHUNKS
    v_mine = pltpu.make_async_copy(pot, vfull.at[slab, :], own.at[0])
    target = pl.ds(pl.multiple_of(orb * SLOTS, SLOTS), SLOTS)
    z_rows, lanes = tile_of(orb)
    p_mine = pltpu.make_async_copy(psi.at[:, z_rows, lanes], pieces.at[target], own.at[1])
    c_mine = pltpu.make_async_copy(psi.at[pl.ds(2 * box, 2)], cube.at[:, slab, :], own.at[2])

    def meanwhile():
        for copy in [*table_copies, v_mine, p_mine, c_mine]:
            copy.start()

    beside = greet(orb, box, x, z, core, plane_sem, meanwhile)

    def send_psi(step, carry):
        to = shifted(orb, step)
        z_rows, lanes = tile_of(to)
        remote(psi.at[:, z_rows, lanes], pieces.at[target], p_sem.at[0], p_sem.at[1], to, box).start()
        return carry

    lax.fori_loop(1, 8, lambda step, carry: send_psi(2 * step, carry), 0)
    for chunk in range(CHUNKS):
        cols = pl.ds(chunk * width, width)
        for step in range(1, BOX):
            to = (box + step) % BOX
            remote(
                psi.at[pl.ds(2 * to, 2), :, cols], cube.at[:, slab, cols],
                y_send.at[chunk], y_recv.at[chunk], orb, to,
            ).start()
            if chunk == CHUNKS - 2:
                remote(pot, vfull.at[slab, :], v_sem.at[0], v_sem.at[1], orb, to).start()
    pl.semaphore_wait(plane_sem, 7)

    def send_far(i, carry):
        apart = 1 + i // 8
        return send_psi((apart // 2) * 16 + (i % 8) * 2 + apart % 2, carry)

    lax.fori_loop(0, ORB - 8, send_far, 0)
    beside(all_sem)

    def tabled():
        for copy in table_copies:
            copy.wait()

    def arrived(chunk):
        if chunk == 0:
            c_mine.wait()
        third = cube.at[:, pl.ds(0, 3 * DEPTH), pl.ds(chunk * width, width)]
        wait_for(third, y_recv.at[chunk])
        if chunk == CHUNKS - 2:
            v_mine.wait()
            wait_for(vfull.at[pl.ds(0, 3 * DEPTH)], v_sem.at[1])

    a_target = pl.ds(orb * SLOTS + 2 * box, 2)

    def source(to_orb, to_box):
        z_rows = pl.ds(pl.multiple_of(to_box * DEPTH + (to_orb // 32) * 8, 8), 8)
        return applied.at[:, z_rows, pl.ds(pl.multiple_of((to_orb % 32) * 128, 128), 128)]

    def ready():
        pl.semaphore_wait(all_sem, BOX - 1)

    def order(i):
        return (z // 2 + (1 + i) * (1 + 2 * core)) % 4 + 4 * ((i // 4 + x) % 2)

    def leave(first):
        def send_applied(step, carry):
            to_orb = ((step // BOX) % 2) * 32 + 2 * first + step // (2 * BOX)
            to_box = (box + step % BOX) % BOX

            @pl.when((to_orb != orb) | (to_box != box))
            def _():
                remote(
                    source(to_orb, to_box), app_pieces.at[a_target], a_sem.at[0], a_sem.at[1], to_orb, to_box
                ).start()

            return carry

        lax.fori_loop(0, 8 * BOX, send_applied, 0)

    filters(
        cube, vfull, z_in, z_out, into, back, kin, applied,
        f_c_hi, f_c_lo, f_t_hi, f_t_lo, f_s_hi, f_s_lo, kz, arrived, tabled, ready, order, leave,
    )
    a_mine = pltpu.make_async_copy(source(orb, box), app_pieces.at[a_target], own.at[3])
    a_mine.start()

    pieces2 = pieces.reshape(SLOTS * ORB * 8, 128)
    applied2 = app_pieces.reshape(SLOTS * ORB * 8, 128)
    resid2 = resid.reshape(ORBS * 8, 128)
    wanted = jnp.broadcast_to(slots[...].astype(F32), (ORBS, ORBS)).T
    column = lax.broadcasted_iota(jnp.int32, (ORBS, ORBS), 1).astype(F32)
    pick = jnp.concatenate(
        [(column + float(k * ORBS) == wanted).astype(F32) for k in range(SLOTS * ORB // ORBS)], 1
    ).astype(BF16)

    def choose(ref, hi, lo, both=None):
        for k in range(8):
            lanes = pl.ds(k * 128, 128)
            high, low = split(ref[pl.ds(k, SLOTS * ORB, stride=8), :])
            high, low = mm(pick, high), mm(pick, low)
            hi[:, lanes] = high.astype(BF16)
            lo[:, lanes] = low.astype(BF16)
            if both is not None:
                both[pl.ds(k * ORBS, ORBS), :] = high + low

    p_mine.wait()
    wait_for(pieces.at[pl.ds(0, SLOTS * (ORB - 1))], p_sem.at[1])
    choose(pieces2, c_hi, c_lo)
    a_mine.wait()
    wait_for(app_pieces.at[pl.ds(0, SLOTS * ORB - 2)], a_sem.at[1])
    choose(applied2, a_hi, a_lo, a_sum)

    scale = 1.0 / float(G**3)
    total = dot_nt(a_hi[...], c_hi[...]) + dot_nt(a_hi[...], c_lo[...]) + dot_nt(a_lo[...], c_hi[...])
    part[...] = (total * scale).reshape(32, 8, ORBS)

    a_me = (x * 4 + box) * 2 + core

    def a_peer(step):
        to_orb = ((x + step // 8) % 4) * 16 + z * 2 + (core + step % 2) % 2
        return to_orb, (box + (step // 2) % 4) % 4

    for step in range(1, 32):
        to_orb, to_box = a_peer(step)
        a_to = ((to_orb // 16) * 4 + to_box) * 2 + to_orb % 2
        remote(part.at[a_to], rs.at[a_me], r_sem.at[0], r_sem.at[1], to_orb, to_box).start()
    rs[a_me] = part[a_me]
    wait_for(rs.at[pl.ds(0, 31)], r_sem.at[1])
    bb[z] = jnp.sum(rs[...], axis=0)
    for step in range(1, 8):
        to_orb = x * 16 + ((z + step) % 8) * 2 + core
        remote(bb.at[z], bb.at[z], r_sem.at[2], r_sem.at[3], to_orb, box).start()
    wait_for(bb.at[pl.ds(0, 7)], r_sem.at[3])
    mult[a_me] = jnp.sum(bb[...], axis=0)
    for step in range(1, 32):
        to_orb, to_box = a_peer(step)
        remote(mult.at[a_me], mult.at[a_me], r_sem.at[4], r_sem.at[5], to_orb, to_box).start()
    wait_for(mult.at[pl.ds(0, 31)], r_sem.at[5])
    z_rows = pl.ds(pl.multiple_of(8 + (orb // 32) * 8, 8), 8)
    lanes = pl.ds(pl.multiple_of((orb % 32) * 128, 128), 128)
    r_mine = []
    mult2 = mult.reshape(ORBS, ORBS)
    for h in range(2):
        m_side[pl.ds(h * ORBS, ORBS), :] = mult2[:, pl.ds(h * 128, 128)]
    for g, (first, count) in enumerate(GROUPS):
        members = range(first, first + count)
        sides = [
            jnp.concatenate([m_side[pl.ds(h * ORBS + n, ORB, stride=OWN), :] for n in members], 0)
            for h in range(2)
        ]
        m_hi, m_lo = split(jnp.concatenate(sides, 1))
        fix = mm(m_hi, c_hi[...]) + mm(m_hi, c_lo[...]) + mm(m_lo, c_hi[...])
        for i, n in enumerate(members):
            for k in range(8):
                part_fix = fix[i * ORB : (i + 1) * ORB, k * 128 : (k + 1) * 128]
                value = a_sum[pl.ds(k * ORBS + n, ORB, stride=OWN), :] - part_fix
                resid2[pl.ds(n * 8 + k, ORB, stride=OWN * 8), :] = value
        landing = ext.at[pl.ds(first, count), z_rows, lanes]
        copy = pltpu.make_async_copy(resid.at[pl.ds(orb * OWN + first, count)], landing, own.at[4 + g])
        copy.start()
        r_mine.append(copy)

        def send_resid(step, carry, g=g, first=first, count=count, landing=landing):
            to = shifted(orb, step)
            remote(
                resid.at[pl.ds(to * OWN + first, count)], landing, f_send, f_recv.at[g], to, box
            ).start()
            return carry

        lax.fori_loop(1, ORB, send_resid, 0)

    def halo(g):
        r_mine[g].wait()
        first, count = GROUPS[g]
        wait_for(resid.at[pl.ds(0, count * (ORB - 1))], f_recv.at[g])
        some = pl.ds(first, count)
        up = remote(
            ext.at[some, pl.ds(20, 4), :], ext.at[some, pl.ds(4, 4), :],
            h_send.at[2 * g], h_recv.at[2 * g], orb, (box + 1) % BOX,
        )
        down = remote(
            ext.at[some, pl.ds(8, 4), :], ext.at[some, pl.ds(24, 4), :],
            h_send.at[2 * g + 1], h_recv.at[2 * g + 1], orb, (box + 3) % BOX,
        )
        up.start()
        down.start()
        return up, down

    def finish(g, pair):
        for copy in pair:
            copy.wait()
        first, count = GROUPS[g]
        for n in range(first, first + count):
            resid_out[n] = ext[n, 8:24, :]
            relax(ext[n], inverse_of(mult, orb * OWN + n), box, direct_out.at[n])

    mult_out[...] = mult2[...].T
    inverse_out[...] = jnp.broadcast_to(inverse_of(mult, orb * OWN + OWN - 1), (8, 128))
    pair = halo(0)
    for g in range(1, len(GROUPS)):
        following = halo(g)
        finish(g - 1, pair)
        pair = following
    for chunk in range(CHUNKS):
        wait_for(cube.at[:, pl.ds(0, 3 * DEPTH), pl.ds(chunk * width, width)], y_send.at[chunk])
    wait_for(vfull.at[pl.ds(0, 3 * DEPTH)], v_sem.at[0])
    wait_for(pieces.at[pl.ds(0, SLOTS * (ORB - 1))], p_sem.at[0])
    wait_for(app_pieces.at[pl.ds(0, SLOTS * ORB - 2)], a_sem.at[0])
    wait_for(part.at[pl.ds(0, 31)], r_sem.at[0])
    wait_for(bb.at[pl.ds(0, 7)], r_sem.at[2])
    wait_for(mult.at[pl.ds(0, 31)], r_sem.at[4])
    wait_for(resid.at[pl.ds(0, OWN * (ORB - 1))], f_send)
    for copy in pair:
        copy.wait()
    ext_out[...] = ext[OWN - 1]


DMA = pltpu.SemaphoreType.DMA
REGULAR = pltpu.SemaphoreType.REGULAR


def shape(*dims, dtype=F32):
    return jax.ShapeDtypeStruct(dims, dtype)


def local(psi, potential, orbital_slot):
    consts = [jnp.asarray(t) for t in tables()]
    v32 = lambda *dims: pltpu.VMEM(dims, F32)
    v16 = lambda *dims: pltpu.VMEM(dims, BF16)
    padded = lambda pad: v16(TILES + 2 * pad, 2 * G, LANES)
    residual, direction, mult, ext, inverse = pl.pallas_call(
        step_kernel,
        out_shape=[
            v32(OWN - 1, DEPTH, PLANE), v32(OWN - 1, DEPTH, PLANE), v32(ORBS, ORBS),
            v32(32, PLANE), v32(8, 128),
        ],
        in_specs=[ANY, ANY, VMEM] + [ANY] * 5,
        out_specs=[VMEM] * 5,
        scratch_shapes=[
            v32(SLOTS * ORB, 8, 128), v32(SLOTS * ORB, 8, 128),
            v32(2, G, PLANE), v32(G, PLANE), v32(2, G, PLANE),
        ]
        + [v16(*t.shape) for t in consts]
        + [padded(KPAD)] * 2 + [padded(FPAD)] * 4 + [v32(TILES, 2 * G, LANES)]
        + [v32(32, 8, ORBS)] * 2 + [v32(8, 8, ORBS)] + [v32(32, 8, ORBS)] + [v32(ORBS, 8, 128)]
        + [v16(ORBS, 1024)] * 4 + [v32(8 * ORBS, 128), v32(2 * ORBS, 128)] + [v32(OWN, 32, PLANE)]
        + [
            DMA((8,)), DMA((CHUNKS,)), DMA((CHUNKS,)), DMA((2,)), DMA((2,)), DMA((2,)), DMA((6,)),
            DMA, DMA((OWN,)), DMA((2 * OWN,)), DMA((2 * OWN,)), DMA((5,)), REGULAR, REGULAR,
        ],
        compiler_params=pltpu.CompilerParams(
            has_side_effects=True, vmem_limit_bytes=VLIMIT, collective_id=0
        ),
        name="orbital_step",
    )(psi, potential, orbital_slot.reshape(1, ORBS), *consts)
    return pl.pallas_call(
        finish_kernel,
        out_shape=[shape(OWN, DEPTH, PLANE), shape(OWN, DEPTH, PLANE), shape(ORBS, ORBS)],
        in_specs=[VMEM] * 5,
        out_specs=[ANY] * 3,
        scratch_shapes=[v32(DEPTH, PLANE), DMA((5,))],
        compiler_params=pltpu.CompilerParams(vmem_limit_bytes=16 * 2**20),
        name="last_orbital",
    )(residual, direction, mult, ext, inverse)


def solution(mesh):
    in_specs = (P("orb", "box", None), P("box", None), P())
    out_specs = (P("orb", "box", None), P("orb", "box", None), P())
    return jax.shard_map(local, mesh=mesh, in_specs=in_specs, out_specs=out_specs, check_vma=False)
```

```python
import math

import jax
import jax.numpy as jnp
import ml_dtypes
import numpy as np
from jax import lax
from jax.experimental import pallas as pl
from jax.experimental.pallas import tpu as pltpu
from jax.sharding import PartitionSpec as P

G = 64
MTAPS = 16
KREACH = 14
SWEEPS = 4
ORB, BOX = 64, 4
SLOTS, ORBS, OWN = 8, 256, 4
DEPTH = 16
PLANE = G * G
LANES = 256
TILES = PLANE // LANES
FPAD, KPAD = 2, 4

coupling_z = 4.0
coupling_xy = 1.0

F32, BF16 = jnp.float32, jnp.bfloat16
ANY = pl.BlockSpec(memory_space=pl.ANY)
VMEM = pl.BlockSpec(memory_space=pltpu.VMEM)
VLIMIT = 56 * 2**20


def magic_weights(tap_count):
    half_len = tap_count // 2
    offsets = np.arange(1 - half_len, half_len + 1) * 1.0
    weights = np.ones(tap_count)
    for index_a in range(tap_count):
        for index_b in range(tap_count):
            if index_b != index_a:
                weights[index_a] *= (0.25 - offsets[index_b]) / (
                    offsets[index_a] - offsets[index_b]
                )
    return weights


def second_weights(reach_cells):
    factor = math.factorial(reach_cells) ** 2
    weights = np.zeros(2 * reach_cells + 1)
    for distance in range(1, reach_cells + 1):
        entry_value = (
            2.0
            * (-1) ** (distance + 1)
            * factor
            / (
                distance
                * distance
                * math.factorial(reach_cells - distance)
                * math.factorial(reach_cells + distance)
            )
        )
        weights[reach_cells + distance] = entry_value
        weights[reach_cells - distance] = entry_value
    weights[reach_cells] = -weights.sum()
    return -0.5 * weights


def banded(row_count, col_count, row_start, col_start, weights, offset_low):
    row_index = np.arange(row_count)[:, None] + row_start
    col_index = np.arange(col_count)[None, :] + col_start
    position = row_index - col_index - offset_low
    inside = (position >= 0) & (position < len(weights))
    return np.where(inside, weights[np.clip(position, 0, len(weights) - 1)], 0.0)


def halves(table):
    table = np.asarray(table, np.float32)
    high = table.astype(ml_dtypes.bfloat16)
    low = (table - high.astype(np.float32)).astype(ml_dtypes.bfloat16)
    return high, low


def tables():
    magic = magic_weights(MTAPS)
    kinetic_row = second_weights(KREACH)
    forward = banded(G, G, 0, 0, magic, 1 - MTAPS // 2)
    kinetic = banded(G, G, 0, 0, kinetic_row, -KREACH)
    rows = LANES // G

    def beside(high, low):
        return np.concatenate([high, high, low], 1)

    z_in = beside(*halves(np.concatenate([forward.T, kinetic], 0)))
    z_out = beside(*halves(forward))
    into, back, kin = [], [], []
    for step in range(-FPAD, FPAD + 1):
        block = banded(rows, rows, rows * step, 0, magic, 1 - MTAPS // 2)
        into.append(np.kron(block, forward))
        block = banded(rows, rows, -rows * step, 0, magic, 1 - MTAPS // 2).T
        back.append(np.kron(block, forward.T))
    for step in range(-KPAD, KPAD + 1):
        block = np.kron(banded(rows, rows, rows * step, 0, kinetic_row, -KREACH), np.eye(G))
        if step == 0:
            block = block + np.kron(np.eye(rows), kinetic)
        kin.append(block)
    return [z_in, z_out] + [np.stack(halves(np.stack(m))) for m in (into, back, kin)]


def split(values):
    high = values.astype(BF16)
    return high, (values - high.astype(F32)).astype(BF16)


def mm(left, right):
    return jnp.dot(left, right, preferred_element_type=F32)


def place():
    orb = lax.axis_index("orb")
    box = lax.axis_index("box")
    return orb, box, orb // 16, (orb // 2) % 8, orb % 2


def shifted(orb, step):
    x, z, core = orb // 16, (orb // 2) % 8, orb % 2
    dx, dz, dc = step // 16, (step // 2) % 8, step % 2
    return ((x + dx) % 4) * 16 + ((z + dz) % 8) * 2 + (core + dc) % 2


def remote(src, dst, send, recv, orb, box):
    return pltpu.make_async_remote_copy(
        src_ref=src,
        dst_ref=dst,
        send_sem=send,
        recv_sem=recv,
        device_id={"orb": orb, "box": box},
        device_id_type=pl.DeviceIdType.MESH,
    )


def wait_for(ref, sem):
    pltpu.make_async_copy(ref, ref, sem).wait()


def tile_of(orb):
    return pl.ds(pl.multiple_of((orb // 32) * 8, 8), 8), pl.ds(
        pl.multiple_of((orb % 32) * 128, 128), 128
    )


CHUNKS = 4
GROUPS = ((0, 2), (2, 1), (3, 1))


def greet(orb, box, x, z, core, plane_sem, meanwhile):
    barrier = pltpu.get_barrier_semaphore()

    def signal(sem, to_orb, to_box):
        pl.semaphore_signal(
            sem, inc=1, device_id={"orb": to_orb, "box": to_box}, device_id_type=pl.DeviceIdType.MESH
        )

    def along_z(step, carry):
        signal(barrier, x * 16 + ((z + step) % 8) * 2 + core, box)
        return carry

    def across(sem):
        def body(step, carry):
            signal(sem, ((x + step // 2) % 4) * 16 + z * 2 + (core + step % 2) % 2, box)
            return carry

        return body

    def beside(sem):
        for step in range(1, BOX):
            signal(sem, orb, (box + step) % BOX)

    lax.fori_loop(1, 8, along_z, 0)
    lax.fori_loop(1, 8, across(barrier), 0)
    beside(barrier)
    meanwhile()
    pl.semaphore_wait(barrier, 7 + 7 + 3)
    lax.fori_loop(1, 8, across(plane_sem), 0)
    return beside


def filters(cube, vfull, z_in, z_out, into, back, kin, out, c_hi, c_lo, t_hi, t_lo, s_hi, s_lo, kz, arrived, tabled, ready, order, leave):
    for buf, pad in ((c_hi, KPAD), (c_lo, KPAD), (t_hi, FPAD), (t_lo, FPAD), (s_hi, FPAD), (s_lo, FPAD)):
        edge = jnp.zeros((pad, 2 * G, LANES), BF16)
        buf[pl.ds(0, pad)] = edge
        buf[pl.ds(TILES + pad, pad)] = edge

    def along_z(t, carry):
        lanes = pl.ds(pl.multiple_of(t * LANES, LANES), LANES)
        for s in range(2):
            rows = pl.ds(s * G, G)
            high, low = split(cube[s, :, lanes])
            c_hi[t + KPAD, rows, :] = high
            c_lo[t + KPAD, rows, :] = low
            both = mm(z_in[...], jnp.concatenate([high, low, high], 0))
            kz[t, rows, :] = both[G:]
            high, low = split(both[:G])
            t_hi[t + FPAD, rows, :] = high
            t_lo[t + FPAD, rows, :] = low
        return carry

    group = 2

    def spread(hi, lo, table, count, first, acc):
        for d in range(count):
            high = hi[pl.ds(first + d, group)].reshape(group * 2 * G, LANES)
            low = lo[pl.ds(first + d, group)].reshape(group * 2 * G, LANES)
            term = mm(high, table[0, d]) + mm(low, table[0, d]) + mm(high, table[1, d])
            acc = term if acc is None else acc + term
        return acc

    def middle(i, carry):
        first = i * group
        grid = spread(t_hi, t_lo, into, 2 * FPAD + 1, first, None)
        for j in range(group):
            lanes = pl.ds(pl.multiple_of((first + j) * LANES, LANES), LANES)
            local = vfull[:, lanes]
            for s in range(2):
                low_row = (j * 2 + s) * G
                high, low = split(grid[low_row : low_row + G] * local)
                done = mm(z_out[...], jnp.concatenate([high, low, high], 0))
                high, low = split(done)
                s_hi[first + j + FPAD, pl.ds(s * G, G), :] = high
                s_lo[first + j + FPAD, pl.ds(s * G, G), :] = low
        return carry

    def kinetic(i, carry):
        first = i * group
        acc = kz[pl.ds(first, group)].reshape(group * 2 * G, LANES)
        acc = spread(c_hi, c_lo, kin, 2 * KPAD + 1, first, acc)
        kz[pl.ds(first, group)] = acc.reshape(group, 2 * G, LANES)
        return carry

    tabled()
    per = TILES // CHUNKS
    for chunk in range(CHUNKS - 1):
        arrived(chunk)
        lax.fori_loop(chunk * per, (chunk + 1) * per, along_z, 0)
    early = (TILES - per - KPAD) // group
    lax.fori_loop(0, early, kinetic, 0)
    lax.fori_loop(0, early, middle, 0)
    arrived(CHUNKS - 1)
    lax.fori_loop(TILES - per, TILES, along_z, 0)
    lax.fori_loop(early, TILES // group, middle, 0)
    lax.fori_loop(early, TILES // group, kinetic, 0)

    def last(i, carry):
        first = order(i) * group
        acc = kz[pl.ds(first, group)].reshape(group * 2 * G, LANES)
        acc = spread(s_hi, s_lo, back, 2 * FPAD + 1, first, acc)
        for j in range(group):
            lanes = pl.ds(pl.multiple_of((first + j) * LANES, LANES), LANES)
            for s in range(2):
                low_row = (j * 2 + s) * G
                out[s, :, lanes] = acc[low_row : low_row + G]
        leave(first)
        return carry

    ready()
    lax.fori_loop(0, TILES // group, last, 0)


def inverse_of(mult_t, which):
    line = mult_t[which // 8, pl.ds(which % 8, 1), :]
    keep = lax.broadcasted_iota(jnp.int32, (1, ORBS), 1) == which
    diagonal = jnp.sum(jnp.where(keep, line, 0.0), axis=1, keepdims=True)
    return 1.0 / (2.0 * coupling_z + 4.0 * coupling_xy + 1.0 + jnp.abs(diagonal))


def relax(resid, inverse, box, direct_out):
    lane = lax.broadcasted_iota(jnp.int32, (32, 128), 1)
    row = lax.broadcasted_iota(jnp.int32, (32, 128), 0)
    inside = ((row >= 8) | (box > 0)) & ((row < 24) | (box < BOX - 1))
    factor = jnp.where(inside, jnp.broadcast_to(inverse, (32, 128)), 0.0)
    first_col, last_col, first_row = lane % G == 0, lane % G == G - 1, lane < G
    count = PLANE // 128
    start = [jnp.where(inside, resid[:, k * 128 : (k + 1) * 128], 0.0) for k in range(count)]
    now = [part * factor for part in start]
    for _ in range(SWEEPS):
        turned = [pltpu.roll(part, G, 1) for part in now]
        pairs = [turned[0]] + [turned[k - 1] + turned[k] for k in range(1, count)] + [turned[-1]]
        following = []
        for k in range(count):
            side = jnp.where(first_row, pairs[k], pairs[k + 1])
            side = side + jnp.where(first_col, 0.0, pltpu.roll(now[k], 1, 1))
            side = side + jnp.where(last_col, 0.0, pltpu.roll(now[k], 127, 1))
            along_z = pltpu.roll(now[k], 1, 0) + pltpu.roll(now[k], 31, 0)
            following.append((start[k] + coupling_xy * side + coupling_z * along_z) * factor)
        now = following
    for k in range(count):
        direct_out[:, k * 128 : (k + 1) * 128] = now[k][8:24]


def finish_kernel(resid, direct, mult, ext, inverse, resid_out, direct_out, mult_out, last, sems):
    box = lax.axis_index("box")
    done = pl.ds(0, OWN - 1)
    copies = [
        pltpu.make_async_copy(direct, direct_out.at[done], sems.at[0]),
        pltpu.make_async_copy(resid, resid_out.at[done], sems.at[1]),
        pltpu.make_async_copy(ext.at[pl.ds(8, DEPTH)], resid_out.at[OWN - 1], sems.at[2]),
        pltpu.make_async_copy(mult, mult_out, sems.at[3]),
    ]
    for copy in copies:
        copy.start()
    relax(ext[...], inverse[0:1, 0:1], box, last)
    copies.append(pltpu.make_async_copy(last, direct_out.at[OWN - 1], sems.at[4]))
    copies[-1].start()
    for copy in copies:
        copy.wait()


def step_kernel(
    psi, pot, slots, z_in_h, z_out_h, into_h, back_h, kin_h,
    resid_out, direct_out, mult_out, ext_out, inverse_out,
    pieces, app_pieces, cube, vfull, applied,
    z_in, z_out, into, back, kin,
    f_c_hi, f_c_lo, f_t_hi, f_t_lo, f_s_hi, f_s_lo, kz,
    part, rs, bb, mult, resid, c_hi, c_lo, a_hi, a_lo, a_sum, m_side, c_turned, ext,
    own, y_send, y_recv, v_sem, p_sem, a_sem, r_sem, f_send, f_recv, h_send, h_recv, tab, plane_sem, all_sem,
):
    orb, box, x, z, core = place()
    table_copies = [
        pltpu.make_async_copy(src, dst, tab.at[i])
        for i, (src, dst) in enumerate(
            ((z_in_h, z_in), (z_out_h, z_out), (into_h, into), (back_h, back), (kin_h, kin))
        )
    ]
    slab = pl.ds(pl.multiple_of(box * DEPTH, DEPTH), DEPTH)
    width = PLANE // CHUNKS
    v_mine = pltpu.make_async_copy(pot, vfull.at[slab, :], own.at[0])
    target = pl.ds(pl.multiple_of(orb * SLOTS, SLOTS), SLOTS)
    z_rows, lanes = tile_of(orb)
    p_mine = pltpu.make_async_copy(psi.at[:, z_rows, lanes], pieces.at[target], own.at[1])
    c_mine = pltpu.make_async_copy(psi.at[pl.ds(2 * box, 2)], cube.at[:, slab, :], own.at[2])

    def meanwhile():
        for copy in [*table_copies, v_mine, p_mine, c_mine]:
            copy.start()

    beside = greet(orb, box, x, z, core, plane_sem, meanwhile)
    for chunk in range(CHUNKS):
        cols = pl.ds(chunk * width, width)
        for step in range(1, BOX):
            to = (box + step) % BOX
            remote(
                psi.at[pl.ds(2 * to, 2), :, cols], cube.at[:, slab, cols],
                y_send.at[chunk], y_recv.at[chunk], orb, to,
            ).start()
            if chunk == CHUNKS - 2:
                remote(pot, vfull.at[slab, :], v_sem.at[0], v_sem.at[1], orb, to).start()
    pl.semaphore_wait(plane_sem, 7)

    def send_psi(step, carry):
        to = shifted(orb, step)
        z_rows, lanes = tile_of(to)
        remote(psi.at[:, z_rows, lanes], pieces.at[target], p_sem.at[0], p_sem.at[1], to, box).start()
        return carry

    lax.fori_loop(1, ORB, send_psi, 0)
    beside(all_sem)

    def tabled():
        for copy in table_copies:
            copy.wait()

    def arrived(chunk):
        if chunk == 0:
            c_mine.wait()
        third = cube.at[:, pl.ds(0, 3 * DEPTH), pl.ds(chunk * width, width)]
        wait_for(third, y_recv.at[chunk])
        if chunk == CHUNKS - 2:
            v_mine.wait()
            wait_for(vfull.at[pl.ds(0, 3 * DEPTH)], v_sem.at[1])

    a_target = pl.ds(orb * SLOTS + 2 * box, 2)

    def source(to_orb, to_box):
        z_rows = pl.ds(pl.multiple_of(to_box * DEPTH + (to_orb // 32) * 8, 8), 8)
        return applied.at[:, z_rows, pl.ds(pl.multiple_of((to_orb % 32) * 128, 128), 128)]

    def ready():
        pl.semaphore_wait(all_sem, BOX - 1)

    def order(i):
        return (z // 2 + (1 + i) * (1 + 2 * core)) % 4 + 4 * ((i // 4 + x) % 2)

    def leave(first):
        def send_applied(step, carry):
            to_orb = ((step // BOX) % 2) * 32 + 2 * first + step // (2 * BOX)
            to_box = (box + step % BOX) % BOX

            @pl.when((to_orb != orb) | (to_box != box))
            def _():
                remote(
                    source(to_orb, to_box), app_pieces.at[a_target], a_sem.at[0], a_sem.at[1], to_orb, to_box
                ).start()

            return carry

        lax.fori_loop(0, 8 * BOX, send_applied, 0)

    filters(
        cube, vfull, z_in, z_out, into, back, kin, applied,
        f_c_hi, f_c_lo, f_t_hi, f_t_lo, f_s_hi, f_s_lo, kz, arrived, tabled, ready, order, leave,
    )
    a_mine = pltpu.make_async_copy(source(orb, box), app_pieces.at[a_target], own.at[3])
    a_mine.start()

    pieces2 = pieces.reshape(SLOTS * ORB * 8, 128)
    applied2 = app_pieces.reshape(SLOTS * ORB * 8, 128)
    resid2 = resid.reshape(ORBS * 8, 128)
    wanted = jnp.broadcast_to(slots[...].astype(F32), (ORBS, ORBS)).T
    column = lax.broadcasted_iota(jnp.int32, (ORBS, ORBS), 1).astype(F32)
    pick = jnp.concatenate(
        [(column + float(k * ORBS) == wanted).astype(F32) for k in range(SLOTS * ORB // ORBS)], 1
    ).astype(BF16)

    def choose(ref, hi, lo, both=None, turned=None):
        for k in range(8):
            lanes = pl.ds(k * 128, 128)
            high, low = split(ref[pl.ds(k, SLOTS * ORB, stride=8), :])
            picked = mm(pick, jnp.concatenate([high, low], 1))
            high, low = picked[:, :128], picked[:, 128:]
            hi[:, lanes] = high.astype(BF16)
            lo[:, lanes] = low.astype(BF16)
            if turned is not None:
                turned[0, lanes, :] = high.T.astype(BF16)
                turned[1, lanes, :] = low.T.astype(BF16)
            if both is not None:
                both[pl.ds(k * ORBS, ORBS), :] = high + low

    p_mine.wait()
    wait_for(pieces.at[pl.ds(0, SLOTS * (ORB - 1))], p_sem.at[1])
    choose(pieces2, c_hi, c_lo, turned=c_turned)
    a_mine.wait()
    wait_for(app_pieces.at[pl.ds(0, SLOTS * ORB - 2)], a_sem.at[1])
    choose(applied2, a_hi, a_lo, a_sum)

    scale = 1.0 / float(G**3)
    total = mm(a_hi[...], c_turned[0]) + mm(a_hi[...], c_turned[1]) + mm(a_lo[...], c_turned[0])
    part[...] = (total * scale).reshape(32, 8, ORBS)

    a_me = (x * 4 + box) * 2 + core

    def a_peer(step):
        to_orb = ((x + step // 8) % 4) * 16 + z * 2 + (core + step % 2) % 2
        return to_orb, (box + (step // 2) % 4) % 4

    for step in range(1, 32):
        to_orb, to_box = a_peer(step)
        a_to = ((to_orb // 16) * 4 + to_box) * 2 + to_orb % 2
        remote(part.at[a_to], rs.at[a_me], r_sem.at[0], r_sem.at[1], to_orb, to_box).start()
    rs[a_me] = part[a_me]
    wait_for(rs.at[pl.ds(0, 31)], r_sem.at[1])
    bb[z] = jnp.sum(rs[...], axis=0)
    for step in range(1, 8):
        to_orb = x * 16 + ((z + step) % 8) * 2 + core
        remote(bb.at[z], bb.at[z], r_sem.at[2], r_sem.at[3], to_orb, box).start()
    wait_for(bb.at[pl.ds(0, 7)], r_sem.at[3])
    mult[a_me] = jnp.sum(bb[...], axis=0)
    for step in range(1, 32):
        to_orb, to_box = a_peer(step)
        remote(mult.at[a_me], mult.at[a_me], r_sem.at[4], r_sem.at[5], to_orb, to_box).start()
    wait_for(mult.at[pl.ds(0, 31)], r_sem.at[5])
    z_rows = pl.ds(pl.multiple_of(8 + (orb // 32) * 8, 8), 8)
    lanes = pl.ds(pl.multiple_of((orb % 32) * 128, 128), 128)
    r_mine = []
    mult2 = mult.reshape(ORBS, ORBS)
    for h in range(2):
        m_side[pl.ds(h * ORBS, ORBS), :] = mult2[:, pl.ds(h * 128, 128)]
    for g, (first, count) in enumerate(GROUPS):
        members = range(first, first + count)
        sides = [
            jnp.concatenate([m_side[pl.ds(h * ORBS + n, ORB, stride=OWN), :] for n in members], 0)
            for h in range(2)
        ]
        m_hi, m_lo = split(jnp.concatenate(sides, 1))
        fix = mm(m_hi, c_hi[...]) + mm(m_hi, c_lo[...]) + mm(m_lo, c_hi[...])
        for i, n in enumerate(members):
            for k in range(8):
                part_fix = fix[i * ORB : (i + 1) * ORB, k * 128 : (k + 1) * 128]
                value = a_sum[pl.ds(k * ORBS + n, ORB, stride=OWN), :] - part_fix
                resid2[pl.ds(n * 8 + k, ORB, stride=OWN * 8), :] = value
        landing = ext.at[pl.ds(first, count), z_rows, lanes]
        copy = pltpu.make_async_copy(resid.at[pl.ds(orb * OWN + first, count)], landing, own.at[4 + g])
        copy.start()
        r_mine.append(copy)

        def send_resid(step, carry, g=g, first=first, count=count, landing=landing):
            to = shifted(orb, step)
            remote(
                resid.at[pl.ds(to * OWN + first, count)], landing, f_send, f_recv.at[g], to, box
            ).start()
            return carry

        lax.fori_loop(1, ORB, send_resid, 0)

    def halo(g):
        r_mine[g].wait()
        first, count = GROUPS[g]
        wait_for(resid.at[pl.ds(0, count * (ORB - 1))], f_recv.at[g])
        some = pl.ds(first, count)
        up = remote(
            ext.at[some, pl.ds(20, 4), :], ext.at[some, pl.ds(4, 4), :],
            h_send.at[2 * g], h_recv.at[2 * g], orb, (box + 1) % BOX,
        )
        down = remote(
            ext.at[some, pl.ds(8, 4), :], ext.at[some, pl.ds(24, 4), :],
            h_send.at[2 * g + 1], h_recv.at[2 * g + 1], orb, (box + 3) % BOX,
        )
        up.start()
        down.start()
        return up, down

    def finish(g, pair):
        for copy in pair:
            copy.wait()
        first, count = GROUPS[g]
        for n in range(first, first + count):
            resid_out[n] = ext[n, 8:24, :]
            relax(ext[n], inverse_of(mult, orb * OWN + n), box, direct_out.at[n])

    mult_out[...] = mult2[...].T
    inverse_out[...] = jnp.broadcast_to(inverse_of(mult, orb * OWN + OWN - 1), (8, 128))
    pair = halo(0)
    for g in range(1, len(GROUPS)):
        following = halo(g)
        finish(g - 1, pair)
        pair = following
    for chunk in range(CHUNKS):
        wait_for(cube.at[:, pl.ds(0, 3 * DEPTH), pl.ds(chunk * width, width)], y_send.at[chunk])
    wait_for(vfull.at[pl.ds(0, 3 * DEPTH)], v_sem.at[0])
    wait_for(pieces.at[pl.ds(0, SLOTS * (ORB - 1))], p_sem.at[0])
    wait_for(app_pieces.at[pl.ds(0, SLOTS * ORB - 2)], a_sem.at[0])
    wait_for(part.at[pl.ds(0, 31)], r_sem.at[0])
    wait_for(bb.at[pl.ds(0, 7)], r_sem.at[2])
    wait_for(mult.at[pl.ds(0, 31)], r_sem.at[4])
    wait_for(resid.at[pl.ds(0, OWN * (ORB - 1))], f_send)
    for copy in pair:
        copy.wait()
    ext_out[...] = ext[OWN - 1]


DMA = pltpu.SemaphoreType.DMA
REGULAR = pltpu.SemaphoreType.REGULAR


def shape(*dims, dtype=F32):
    return jax.ShapeDtypeStruct(dims, dtype)


def local(psi, potential, orbital_slot):
    consts = [jnp.asarray(t) for t in tables()]
    v32 = lambda *dims: pltpu.VMEM(dims, F32)
    v16 = lambda *dims: pltpu.VMEM(dims, BF16)
    padded = lambda pad: v16(TILES + 2 * pad, 2 * G, LANES)
    residual, direction, mult, ext, inverse = pl.pallas_call(
        step_kernel,
        out_shape=[
            v32(OWN - 1, DEPTH, PLANE), v32(OWN - 1, DEPTH, PLANE), v32(ORBS, ORBS),
            v32(32, PLANE), v32(8, 128),
        ],
        in_specs=[ANY, ANY, VMEM] + [ANY] * 5,
        out_specs=[VMEM] * 5,
        scratch_shapes=[
            v32(SLOTS * ORB, 8, 128), v32(SLOTS * ORB, 8, 128),
            v32(2, G, PLANE), v32(G, PLANE), v32(2, G, PLANE),
        ]
        + [v16(*t.shape) for t in consts]
        + [padded(KPAD)] * 2 + [padded(FPAD)] * 4 + [v32(TILES, 2 * G, LANES)]
        + [v32(32, 8, ORBS)] * 2 + [v32(8, 8, ORBS)] + [v32(32, 8, ORBS)] + [v32(ORBS, 8, 128)]
        + [v16(ORBS, 1024)] * 4 + [v32(8 * ORBS, 128), v32(2 * ORBS, 128), v16(2, 1024, ORBS)] + [v32(OWN, 32, PLANE)]
        + [
            DMA((8,)), DMA((CHUNKS,)), DMA((CHUNKS,)), DMA((2,)), DMA((2,)), DMA((2,)), DMA((6,)),
            DMA, DMA((OWN,)), DMA((2 * OWN,)), DMA((2 * OWN,)), DMA((5,)), REGULAR, REGULAR,
        ],
        compiler_params=pltpu.CompilerParams(
            has_side_effects=True, vmem_limit_bytes=VLIMIT, collective_id=0
        ),
        name="orbital_step",
    )(psi, potential, orbital_slot.reshape(1, ORBS), *consts)
    return pl.pallas_call(
        finish_kernel,
        out_shape=[shape(OWN, DEPTH, PLANE), shape(OWN, DEPTH, PLANE), shape(ORBS, ORBS)],
        in_specs=[VMEM] * 5,
        out_specs=[ANY] * 3,
        scratch_shapes=[v32(DEPTH, PLANE), DMA((5,))],
        compiler_params=pltpu.CompilerParams(vmem_limit_bytes=16 * 2**20),
        name="last_orbital",
    )(residual, direction, mult, ext, inverse)


def solution(mesh):
    in_specs = (P("orb", "box", None), P("box", None), P())
    out_specs = (P("orb", "box", None), P("orb", "box", None), P())
    return jax.shard_map(local, mesh=mesh, in_specs=in_specs, out_specs=out_specs, check_vma=False)
```
